32 devices in a mesh: wide: 8 (over y, x, core), narrow: 4 (over z).
Axes of the slice: x: 2, y: 2, z: 4, core: 2. Of those that a mesh axis runs over, the one named last changes fastest.
Arguments:
- targets: bfloat16 [32, 512, 768], P('wide', 'narrow'), may hold values from -6 to 6
- memory: bfloat16 [32, 512, 768], P('wide', 'narrow'), may hold values from -6 to 6
- cotangent: bfloat16 [32, 512, 768], P('wide', 'narrow'), may hold values from -6 to 6
- target_segments: int32 [32, 512], P('wide', 'narrow'), may hold values from 0 to 3, as said below
- memory_segments: int32 [32, 512], P('wide', 'narrow'), may hold values from 0 to 3, as said below
- buckets: int32 [512, 512], P('narrow'), may hold values from 0 to 31
- attn_in: float32 [6, 768, 768], P(None, ('wide', 'narrow')), may hold values from -0.109375 to 0.109375
- attn_out: float32 [2, 768, 768], P(None, ('wide', 'narrow')), may hold values from -1.75 to 1.75
- gains: float32 [3, 768], P(None, ('wide', 'narrow')), may hold values from 0.5 to 1.5
- ff_in: float32 [2, 768, 2048], P(None, ('wide', 'narrow')), may hold values from -0.21875 to 0.21875
- ff_out: float32 [2048, 768], P(('wide', 'narrow')), may hold values from -0.125 to 0.125
- bias_table: float32 [32, 12], replicated, may hold values from -4 to 4
Outputs:
- output: bfloat16 [32, 512, 768], P('wide', 'narrow')
- grad_targets: bfloat16 [32, 512, 768], P('wide', 'narrow')
- grad_memory: bfloat16 [32, 512, 768], P('wide', 'narrow')
- grad_attn_in: float32 [6, 768, 768], P(None, ('wide', 'narrow'))
- grad_attn_out: float32 [2, 768, 768], P(None, ('wide', 'narrow'))
- grad_gains: float32 [3, 768], P(None, ('wide', 'narrow'))
- grad_ff_in: float32 [2, 768, 2048], P(None, ('wide', 'narrow'))
- grad_ff_out: float32 [2048, 768], P(('wide', 'narrow'))
- grad_table: float32 [32, 12], replicated
- attn_in_rows: float32 [6, 768], P(None, ('wide', 'narrow'))
- attn_in_cols: float32 [6, 768], replicated
- attn_out_rows: float32 [2, 768], P(None, ('wide', 'narrow'))
- attn_out_cols: float32 [2, 768], replicated
- ff_in_rows: float32 [2, 768], P(None, ('wide', 'narrow'))
- ff_in_cols: float32 [2, 2048], replicated
- ff_out_rows: float32 [2048], P(('wide', 'narrow'))
- ff_out_cols: float32 [768], replicated
- new_attn_in: float32 [6, 768, 768], P(None, ('wide', 'narrow'))
- new_attn_out: float32 [2, 768, 768], P(None, ('wide', 'narrow'))
- new_ff_in: float32 [2, 768, 2048], P(None, ('wide', 'narrow'))
- new_ff_out: float32 [2048, 768], P(('wide', 'narrow'))
- new_table: float32 [32, 12], replicated
The draws below stay inside these ranges and needn't reach their ends.
Inputs may be any that keep to these rules, and one draw needn't show every extreme that they name: `target_segments`: along each row the document numbers never fall and every number 0 to 3 occurs. `memory_segments`: along each row the document numbers never fall and every number 0 to 3 occurs.
All inputs are finite; a program needn't handle non-finite values.
Results may differ from the reference program's by a relative error of at most 0.03.
The reference program's roundings to bfloat16 on the way count: a program that leaves them out, or rounds other values in their place, can miss the bound.
Values may be sent and summed in bfloat16 or wider, within the bound.
No kernel may reach another device: no remote copies, remote signals or barrier semaphores. Data moves between devices by JAX's collectives and lax.ppermute only.
A program may use at most 256 MiB of HBM per device.

```python
import math
import jax
import jax.numpy as jnp
from jax import lax

D = 768
FF = 2048
HEADS = 12
HEAD = 64
NB = 32
DOCS = 4
TLOC = 128
MLOC = 128
TLEN = 512
MLEN = 512
ROWS = 32


def cut_rows(key, span_total, edge_span):
    first_cuts = jnp.arange(1, edge_span, dtype=jnp.int32)
    last_cuts = jnp.arange(span_total - edge_span, span_total, dtype=jnp.int32)
    places = jnp.concatenate([first_cuts, last_cuts])
    row_keys = jax.random.split(key, ROWS)

    def one_row(row_key):
        picked = jax.random.permutation(row_key, places)[:DOCS - 1]
        positions = jnp.arange(span_total, dtype=jnp.int32)
        return jnp.sum((picked[None, :] <= positions[:, None]).astype(jnp.int32), axis=1)
    return jax.vmap(one_row)(row_keys)


def draw_target_segments(key, part):
    key = jax.random.fold_in(key, 11)
    return cut_rows(key, TLEN, TLOC // 2)


def draw_memory_segments(key, part):
    key = jax.random.fold_in(key, 23)
    return cut_rows(key, MLEN, MLOC // 2)


def draw_buckets(key, part):
    key = jax.random.fold_in(key, 37)
    steps_at = jax.random.permutation(key, jnp.arange(1, TLEN, dtype=jnp.int32))[:NB - 1]
    distance = jnp.arange(TLEN, dtype=jnp.int32)
    mapping = jnp.sum((steps_at[None, :] <= distance[:, None]).astype(jnp.int32), axis=1)
    offsets = jnp.abs(distance[:, None] - distance[None, :])
    return mapping[offsets]


def shard_levels(key, dims, cuts, least, top_value):
    def one(dim, blocks):
        draws = jax.random.uniform(jax.random.fold_in(jax.random.fold_in(key, 6), dim), (blocks,), jnp.float32, least / len(cuts), top_value / len(cuts))
        return jnp.repeat(jnp.exp(draws), dims[dim] // blocks).reshape((-1,) + (1,) * (len(dims) - dim - 1))

    gain = one(*cuts[0])
    for cut in cuts[1:]:
        gain = gain * one(*cut)
    return gain


def bell_draw(key, dims, spread, bound, cuts=(), held_as=jnp.bfloat16):
    values = spread * jax.random.normal(key, dims, jnp.float32)
    if cuts:
        values = values * shard_levels(key, dims, cuts, -0.22, 0.18)
    return jnp.clip(values, -bound, bound).astype(held_as)


def setup_inputs(seed: int = 0) -> dict:
    splits = jax.random.split(jax.random.key(seed), 13)
    return {
        "targets": bell_draw(splits[0], (ROWS, TLEN, D), 1.0, 6.0, ((0, 8), (1, 4))),
        "memory": bell_draw(splits[1], (ROWS, MLEN, D), 1.0, 6.0, ((0, 8), (1, 4))),
        "cotangent": bell_draw(splits[2], (ROWS, TLEN, D), 1.0, 6.0, ((0, 8), (1, 4))),
        "target_segments": draw_target_segments(jax.random.fold_in(splits[12], 71), 0),
        "memory_segments": draw_memory_segments(jax.random.fold_in(splits[12], 71), 0),
        "buckets": draw_buckets(jax.random.fold_in(splits[12], 71), 0),
        "attn_in": bell_draw(splits[6], (6, D, D), (4 * D) ** -0.5, 0.109375, ((1, 32),), jnp.float32),
        "attn_out": bell_draw(splits[7], (2, D, D), (D // 64) ** -0.5, 1.75, ((1, 32),), jnp.float32),
        "gains": jnp.clip(1.0 + 0.1 * jax.random.normal(splits[8], (3, D), jnp.float32), 0.5, 1.5),
        "ff_in": bell_draw(splits[9], (2, D, FF), D ** -0.5, 0.21875, ((1, 32),), jnp.float32),
        "ff_out": bell_draw(splits[10], (FF, D), FF ** -0.5, 0.125, ((0, 32),), jnp.float32),
        "bias_table": bell_draw(splits[11], (NB, HEADS), 1.0, 4.0, (), jnp.float32),
    }


@jax.custom_vjp
def low(v):
    return lax.optimization_barrier(v.astype(jnp.bfloat16)).astype(jnp.float32)

@jax.custom_vjp
def low_back(v):
    return v

def low_keep(v):
    return (low(v), None)

def low_pass(kept, grad):
    return (grad,)

def back_keep(v):
    return (v, None)

def back_low(kept, grad):
    return (low(grad),)
low.defvjp(low_keep, low_pass)
low_back.defvjp(back_keep, back_low)
highest = lax.Precision.HIGHEST

def both_low(values_in):
    return low_back(low(values_in))

def rms_norm(values_in, gain_row):
    inv_rms = lax.rsqrt(lax.optimization_barrier(jnp.mean(values_in * values_in, axis=-1, keepdims=True)) + 1e-06)
    return values_in * inv_rms * gain_row

def gelu_tanh(pre_act):
    return 0.5 * pre_act * (1.0 + jnp.tanh(0.7978845608028654 * (pre_act + 0.044715 * pre_act * pre_act * pre_act)))

def times_matrix(left_rows, right_matrix):
    return jnp.matmul(left_rows, right_matrix, precision=highest)

def attention(query_rows, key_rows, value_rows, extra_bias, allowed):
    length_q = query_rows.shape[0]
    length_k = key_rows.shape[0]
    query_heads = query_rows.reshape(length_q, HEADS, HEAD)
    key_heads = key_rows.reshape(length_k, HEADS, HEAD)
    value_heads = value_rows.reshape(length_k, HEADS, HEAD)
    scores = jnp.einsum('qhd,khd->hqk', query_heads, key_heads, precision=highest) + extra_bias
    scores = jnp.where(allowed[None], low_back(scores), -1000000000.0)
    row_peak = lax.optimization_barrier(jnp.max(scores, axis=-1, keepdims=True))
    exponent = jnp.exp(scores - row_peak)
    soft_weights = low(exponent / lax.optimization_barrier(jnp.sum(exponent, axis=-1, keepdims=True)))
    mixed_heads = jnp.einsum('hqk,khd->qhd', soft_weights, value_heads, precision=highest)
    return mixed_heads.reshape(length_q, HEADS * HEAD)

def layer(target_rows, memory_rows, target_segs, memory_segs, buckets, weights):
    attn_in, attn_out, gains, ff_in, ff_out, bias_table = weights
    w_in = low(attn_in)
    w_out = low(attn_out)
    gain_low = low(gains)
    f_in = low(ff_in)
    f_out = low(ff_out)
    one_hot = (buckets[:, :, None] == jnp.arange(NB, dtype=jnp.int32)[None, None, :]).astype(jnp.float32)
    rel_bias = jnp.einsum('qkb,bh->hqk', one_hot, bias_table, precision=highest)
    positions = jnp.arange(TLEN, dtype=jnp.int32)
    causal = positions[:, None] >= positions[None, :]
    normed_attn = low(rms_norm(target_rows, gain_low[0]))
    self_query = both_low(times_matrix(normed_attn, w_in[0]))
    self_key = both_low(times_matrix(normed_attn, w_in[1]))
    self_value = both_low(times_matrix(normed_attn, w_in[2]))

    def self_row(pieces):
        query_rows, key_rows, value_rows, segment = pieces
        allowed = causal & (segment[:, None] == segment[None, :])
        return attention(query_rows, key_rows, value_rows, rel_bias, allowed)
    self_mixed = lax.map(jax.checkpoint(self_row), (self_query, self_key, self_value, target_segs))
    after_self = target_rows + low_back(times_matrix(both_low(self_mixed), w_out[0]))
    normed_cross = low(rms_norm(after_self, gain_low[1]))
    cross_query = both_low(times_matrix(normed_cross, w_in[3]))
    cross_key = both_low(times_matrix(memory_rows, w_in[4]))
    cross_value = both_low(times_matrix(memory_rows, w_in[5]))

    def cross_row(pieces):
        query_rows, key_rows, value_rows, segment, memory_segment = pieces
        allowed = segment[:, None] == memory_segment[None, :]
        return attention(query_rows, key_rows, value_rows, 0.0, allowed)
    cross_mixed = lax.map(jax.checkpoint(cross_row), (cross_query, cross_key, cross_value, target_segs, memory_segs))
    after_cross = after_self + low_back(times_matrix(both_low(cross_mixed), w_out[1]))
    normed_ffn = low(rms_norm(after_cross, gain_low[2]))
    gate_proj = low_back(times_matrix(normed_ffn, f_in[0]))
    up_proj = low_back(times_matrix(normed_ffn, f_in[1]))
    hidden = low(gelu_tanh(gate_proj) * up_proj)
    return after_cross + times_matrix(hidden, f_out)

def factored(gradient, weight):
    squares = gradient * gradient + 1e-30
    rows_stat = lax.optimization_barrier(jnp.sum(squares, axis=-1))
    cols_stat = lax.optimization_barrier(jnp.sum(squares, axis=-2))
    overall = lax.optimization_barrier(jnp.sum(rows_stat, axis=-1))[..., None, None]
    estimate = rows_stat[..., :, None] * cols_stat[..., None, :] / overall
    weight_rms = jnp.sqrt(lax.optimization_barrier(jnp.mean(weight * weight, axis=(-2, -1))) + 1e-06)[..., None, None]
    return (rows_stat, cols_stat, weight - 0.3 * weight_rms * gradient * lax.rsqrt(estimate))

def reference(targets, memory, cotangent, target_segments, memory_segments, buckets, attn_in, attn_out, gains, ff_in, ff_out, bias_table):
    group_rows = math.gcd(ROWS, max(1, 4096 // TLEN))
    blocks = ROWS // group_rows

    def by_groups(stacked):
        return stacked.reshape((blocks, group_rows) + stacked.shape[1:])
    params = (attn_in, attn_out, gains, ff_in, ff_out, bias_table)

    def one_group(running, batch_rows):
        rows_x, rows_m, rows_c, segs_t, segs_m = batch_rows

        def forward(value_x, value_m, weights):
            return layer(value_x, value_m, segs_t, segs_m, buckets, weights)
        result, pull_back = jax.vjp(forward, rows_x.astype(jnp.float32), rows_m.astype(jnp.float32), params)
        grad_x, grad_m, grad_w = pull_back(rows_c.astype(jnp.float32))
        running = jax.tree.map(jnp.add, running, grad_w)
        return (running, (result.astype(jnp.bfloat16), grad_x.astype(jnp.bfloat16), grad_m.astype(jnp.bfloat16)))
    zero_grads = jax.tree.map(jnp.zeros_like, params)
    totals, (outputs, grads_x, grads_m) = lax.scan(one_group, zero_grads, (by_groups(targets), by_groups(memory), by_groups(cotangent), by_groups(target_segments), by_groups(memory_segments)))
    grad_in, grad_out, grad_gain, grad_fin, grad_fout, grad_tab = totals
    in_rows, in_cols, new_in = factored(grad_in, attn_in)
    out_rows, out_cols, new_out = factored(grad_out, attn_out)
    fin_rows, fin_cols, new_fin = factored(grad_fin, ff_in)
    fout_rows, fout_cols, new_fout = factored(grad_fout, ff_out)
    tab_rows, tab_cols, new_tab = factored(grad_tab, bias_table)
    return (outputs.reshape(ROWS, TLEN, D), grads_x.reshape(ROWS, TLEN, D), grads_m.reshape(ROWS, MLEN, D), grad_in, grad_out, grad_gain, grad_fin, grad_fout, grad_tab, in_rows, in_cols, out_rows, out_cols, fin_rows, fin_cols, fout_rows, fout_cols, new_in, new_out, new_fin, new_fout, new_tab)
```

```python
import jax
import jax.numpy as jnp
from jax import lax
from jax.sharding import PartitionSpec as P

highest = lax.Precision.HIGHEST


def gelu_tanh(pre_act):
    return (
        0.5
        * pre_act
        * (1.0 + jnp.tanh(0.7978845608028654 * (pre_act + 0.044715 * pre_act * pre_act * pre_act)))
    )


def norm_parts(values_in, gain_row):
    inv_rms = lax.rsqrt(jnp.mean(values_in * values_in, axis=-1, keepdims=True) + 1e-06)
    unit_rows = values_in * inv_rms
    return (unit_rows, inv_rms, (unit_rows * gain_row).astype(jnp.bfloat16))


def norm_back(incoming, unit_rows, inv_rms, gain_row):
    scaled = incoming * gain_row
    grad_gain = jnp.sum(incoming * unit_rows, axis=(0, 1))
    inner_mean = jnp.mean(scaled * unit_rows, axis=-1, keepdims=True)
    return (inv_rms * (scaled - unit_rows * inner_mean), grad_gain)


def forward_mul(left_rows, right_matrix):
    return jnp.einsum("rld,de->rle", left_rows, right_matrix, preferred_element_type=jnp.float32)


def back_mul(left_rows, right_matrix):
    return jnp.einsum("rle,de->rld", left_rows, right_matrix, preferred_element_type=jnp.float32)


def weight_mul(left_rows, right_rows):
    return jnp.einsum("rld,rle->de", left_rows, right_rows, preferred_element_type=jnp.float32)


def head_split(stacked, head_count):
    return stacked.reshape(
        stacked.shape[0], stacked.shape[1], head_count, stacked.shape[2] // head_count
    )


def masked_scores(query_rows, key_rows, extra_bias, allowed, head_count):
    raw_scores = (
        jnp.einsum(
            "gqhd,gkhd->ghqk",
            head_split(query_rows, head_count),
            head_split(key_rows, head_count),
            preferred_element_type=jnp.float32,
        )
        + extra_bias
    )
    return jnp.where(allowed[:, None], raw_scores, -1000000000.0)


def attend_block(query_rows, key_rows, value_rows, extra_bias, allowed, head_count):
    scores = masked_scores(query_rows, key_rows, extra_bias, allowed, head_count)
    row_peak = jnp.max(scores, axis=-1, keepdims=True)
    exponent = jnp.exp(scores - row_peak)
    row_total = jnp.sum(exponent, axis=-1, keepdims=True)
    soft_weights = (exponent / row_total).astype(jnp.bfloat16)
    mixed_heads = jnp.einsum(
        "ghqk,gkhd->gqhd",
        soft_weights,
        head_split(value_rows, head_count),
        preferred_element_type=jnp.float32,
    )
    return (mixed_heads.reshape(query_rows.shape).astype(jnp.bfloat16), row_peak, row_total)


def attend_back(
    query_rows,
    key_rows,
    value_rows,
    extra_bias,
    allowed,
    row_peak,
    row_total,
    grad_rows,
    head_count,
    want_bias,
):
    scores = masked_scores(query_rows, key_rows, extra_bias, allowed, head_count)
    soft_weights = jnp.exp(scores - row_peak) / row_total
    grad_heads = head_split(grad_rows, head_count)
    grad_probs = jnp.einsum(
        "gqhd,gkhd->ghqk",
        grad_heads,
        head_split(value_rows, head_count),
        preferred_element_type=jnp.float32,
    )
    grad_values = jnp.einsum(
        "ghqk,gqhd->gkhd",
        soft_weights.astype(jnp.bfloat16),
        grad_heads,
        preferred_element_type=jnp.float32,
    ).reshape(key_rows.shape)
    inner_sum = jnp.sum(soft_weights * grad_probs, axis=-1, keepdims=True)
    grad_scores = (soft_weights * (grad_probs - inner_sum)).astype(jnp.bfloat16)
    grad_queries = jnp.einsum(
        "ghqk,gkhd->gqhd",
        grad_scores,
        head_split(key_rows, head_count),
        preferred_element_type=jnp.float32,
    ).reshape(query_rows.shape)
    grad_keys = jnp.einsum(
        "ghqk,gqhd->gkhd",
        grad_scores,
        head_split(query_rows, head_count),
        preferred_element_type=jnp.float32,
    ).reshape(key_rows.shape)
    if want_bias:
        return (
            grad_queries,
            grad_keys,
            grad_values,
            jnp.sum(grad_scores.astype(jnp.float32), axis=0),
        )
    return (grad_queries, grad_keys, grad_values)


def local_stats(gradient):
    squares = gradient * gradient + 1e-30
    return (jnp.sum(squares, axis=-1), jnp.sum(squares, axis=-2))


def adafactor_step(gradient, weight, rows_stat, cols_stat, weight_rms):
    overall = jnp.sum(cols_stat, axis=-1)[..., None, None]
    estimate = rows_stat[..., :, None] * cols_stat[..., None, :] / overall
    return weight - 0.3 * weight_rms * gradient * lax.rsqrt(estimate)


def body(
    targets,
    memory,
    cotangent,
    target_segments,
    memory_segments,
    buckets,
    attn_in,
    attn_out,
    gains,
    ff_in,
    ff_out,
    bias_table,
):
    model_width = targets.shape[2]

    def whole_rows(stacked):
        return lax.all_to_all(stacked, "narrow", split_axis=0, concat_axis=1, tiled=True)

    def back_rows(stacked):
        return lax.all_to_all(stacked, "narrow", split_axis=1, concat_axis=0, tiled=True)

    targets, memory, cotangent = whole_rows(targets), whole_rows(memory), whole_rows(cotangent)
    target_segments, memory_segments = whole_rows(target_segments), whole_rows(memory_segments)
    buckets = lax.all_gather(buckets, "narrow", axis=0, tiled=True)
    rows_here, target_local, _ = targets.shape
    ff_width = ff_in.shape[2]
    head_count = bias_table.shape[1]
    bucket_count = bias_table.shape[0]
    block_rows = max(1, min(rows_here, 512 // target_local))
    while rows_here % block_rows:
        block_rows -= 1
    block_count = rows_here // block_rows

    def grouped(stacked):
        return stacked.reshape((block_count, block_rows) + stacked.shape[1:])

    def ungrouped(stacked):
        return stacked.reshape((rows_here,) + stacked.shape[2:])

    gathered_in, gathered_out, gathered_fin, gathered_fout, gathered_gain = (
        lax.all_gather(attn_in.astype(jnp.bfloat16), ("wide", "narrow"), axis=1, tiled=True),
        lax.all_gather(attn_out.astype(jnp.bfloat16), ("wide", "narrow"), axis=1, tiled=True),
        lax.all_gather(ff_in.astype(jnp.bfloat16), ("wide", "narrow"), axis=1, tiled=True),
        lax.all_gather(ff_out.astype(jnp.bfloat16), ("wide", "narrow"), axis=0, tiled=True),
        lax.all_gather(gains.astype(jnp.bfloat16), ("wide", "narrow"), axis=1, tiled=True),
    )
    gain_full = gathered_gain.astype(jnp.float32)
    query_pos = jnp.arange(target_local, dtype=jnp.int32)
    causal = query_pos[:, None] >= query_pos[None, :]
    one_hot = (
        buckets[:, :, None] == jnp.arange(bucket_count, dtype=jnp.int32)[None, None, :]
    ).astype(jnp.float32)
    rel_bias = jnp.einsum("qkb,bh->hqk", one_hot, bias_table, precision=highest)
    inputs_f = targets.astype(jnp.float32)
    unit_attn, scale_attn, normed_attn = norm_parts(inputs_f, gain_full[0])
    self_query = forward_mul(normed_attn, gathered_in[0]).astype(jnp.bfloat16)
    self_key = forward_mul(normed_attn, gathered_in[1]).astype(jnp.bfloat16)
    self_value = forward_mul(normed_attn, gathered_in[2]).astype(jnp.bfloat16)
    seg_target = target_segments.astype(jnp.bfloat16)
    self_keys_all, self_values_all, target_segs_all = self_key, self_value, seg_target

    def self_mask(seg_query, seg_key):
        return causal[None] & (seg_query[:, :, None] == seg_key[:, None, :])

    def cross_mask(seg_query, seg_key):
        return seg_query[:, :, None] == seg_key[:, None, :]

    def self_forward(pieces):
        query_rows, key_rows, value_rows, seg_query, seg_key = pieces
        return attend_block(
            query_rows, key_rows, value_rows, rel_bias, self_mask(seg_query, seg_key), head_count
        )

    self_mixed, self_peak, self_total = lax.map(
        self_forward,
        (
            grouped(self_query),
            grouped(self_keys_all),
            grouped(self_values_all),
            grouped(seg_target),
            grouped(target_segs_all),
        ),
    )
    self_mixed = ungrouped(self_mixed)
    after_self = inputs_f + forward_mul(self_mixed, gathered_out[0])
    unit_cross, scale_cross, normed_cross = norm_parts(after_self, gain_full[1])
    cross_query = forward_mul(normed_cross, gathered_in[3]).astype(jnp.bfloat16)
    seg_memory = memory_segments.astype(jnp.bfloat16)
    cross_key = forward_mul(memory, gathered_in[4]).astype(jnp.bfloat16)
    cross_value = forward_mul(memory, gathered_in[5]).astype(jnp.bfloat16)
    cross_keys_all, cross_values_all, memory_segs_all = cross_key, cross_value, seg_memory

    def cross_forward(pieces):
        query_rows, key_rows, value_rows, seg_query, seg_key = pieces
        return attend_block(
            query_rows, key_rows, value_rows, 0.0, cross_mask(seg_query, seg_key), head_count
        )

    cross_mixed, cross_peak, cross_total = lax.map(
        cross_forward,
        (
            grouped(cross_query),
            grouped(cross_keys_all),
            grouped(cross_values_all),
            grouped(seg_target),
            grouped(memory_segs_all),
        ),
    )
    cross_mixed = ungrouped(cross_mixed)
    after_cross = after_self + forward_mul(cross_mixed, gathered_out[1])
    unit_ffn, scale_ffn, normed_ffn = norm_parts(after_cross, gain_full[2])
    gate_proj = forward_mul(normed_ffn, gathered_fin[0])
    up_proj = forward_mul(normed_ffn, gathered_fin[1])
    activated, gelu_pull = jax.vjp(gelu_tanh, gate_proj)
    hidden_ff = (activated * up_proj).astype(jnp.bfloat16)
    output = (after_cross + forward_mul(hidden_ff, gathered_fout)).astype(jnp.bfloat16)
    cot_f = cotangent.astype(jnp.float32)
    grad_fout = weight_mul(hidden_ff, cotangent)
    grad_hidden = back_mul(cotangent, gathered_fout)
    grad_gate = gelu_pull(grad_hidden * up_proj)[0].astype(jnp.bfloat16)
    grad_up = (grad_hidden * activated).astype(jnp.bfloat16)
    grad_fin = jnp.stack([weight_mul(normed_ffn, grad_gate), weight_mul(normed_ffn, grad_up)])
    grad_normed_ffn = back_mul(grad_gate, gathered_fin[0]) + back_mul(grad_up, gathered_fin[1])
    back_ffn, gain_grad_ffn = norm_back(grad_normed_ffn, unit_ffn, scale_ffn, gain_full[2])
    grad_after_cross = cot_f + back_ffn
    branch_cross = grad_after_cross.astype(jnp.bfloat16)
    grad_out_cross = weight_mul(cross_mixed, branch_cross)
    grad_mixed_cross = back_mul(branch_cross, gathered_out[1]).astype(jnp.bfloat16)

    def cross_backward(pieces):
        query_rows, key_rows, value_rows, seg_query, seg_key, row_peak, row_total, grad_rows = (
            pieces
        )
        return attend_back(
            query_rows,
            key_rows,
            value_rows,
            0.0,
            cross_mask(seg_query, seg_key),
            row_peak,
            row_total,
            grad_rows,
            head_count,
            False,
        )

    cross_dq, cross_dk, cross_dv = lax.map(
        cross_backward,
        (
            grouped(cross_query),
            grouped(cross_keys_all),
            grouped(cross_values_all),
            grouped(seg_target),
            grouped(memory_segs_all),
            cross_peak,
            cross_total,
            grouped(grad_mixed_cross),
        ),
    )
    cross_key_low = ungrouped(cross_dk).astype(jnp.bfloat16)
    cross_value_low = ungrouped(cross_dv).astype(jnp.bfloat16)
    cross_query_low = ungrouped(cross_dq).astype(jnp.bfloat16)
    grad_q_cross = weight_mul(normed_cross, cross_query_low)
    grad_k_cross = weight_mul(memory, cross_key_low)
    grad_v_cross = weight_mul(memory, cross_value_low)
    grad_memory = (
        back_mul(cross_key_low, gathered_in[4]) + back_mul(cross_value_low, gathered_in[5])
    ).astype(jnp.bfloat16)
    back_cross, gain_grad_cross = norm_back(
        back_mul(cross_query_low, gathered_in[3]), unit_cross, scale_cross, gain_full[1]
    )
    grad_after_self = grad_after_cross + back_cross
    branch_self = grad_after_self.astype(jnp.bfloat16)
    grad_out_self = weight_mul(self_mixed, branch_self)
    grad_mixed_self = back_mul(branch_self, gathered_out[0]).astype(jnp.bfloat16)

    def self_backward(pieces):
        query_rows, key_rows, value_rows, seg_query, seg_key, row_peak, row_total, grad_rows = (
            pieces
        )
        return attend_back(
            query_rows,
            key_rows,
            value_rows,
            rel_bias,
            self_mask(seg_query, seg_key),
            row_peak,
            row_total,
            grad_rows,
            head_count,
            True,
        )

    self_dq, self_dk, self_dv, self_dbias = lax.map(
        self_backward,
        (
            grouped(self_query),
            grouped(self_keys_all),
            grouped(self_values_all),
            grouped(seg_target),
            grouped(target_segs_all),
            self_peak,
            self_total,
            grouped(grad_mixed_self),
        ),
    )
    self_key_low = ungrouped(self_dk).astype(jnp.bfloat16)
    self_value_low = ungrouped(self_dv).astype(jnp.bfloat16)
    self_query_low = ungrouped(self_dq).astype(jnp.bfloat16)
    grad_q_self = weight_mul(normed_attn, self_query_low)
    grad_k_self = weight_mul(normed_attn, self_key_low)
    grad_v_self = weight_mul(normed_attn, self_value_low)
    grad_normed_attn = (
        back_mul(self_query_low, gathered_in[0])
        + back_mul(self_key_low, gathered_in[1])
        + back_mul(self_value_low, gathered_in[2])
    )
    back_attn, gain_grad_attn = norm_back(grad_normed_attn, unit_attn, scale_attn, gain_full[0])
    grad_targets = (grad_after_self + back_attn).astype(jnp.bfloat16)
    table_part = jnp.einsum("qkb,hqk->bh", one_hot, jnp.sum(self_dbias, axis=0), precision=highest)
    grad_in_part = jnp.stack(
        [grad_q_self, grad_k_self, grad_v_self, grad_q_cross, grad_k_cross, grad_v_cross]
    )
    grad_out_part = jnp.stack([grad_out_self, grad_out_cross])
    gain_part = jnp.stack([gain_grad_attn, gain_grad_cross, gain_grad_ffn])
    def scattered(part, dim):
        total = lax.psum_scatter(
            part.astype(jnp.bfloat16), ("wide", "narrow"), scatter_dimension=dim, tiled=True
        )
        return total.astype(jnp.float32)

    sum_in, sum_out, sum_fin, sum_fout, sum_gain = (
        scattered(grad_in_part, 1),
        scattered(grad_out_part, 1),
        scattered(grad_fin, 1),
        scattered(grad_fout, 0),
        lax.psum_scatter(gain_part, ("wide", "narrow"), scatter_dimension=1, tiled=True),
    )
    in_rows, in_part = local_stats(sum_in)
    out_rows, out_part = local_stats(sum_out)
    fin_rows, fin_part = local_stats(sum_fin)
    fout_rows, fout_part = local_stats(sum_fout)
    in_square = jnp.sum(attn_in * attn_in, axis=(1, 2))
    out_square = jnp.sum(attn_out * attn_out, axis=(1, 2))
    fin_square = jnp.sum(ff_in * ff_in, axis=(1, 2))
    fout_square = jnp.sum(ff_out * ff_out).reshape(1)
    (
        in_cols,
        out_cols,
        fin_cols,
        fout_cols,
        grad_table,
        in_total,
        out_total,
        fin_total,
        fout_total,
    ) = lax.psum(
        (
            in_part,
            out_part,
            fin_part,
            fout_part,
            table_part,
            in_square,
            out_square,
            fin_square,
            fout_square,
        ),
        ("wide", "narrow"),
    )
    table_rows, table_cols = local_stats(grad_table)
    square_count = model_width * model_width
    in_rms = jnp.sqrt(in_total / square_count + 1e-06)[:, None, None]
    out_rms = jnp.sqrt(out_total / square_count + 1e-06)[:, None, None]
    fin_rms = jnp.sqrt(fin_total / (model_width * ff_width) + 1e-06)[:, None, None]
    fout_rms = jnp.sqrt(fout_total[0] / (model_width * ff_width) + 1e-06)
    table_rms = jnp.sqrt(jnp.mean(bias_table * bias_table) + 1e-06)
    new_in = adafactor_step(sum_in, attn_in, in_rows, in_cols, in_rms)
    new_out = adafactor_step(sum_out, attn_out, out_rows, out_cols, out_rms)
    new_fin = adafactor_step(sum_fin, ff_in, fin_rows, fin_cols, fin_rms)
    new_fout = adafactor_step(sum_fout, ff_out, fout_rows, fout_cols, fout_rms)
    new_table = adafactor_step(grad_table, bias_table, table_rows, table_cols, table_rms)
    return (
        back_rows(output),
        back_rows(grad_targets),
        back_rows(grad_memory),
        sum_in,
        sum_out,
        sum_gain,
        sum_fin,
        sum_fout,
        grad_table,
        in_rows,
        in_cols,
        out_rows,
        out_cols,
        fin_rows,
        fin_cols,
        fout_rows,
        fout_cols,
        new_in,
        new_out,
        new_fin,
        new_fout,
        new_table,
    )


def solution(mesh):
    in_specs = (
        P("wide", "narrow", None),
        P("wide", "narrow", None),
        P("wide", "narrow", None),
        P("wide", "narrow"),
        P("wide", "narrow"),
        P("narrow", None),
        P(None, ("wide", "narrow"), None),
        P(None, ("wide", "narrow"), None),
        P(None, ("wide", "narrow")),
        P(None, ("wide", "narrow"), None),
        P(("wide", "narrow"), None),
        P(),
    )
    out_specs = (
        P("wide", "narrow", None),
        P("wide", "narrow", None),
        P("wide", "narrow", None),
        P(None, ("wide", "narrow"), None),
        P(None, ("wide", "narrow"), None),
        P(None, ("wide", "narrow")),
        P(None, ("wide", "narrow"), None),
        P(("wide", "narrow"), None),
        P(),
        P(None, ("wide", "narrow")),
        P(),
        P(None, ("wide", "narrow")),
        P(),
        P(None, ("wide", "narrow")),
        P(),
        P(("wide", "narrow")),
        P(),
        P(None, ("wide", "narrow"), None),
        P(None, ("wide", "narrow"), None),
        P(None, ("wide", "narrow"), None),
        P(("wide", "narrow"), None),
        P(),
    )
    return jax.shard_map(body, mesh=mesh, in_specs=in_specs, out_specs=out_specs, check_vma=False)
```

```python
import functools

import jax
import jax.numpy as jnp
from jax import lax
from jax.experimental import pallas as pl
from jax.experimental.pallas import tpu as pltpu
from jax.sharding import PartitionSpec as P

bf16, f32 = jnp.bfloat16, jnp.float32
BOTH = ("wide", "narrow")
NEG = -1e9
TILE = 256
MIB = 1 << 20


def dot_nn(left, right):
    return lax.dot_general(left, right, (((1,), (0,)), ((), ())), preferred_element_type=f32)


def dot_nt(left, right):
    return lax.dot_general(left, right, (((1,), (1,)), ((), ())), preferred_element_type=f32)


def unit_of(values):
    inv_rms = lax.rsqrt(jnp.mean(values * values, axis=-1, keepdims=True) + 1e-06)
    return values * inv_rms, inv_rms


def norm_back(incoming, values, gain_row):
    unit, inv_rms = unit_of(values)
    scaled = incoming * gain_row
    inner = jnp.mean(scaled * unit, axis=-1, keepdims=True)
    return inv_rms * (scaled - unit * inner), jnp.sum(incoming * unit, axis=0, keepdims=True)


def tiles_of(width):
    return [(start, min(TILE, width - start)) for start in range(0, width, TILE)]


def project(left, w_ref, index, store):
    for start, size in tiles_of(w_ref.shape[2]):
        store(start, size, dot_nn(left, w_ref[index, :, start : start + size]))


def half_lanes(second):
    lane = lax.broadcasted_iota(jnp.int32, (1, 128), 1)
    return ((lane >= 64) == bool(second)).astype(bf16)


def biased(table_row, index):
    spread = jnp.broadcast_to(table_row, (index.shape[0], 128))
    return jnp.concatenate(
        [
            jnp.take_along_axis(
                spread, index[:, at : at + 128], axis=1, mode="promise_in_bounds"
            )
            for at in range(0, index.shape[1], 128)
        ],
        axis=1,
    )


def query_blocks(keys, queries, causal):
    return [
        (at, min(keys, at + TILE) if causal else keys) for at in range(0, queries, TILE)
    ]


def attend(qkv_ref, extra_ref, table_ref, o_ref, peak_ref, inv_ref, ot_ref):
    causal = table_ref is not None
    keys = qkv_ref.shape[1]

    def pair(at_pair, carry):
        lanes = pl.ds(pl.multiple_of(at_pair * 128, 128), 128)
        query, key, value = (qkv_ref[i, :, lanes] for i in range(3))
        value_t = value.T
        for second in range(2):
            head = at_pair * 2 + second
            key_half = key * half_lanes(second)
            for start, last in query_blocks(keys, keys, causal):
                part = slice(start, start + TILE)
                scores = dot_nt(key_half[:last], query[part])
                if causal:
                    scores += biased(table_ref[pl.ds(head, 1), :], extra_ref[:last, part])
                else:
                    scores += extra_ref[:last, part]
                peak = jnp.max(scores, axis=0, keepdims=True)
                grown = jnp.exp(scores - peak)
                inverse = 1.0 / jnp.sum(grown, axis=0, keepdims=True)
                mixed = dot_nn(value_t[second * 64 : second * 64 + 64, :last], grown.astype(bf16))
                ot_ref[second * 64 : second * 64 + 64, part] = mixed * inverse
                peak_ref[head, :, part] = peak
                inv_ref[head, :, part] = inverse
        o_ref[:, lanes] = ot_ref[...].T.astype(bf16)
        return carry

    lax.fori_loop(0, qkv_ref.shape[2] // 128, pair, 0)


def attend_back(
    qkv_ref, extra_ref, table_ref, do_ref, dsum_ref, peak_ref, inv_ref,
    dqkv_ref, p_ref, ds_ref, dqt_ref, ds_out,
):
    causal = table_ref is not None
    keys = qkv_ref.shape[1]
    first_half = lax.broadcasted_iota(jnp.int32, (1, 128), 1) < 64

    def pair(at_pair, carry):
        lanes = pl.ds(pl.multiple_of(at_pair * 128, 128), 128)
        query, key, value = (qkv_ref[i, :, lanes] for i in range(3))
        grad = do_ref[:, lanes]
        key_t = key.T
        for second in range(2):
            head = at_pair * 2 + second
            half = half_lanes(second)
            key_half, value_half = key * half, value * half
            for start, last in query_blocks(keys, keys, causal):
                part = slice(start, start + TILE)
                scores = dot_nt(key_half[:last], query[part])
                if causal:
                    scores += biased(table_ref[pl.ds(head, 1), :], extra_ref[:last, part])
                else:
                    scores += extra_ref[:last, part]
                weights = jnp.exp(scores - peak_ref[head, :, part]) * inv_ref[head, :, part]
                grad_weights = dot_nt(value_half[:last], grad[part])
                grad_scores = (weights * (grad_weights - dsum_ref[head, :, part])).astype(bf16)
                p_ref[:last, part] = weights.astype(bf16)
                ds_ref[:last, part] = grad_scores
                dqt_ref[second * 64 : second * 64 + 64, part] = dot_nn(
                    key_t[second * 64 : second * 64 + 64, :last], grad_scores
                )
            for start in range(0, keys, TILE):
                rows = slice(start, start + TILE)
                begin = start if causal else 0
                d_value = dot_nn(p_ref[rows, begin:], grad[begin:]).astype(bf16)
                d_key = dot_nn(ds_ref[rows, begin:], query[begin:]).astype(bf16)
                if second:
                    d_value = jnp.where(first_half, dqkv_ref[2, rows, lanes], d_value)
                    d_key = jnp.where(first_half, dqkv_ref[1, rows, lanes], d_key)
                dqkv_ref[2, rows, lanes] = d_value
                dqkv_ref[1, rows, lanes] = d_key
            if ds_out is not None:
                ds_out[head] = ds_ref[...]
        dqkv_ref[0, :, lanes] = dqt_ref[...].T.astype(bf16)
        return carry

    if causal:
        p_ref[...] = jnp.zeros_like(p_ref)
        ds_ref[...] = jnp.zeros_like(ds_ref)
    lax.fori_loop(0, qkv_ref.shape[2] // 128, pair, 0)


def head_sums(grad, mixed, dsum_ref):
    heads = dsum_ref.shape[0]
    product = grad.astype(f32) * mixed.astype(f32)
    width = product.shape[1]
    pick = (
        lax.broadcasted_iota(jnp.int32, (16, width), 1) // (width // heads)
        == lax.broadcasted_iota(jnp.int32, (16, width), 0)
    ).astype(f32)
    sums = lax.dot_general(
        pick, product, (((1,), (1,)), ((), ())),
        preferred_element_type=f32, precision=lax.Precision.HIGHEST,
    )
    for head in range(heads):
        dsum_ref[head] = sums[head : head + 1]


def fold_rows(core, turned, turned_ref, out_ref, fold):
    if not fold:
        out_ref[...] = turned
        return
    turned_ref[...] = turned
    total = turned.shape[0]
    size = total // 8
    for group in range(4):
        for place, which in ((0, core), (1, 1 - core)):
            begin = pl.multiple_of(group * 2 * size + which * size, 16)
            to = place * (total // 2) + group * size
            out_ref[to : to + size, :] = turned_ref[pl.ds(begin, size), :]


def weight_grad(left_ref, right, keep_ref, send_ref, index):
    half = left_ref.shape[0] // 2
    for start, size in tiles_of(right.shape[1]):
        product = dot_nn(left_ref[...], right[:, start : start + size]).astype(bf16)
        keep_ref[index, :, start : start + size] = product[:half]
        send_ref[index, :, start : start + size] = product[half:]


def start_weights(place, pieces, target_ref, sems, only=None):
    rows = target_ref.shape[1] // len(pieces)
    copies = []
    for d, piece in enumerate(pieces):
        begin = pl.multiple_of((place ^ d) * rows, rows) if len(pieces) > 1 else 0
        source = piece if only is None else piece.at[only]
        copies.append(
            pltpu.make_async_copy(source, target_ref.at[:, pl.ds(begin, rows), :], sems.at[d])
        )
        copies[-1].start()
    return copies


def join_rows(place, pieces, target_ref):
    rows = pieces[0].shape[0]
    for d, piece in enumerate(pieces):
        target_ref[pl.ds(pl.multiple_of((place ^ d) * rows, 16), rows), :] = piece[...]


def split_rows(place, source_ref, pieces):
    rows = pieces[0].shape[0]
    for d, piece in enumerate(pieces):
        piece[...] = source_ref[pl.ds(pl.multiple_of((place ^ d) * rows, 16), rows), :].astype(
            piece.dtype
        )


def first_kernel(at_ref, *refs, pieces, narrow, chunk):
    x_refs, refs = refs[:narrow], refs[narrow:]
    w_refs, refs = refs[:pieces], refs[pieces:]
    (extra_ref, table_ref, g_ref, x_ref, h_ref, qkv_ref, o_ref, peak_ref, inv_ref,
     ot_ref, w_ref, sems) = refs
    copies = start_weights(at_ref[3], w_refs, w_ref, sems)
    join_rows(at_ref[2], x_refs, x_ref)
    width = x_ref.shape[1]
    pick = (
        lax.broadcasted_iota(jnp.int32, (8, width), 1) % chunk
        == lax.broadcasted_iota(jnp.int32, (8, width), 0)
    ).astype(bf16)
    unit, _ = unit_of(x_ref[...].astype(f32))
    for copy in copies:
        copy.wait()
    gains = dot_nn(pick, w_ref[3])
    g_ref[...] = gains
    h_ref[...] = (unit * gains[0:1]).astype(bf16)
    for i in range(3):
        def store(start, size, product, i=i):
            qkv_ref[i, :, start : start + size] = product.astype(bf16)

        project(h_ref[...], w_ref, i, store)
    attend(qkv_ref, extra_ref, table_ref, o_ref, peak_ref, inv_ref, ot_ref)


def second_kernel(at_ref, *refs, pieces, narrow):
    m_refs, refs = refs[:narrow], refs[narrow:]
    w_refs, refs = refs[:pieces], refs[pieces:]
    (x_ref, o1_ref, extra_ref, g_ref, m_ref, x1_ref, h_ref, qkv_ref, o_ref, x2_ref, h3_ref,
     peak_ref, inv_ref, ot_ref, w_ref, sems) = refs
    copies = start_weights(at_ref[3], w_refs, w_ref, sems)
    join_rows(at_ref[2], m_refs, m_ref)
    for copy in copies:
        copy.wait()

    def store_x1(start, size, product):
        part = slice(start, start + size)
        x1_ref[:, part] = x_ref[:, part].astype(f32) + product

    project(o1_ref[...], w_ref, 0, store_x1)
    unit, _ = unit_of(x1_ref[...])
    h_ref[...] = (unit * g_ref[1:2, :]).astype(bf16)
    for i in range(3):
        def store(start, size, product, i=i):
            qkv_ref[i, :, start : start + size] = product.astype(bf16)

        project(m_ref[...] if i else h_ref[...], w_ref, i + 1, store)
    attend(qkv_ref, extra_ref, None, o_ref, peak_ref, inv_ref, ot_ref)

    def store_x2(start, size, product):
        part = slice(start, start + size)
        x2_ref[:, part] = x1_ref[:, part] + product

    project(o_ref[...], w_ref, 4, store_x2)
    unit, _ = unit_of(x2_ref[...])
    h3_ref[...] = (unit * g_ref[2:3, :]).astype(bf16)


def prepare_kernel(at_ref, *refs, narrow, bucket_count):
    in_refs, (index_ref, mask_ref, seg_ref, near_ref) = refs[:narrow], refs[narrow:]
    local = in_refs[0].shape[0] - 16
    for d, ref in enumerate(in_refs):
        lanes = pl.ds(pl.multiple_of((at_ref[2] ^ d) * local, 128), local)
        near_ref[:, lanes] = ref[:local, :].astype(f32).T
        tail = ref[local:, :].astype(f32)
        seg_ref[0:8, lanes] = jnp.broadcast_to(tail[0:1, :local], (8, local))
        seg_ref[8:16, lanes] = jnp.broadcast_to(tail[0:1, local : 2 * local], (8, local))
    seg = seg_ref[...]
    seg_t = seg.T
    tokens = near_ref.shape[0]
    key = lax.broadcasted_iota(jnp.int32, (tokens, tokens), 0)
    query = lax.broadcasted_iota(jnp.int32, (tokens, tokens), 1)
    allowed = (key <= query) & (seg_t[:, 0:1] == seg[0:1, :])
    index_ref[...] = jnp.where(allowed, near_ref[...], float(bucket_count)).astype(jnp.int32)
    mask_ref[...] = jnp.where(seg_t[:, 8:9] == seg[0:1, :], 0.0, NEG)


def order_kernel(at_ref, *refs):
    pieces, out_ref = refs[:-1], refs[-1]
    for d, piece in enumerate(pieces):
        if piece.ndim == 2:
            out_ref[at_ref[2] ^ d] = piece[...]
        else:
            out_ref[:, at_ref[2] ^ d] = piece[...]


def spread_kernel(at_ref, *refs, count):
    for i in range(count):
        keep_ref, recv_ref = refs[2 * i : 2 * i + 2]
        rows = keep_ref.shape[1] // 4
        for d in range(4):
            part = pl.ds(pl.multiple_of((at_ref[1] ^ d) * rows, 16), rows)
            out_ref = refs[2 * count + 4 * i + d]
            total = keep_ref[:, part, :].astype(f32) + recv_ref[:, part, :].astype(f32)
            out_ref[...] = total.astype(out_ref.dtype)


def narrow_kernel(at_ref, *refs, count, narrow):
    outs, scratch = refs[4 * count : (4 + narrow) * count], refs[(4 + narrow) * count :]
    for i in range(count):
        first, second, third, fourth = (ref[...].astype(f32) for ref in refs[4 * i : 4 * i + 4])
        scratch[i][...] = (first + second) + (third + fourth)
        rows = scratch[i].shape[1] // narrow
        for d in range(narrow):
            part = pl.ds(pl.multiple_of((at_ref[2] ^ d) * rows, 8), rows)
            out_ref = outs[narrow * i + d]
            out_ref[...] = scratch[i][:, part, :].astype(out_ref.dtype)


def total_kernel(*refs, count, narrow):
    for i in range(count):
        total = refs[narrow * i][...]
        for ref in refs[narrow * i + 1 : narrow * i + narrow]:
            total = total + ref[...].astype(f32)
        total_ref, rows_ref, cols_ref = refs[narrow * count + 3 * i : narrow * count + 3 * i + 3]
        total_ref[...] = total
        squares = total * total + 1e-30
        rows_ref[...] = jnp.sum(squares, axis=-1, keepdims=True)
        cols_ref[...] = jnp.sum(squares, axis=1, keepdims=True)


def ffn_kernel(at_ref, *refs, fold, narrow):
    c_refs, refs = refs[:narrow], refs[narrow:]
    (x2_ref, h_ref, g_ref, gate_ref, up_ref, wout_ref), refs = refs[:6], refs[6:]
    out_refs, refs = refs[:narrow], refs[narrow:]
    (dx_ref, dg_ref, kin_ref, sin_ref, kout_ref, sout_ref, acc_ref, dh_ref, turned_ref, ht_ref,
     gout_ref, c_ref) = refs
    step, steps = pl.program_id(0), pl.num_programs(0)
    core = at_ref[0]

    @pl.when(step == 0)
    def _():
        join_rows(at_ref[2], c_refs, c_ref)
        acc_ref[...] = x2_ref[...]
        dh_ref[...] = jnp.zeros_like(dh_ref)
        fold_rows(core, h_ref[...].T, turned_ref, ht_ref, fold)

    hidden_in, cot = h_ref[...], c_ref[...]
    for block in range(gate_ref.shape[0]):
        size = gate_ref.shape[2]
        part = slice(block * size, (block + 1) * size)
        gate = dot_nn(hidden_in, gate_ref[block])
        up = dot_nn(hidden_in, up_ref[block])
        square = gate * gate
        bent = jnp.tanh(0.7978845608028654 * (gate + 0.044715 * square * gate))
        plus = 0.5 * (1.0 + bent)
        act = gate * plus
        slope = plus + 0.5 * gate * (1.0 - bent * bent) * (
            0.7978845608028654 + (3 * 0.044715 * 0.7978845608028654) * square
        )
        hidden = (act * up).astype(bf16)
        down = jnp.concatenate([wout_ref[i, part, :] for i in range(wout_ref.shape[0])], axis=1)
        acc_ref[...] += dot_nn(hidden, down)
        grad = dot_nt(cot, down)
        d_gate = (grad * up * slope).astype(bf16)
        d_up = (grad * act).astype(bf16)
        dh_ref[...] += dot_nt(d_gate, gate_ref[block]) + dot_nt(d_up, up_ref[block])
        half = ht_ref.shape[0] // 2
        for index, right in ((0, d_gate), (1, d_up)):
            product = dot_nn(ht_ref[...], right).astype(bf16)
            kin_ref[index, :, part] = product[:half]
            sin_ref[index, :, part] = product[half:]
        gout_ref[part, :] = dot_nn(hidden.T, cot).astype(bf16)
    rows = gout_ref.shape[0] // 2
    kept = pl.multiple_of(core * rows, 16) if fold else 0
    sent = pl.multiple_of((1 - core) * rows, 16) if fold else rows
    kout_ref[...] = gout_ref[pl.ds(kept, rows), :]
    sout_ref[...] = gout_ref[pl.ds(sent, rows), :]

    @pl.when(step == steps - 1)
    def _():
        split_rows(at_ref[2], acc_ref, out_refs)
        back, d_gain = norm_back(dh_ref[...], x2_ref[...], g_ref[2:3, :])
        dx_ref[...] = cot.astype(f32) + back
        dg_ref[...] = d_gain


def cross_back_kernel(at_ref, *refs, pieces, narrow, fold):
    w_refs, refs = refs[:pieces], refs[pieces:]
    (dx2_ref, o_ref, h_ref, m_ref, x1_ref, o1_ref, qkv_ref, extra_ref, g_ref, peak_ref,
     inv_ref), refs = refs[:11], refs[11:]
    gm_refs, refs = refs[:narrow], refs[narrow:]
    (dx1_ref, dg_ref, keep_ref, send_ref, do_ref, dqkv_ref, dsum_ref, p_ref, ds_ref, dqt_ref,
     turned_ref, left_ref, gm_ref, w_ref, sems) = refs
    core = at_ref[0]
    copies = start_weights(at_ref[3], w_refs, w_ref, sems)
    branch = dx2_ref[...].astype(bf16)
    for copy in copies:
        copy.wait()
    for start, size in tiles_of(o_ref.shape[1]):
        do_ref[:, start : start + size] = dot_nt(
            branch, w_ref[4, start : start + size, :]
        ).astype(bf16)
    head_sums(do_ref[...], o_ref[...], dsum_ref)
    fold_rows(core, o_ref[...].T, turned_ref, left_ref, fold)
    weight_grad(left_ref, branch, keep_ref, send_ref, 4)
    attend_back(qkv_ref, extra_ref, None, do_ref, dsum_ref, peak_ref, inv_ref, dqkv_ref, p_ref,
                ds_ref, dqt_ref, None)
    fold_rows(core, h_ref[...].T, turned_ref, left_ref, fold)
    weight_grad(left_ref, dqkv_ref[0], keep_ref, send_ref, 1)
    fold_rows(core, m_ref[...].T, turned_ref, left_ref, fold)
    for i in (1, 2):
        weight_grad(left_ref, dqkv_ref[i], keep_ref, send_ref, i + 1)
    for start, size in tiles_of(o_ref.shape[1]):
        rows = slice(start, start + size)
        gm_ref[:, rows] = (
            dot_nt(dqkv_ref[1], w_ref[2, rows, :]) + dot_nt(dqkv_ref[2], w_ref[3, rows, :])
        ).astype(bf16)
        dx1_ref[:, rows] = dot_nt(dqkv_ref[0], w_ref[1, rows, :])
    split_rows(at_ref[2], gm_ref, gm_refs)
    back, d_gain = norm_back(dx1_ref[...], x1_ref[...], g_ref[1:2, :])
    d_x1 = dx2_ref[...] + back
    dx1_ref[...] = d_x1
    dg_ref[...] = d_gain
    fold_rows(core, o1_ref[...].T, turned_ref, left_ref, fold)
    weight_grad(left_ref, d_x1.astype(bf16), keep_ref, send_ref, 0)


def self_back_kernel(at_ref, *refs, pieces, narrow, fold):
    w_refs, refs = refs[:pieces], refs[pieces:]
    wo_refs, refs = refs[:pieces], refs[pieces:]
    (dx1_ref, o_ref, h_ref, x_ref, qkv_ref, extra_ref, table_ref, g_ref, peak_ref,
     inv_ref), refs = refs[:10], refs[10:]
    gx_refs, refs = refs[:narrow], refs[narrow:]
    (dg_ref, keep_ref, send_ref, ds_out, do_ref, dqkv_ref, dsum_ref, p_ref, ds_ref, dqt_ref,
     turned_ref, left_ref, dh_ref, w_ref, wo_ref, sems, wo_sems) = refs
    core = at_ref[0]
    wo_copies = start_weights(at_ref[3], wo_refs, wo_ref, wo_sems, pl.ds(0, 1))
    copies = start_weights(at_ref[3], w_refs, w_ref, sems, pl.ds(0, 3))
    branch = dx1_ref[...].astype(bf16)
    for copy in wo_copies:
        copy.wait()
    for start, size in tiles_of(o_ref.shape[1]):
        do_ref[:, start : start + size] = dot_nt(
            branch, wo_ref[0, start : start + size, :]
        ).astype(bf16)
    head_sums(do_ref[...], o_ref[...], dsum_ref)
    attend_back(qkv_ref, extra_ref, table_ref, do_ref, dsum_ref, peak_ref, inv_ref, dqkv_ref,
                p_ref, ds_ref, dqt_ref, ds_out)
    fold_rows(core, h_ref[...].T, turned_ref, left_ref, fold)
    for i in range(3):
        weight_grad(left_ref, dqkv_ref[i], keep_ref, send_ref, i)
    for copy in copies:
        copy.wait()
    for start, size in tiles_of(o_ref.shape[1]):
        rows = slice(start, start + size)
        dh_ref[:, rows] = (
            dot_nt(dqkv_ref[0], w_ref[0, rows, :])
            + dot_nt(dqkv_ref[1], w_ref[1, rows, :])
            + dot_nt(dqkv_ref[2], w_ref[2, rows, :])
        )
    back, d_gain = norm_back(dh_ref[...], x_ref[...].astype(f32), g_ref[0:1, :])
    dh_ref[...] = dx1_ref[...] + back
    split_rows(at_ref[2], dh_ref, gx_refs)
    dg_ref[...] = d_gain


def table_kernel(ds_ref, index_ref, out_ref, acc_ref, *, buckets):
    heads, keys, queries = ds_ref.shape
    acc_ref[...] = jnp.zeros_like(acc_ref)

    def group(at, carry):
        rows = pl.ds(pl.multiple_of(at * 16, 16), 16)
        index = index_ref[rows, :]
        grads = ds_ref[:, rows, :].reshape(heads * 16, queries)
        hot = jnp.concatenate(
            [(index == b).astype(f32).astype(bf16) for b in range(buckets)], axis=0
        )
        acc_ref[...] += dot_nt(grads, hot)
        return carry

    lax.fori_loop(0, keys // 16, group, 0)
    shape = acc_ref.shape
    same = (
        lax.broadcasted_iota(jnp.int32, shape, 0) % 16
        == lax.broadcasted_iota(jnp.int32, shape, 1) % 16
    )
    kept = jnp.where(same, acc_ref[...], 0.0).reshape(heads, 16, shape[1]).sum(axis=1)
    gather = (
        lax.broadcasted_iota(jnp.int32, (shape[1], 128), 0) // 16
        == lax.broadcasted_iota(jnp.int32, (shape[1], 128), 1)
    ).astype(f32)
    out_ref[...] = lax.dot_general(
        kept, gather, (((1,), (0,)), ((), ())),
        preferred_element_type=f32, precision=lax.Precision.HIGHEST,
    )


def call(kernel, outs, scratch, limit, *args, scalars=1, loose=(), flops=0):
    spaces = [
        pltpu.SMEM if i < scalars else pl.ANY if i in loose else pltpu.VMEM
        for i in range(len(args))
    ]
    moved = sum(a.size * a.dtype.itemsize for a in (*args, *outs))
    return pl.pallas_call(
        kernel,
        out_shape=outs,
        in_specs=[pl.BlockSpec(memory_space=space) for space in spaces],
        out_specs=[pl.BlockSpec(memory_space=pltpu.VMEM)] * len(outs),
        scratch_shapes=scratch,
        compiler_params=pltpu.CompilerParams(vmem_limit_bytes=limit * MIB),
        cost_estimate=pl.CostEstimate(flops=flops, bytes_accessed=moved, transcendentals=0),
    )(*args)


def shape_of(shape, dtype):
    return jax.ShapeDtypeStruct(tuple(shape), dtype)


def permuted(value, wide_bits, narrow_bits):
    wide, narrow = lax.axis_size("wide"), lax.axis_size("narrow")
    pairs = [
        (w * narrow + n, (w ^ wide_bits) * narrow + (n ^ narrow_bits))
        for w in range(wide)
        for n in range(narrow)
    ]
    return lax.ppermute(value, BOTH, pairs)


def ordered(at, pieces):
    first = pieces[0]
    if first.ndim == 2:
        shape = (len(pieces),) + first.shape
    else:
        shape = first.shape[:1] + (len(pieces),) + first.shape[1:]
    return call(order_kernel, [shape_of(shape, first.dtype)], [], 16, at, *pieces)[0]


def gathered(at, local, fast):
    if not fast:
        return [lax.all_gather(local, BOTH, axis=1, tiled=True)]
    narrow = lax.axis_size("narrow")
    near = [local] + [permuted(local, 0, d) for d in range(1, narrow)]
    stack = ordered(at, near)
    stack = stack.reshape(stack.shape[0], -1, stack.shape[3])
    plane = [stack] + [permuted(stack, 2 * d, 0) for d in range(1, 4)]
    return [piece for part in plane for piece in (part, permuted(part, 1, 0))]


def local_stats(gradient):
    squares = gradient * gradient + 1e-30
    return (jnp.sum(squares, axis=-1), jnp.sum(squares, axis=-2))


def scattered(at, pairs, fast, narrow):
    if not fast:
        results = []
        for keep, send in pairs:
            whole = jnp.concatenate([keep, send], axis=1)
            if keep.shape[0] == 4:
                whole = whole.reshape(1, -1, whole.shape[2])
            total = lax.psum_scatter(whole, BOTH, scatter_dimension=1, tiled=True).astype(f32)
            results.append((total, *local_stats(total)))
        return results
    count = len(pairs)
    keeps, sends = [], []
    for keep, send in pairs:
        stack = 1 if keep.shape[0] == 4 else keep.shape[0]
        keeps.append(keep.reshape(stack, -1, keep.shape[2]))
        sends.append(send.reshape(keeps[-1].shape))
    flat = [v for keep, send in zip(keeps, sends) for v in (keep, permuted(send, 1, 0))]
    outs = [
        shape_of((k.shape[0], k.shape[1] // 4, k.shape[2]), bf16 if d else f32)
        for k in keeps
        for d in range(4)
    ]
    parts = call(functools.partial(spread_kernel, count=count), outs, [], 40, at, *flat)
    parts = [permuted(v, 2 * (i % 4), 0) if i % 4 else v for i, v in enumerate(parts)]
    wholes = [(k.shape[0], k.shape[1] // 4, k.shape[2]) for k in keeps]
    outs = [
        shape_of((k, rows // narrow, cols), bf16 if d else f32)
        for k, rows, cols in wholes
        for d in range(narrow)
    ]
    parts = call(
        functools.partial(narrow_kernel, count=count, narrow=narrow),
        outs, [pltpu.VMEM(shape, f32) for shape in wholes], 32, at, *parts,
    )
    parts = [permuted(v, 0, i % narrow) if i % narrow else v for i, v in enumerate(parts)]
    outs = []
    for k, rows, cols in wholes:
        rows //= narrow
        outs += [
            shape_of((k, rows, cols), f32), shape_of((k, rows, 1), f32), shape_of((k, 1, cols), f32)
        ]
    flat = call(
        functools.partial(total_kernel, count=count, narrow=narrow), outs, [], 16, *parts, scalars=0
    )
    return [
        (flat[3 * i], flat[3 * i + 1][:, :, 0], flat[3 * i + 2][:, 0]) for i in range(count)
    ]


def summed_all(parts, fast):
    if not fast:
        return lax.psum(parts, BOTH)
    sizes = [v.size for v in parts]
    flat = jnp.concatenate([v.reshape(-1) for v in parts])
    flat = jnp.pad(flat, (0, -flat.size % 1024)).reshape(-1, 128)
    for bits in (1, 2, 4):
        flat = flat + permuted(flat, bits, 0)
    flat = (flat + permuted(flat, 0, 1)) + (permuted(flat, 0, 2) + permuted(flat, 0, 3))
    flat = flat.reshape(-1)
    results, at = [], 0
    for part, size in zip(parts, sizes):
        results.append(flat[at : at + size].reshape(part.shape))
        at += size
    return results


def adafactor_step(gradient, weight, rows_stat, cols_stat, weight_rms):
    overall = jnp.sum(cols_stat, axis=-1)[..., None, None]
    estimate = rows_stat[..., :, None] * cols_stat[..., None, :] / overall
    return weight - 0.3 * weight_rms * gradient * lax.rsqrt(estimate)


def body(
    targets, memory, cotangent, target_segments, memory_segments, buckets,
    attn_in, attn_out, gains, ff_in, ff_out, bias_table,
):
    wide, narrow = lax.axis_size("wide"), lax.axis_size("narrow")
    at_wide, at_narrow = lax.axis_index("wide"), lax.axis_index("narrow")
    fast = wide == 8 and narrow == 4
    at = jnp.stack([at_wide % 2, at_wide // 2, at_narrow, at_wide]).astype(jnp.int32)
    width, ff_width = attn_in.shape[2], ff_in.shape[2]
    bucket_count, heads = bias_table.shape
    chunk = gains.shape[1]
    local_tokens = targets.shape[1]
    tokens = local_tokens * narrow
    assert targets.shape[0] == narrow

    def row_pieces(stacked):
        return [
            permuted(lax.dynamic_index_in_dim(stacked, at_narrow ^ d, 0, False), 0, d)
            if d
            else lax.dynamic_index_in_dim(stacked, at_narrow, 0, False)
            for d in range(narrow)
        ]

    def to_owners(pieces):
        return ordered(at, [permuted(v, 0, d) if d else v for d, v in enumerate(pieces)])

    x_pieces = row_pieces(targets)
    device = at_wide * narrow + at_narrow
    gain_rows = lax.dynamic_update_slice(
        jnp.zeros((chunk, width), bf16), gains.astype(bf16), (0, device * chunk)
    )
    w_first = gathered(at, jnp.concatenate([attn_in[:3].astype(bf16), gain_rows[None]]), fast)
    segments = jnp.concatenate([target_segments, memory_segments], axis=1).astype(bf16)
    segments = jnp.pad(segments, ((0, 0), (0, buckets.shape[1] - segments.shape[1])))
    near = jnp.concatenate(
        [
            jnp.broadcast_to(buckets.astype(bf16)[None], (narrow,) + buckets.shape),
            jnp.broadcast_to(segments[:, None], (narrow, 16, buckets.shape[1])),
        ],
        axis=1,
    )
    index, cross_mask = call(
        functools.partial(prepare_kernel, narrow=narrow, bucket_count=bucket_count),
        [shape_of((tokens, tokens), jnp.int32), shape_of((tokens, tokens), f32)],
        [pltpu.VMEM((16, tokens), f32), pltpu.VMEM((tokens, tokens), f32)],
        24, at, *row_pieces(near),
    )
    table = jnp.concatenate(
        [bias_table.T, jnp.full((heads, 128 - bucket_count), NEG, f32)], axis=1
    )
    m_pieces = row_pieces(memory)
    w_second = gathered(
        at, jnp.concatenate([attn_out[:1], attn_in[3:], attn_out[1:]]).astype(bf16), fast
    )
    c_pieces = row_pieces(cotangent)
    lanes = TILE
    fin_blocks = ff_in.astype(bf16).reshape(2, chunk, ff_width // lanes, lanes)
    fin_blocks = fin_blocks.transpose(0, 2, 1, 3).reshape(-1, chunk, lanes)
    out_rows_here = ff_out.shape[0]
    fout_blocks = ff_out.astype(bf16).reshape(out_rows_here, width // lanes, lanes)
    fout_blocks = fout_blocks.transpose(1, 0, 2).reshape(-1, chunk, lanes)
    w_ffn = lax.all_gather(
        jnp.concatenate([fin_blocks, fout_blocks]), BOTH, axis=1, tiled=True
    )
    w_fout = w_ffn[fin_blocks.shape[0] :].reshape(-1, wide * narrow, chunk, lanes)
    w_fout = w_fout.transpose(1, 0, 2, 3).reshape(wide * narrow, -1, out_rows_here, lanes)
    w_fout = w_fout.transpose(1, 0, 2, 3).reshape(-1, ff_width, lanes)

    row16 = shape_of((tokens, width), bf16)
    row32 = shape_of((tokens, width), f32)
    three = shape_of((3, tokens, width), bf16)
    stat = shape_of((heads, 1, tokens), f32)
    gain_out = shape_of((1, width), f32)
    piece16 = shape_of((local_tokens, width), bf16)
    pair_t = pltpu.VMEM((128, tokens), f32)
    pieces = len(w_first)
    weights = lambda count: pltpu.VMEM((count, width, width), bf16)
    sems = pltpu.SemaphoreType.DMA((pieces,))
    g, x, h1, qkv1, o1, peak1, inv1 = call(
        functools.partial(first_kernel, pieces=pieces, narrow=narrow, chunk=chunk),
        [shape_of((8, width), f32), row16, row16, three, row16, stat, stat],
        [pair_t, weights(4), sems], 48,
        at, *x_pieces, *w_first, index, table,
        loose=range(1 + narrow, 1 + narrow + pieces),
    )
    m, x1, h2, qkv2, o2, x2, h3, peak2, inv2 = call(
        functools.partial(second_kernel, pieces=pieces, narrow=narrow),
        [row16, row32, row16, three, row16, row32, row16, stat, stat],
        [pair_t, weights(5), sems], 48,
        at, *m_pieces, *w_second, x, o1, cross_mask, g,
        loose=range(1 + narrow, 1 + narrow + pieces),
    )

    steps = 4
    part = ff_width // steps
    blocks = part // lanes
    half = width // 2
    whole = lambda shape: pl.BlockSpec(shape, lambda i: (0,) * len(shape))
    outs = pl.pallas_call(
        functools.partial(ffn_kernel, fold=fast, narrow=narrow),
        grid=(steps,),
        in_specs=[pl.BlockSpec(memory_space=pltpu.SMEM)]
        + [whole((local_tokens, width))] * narrow
        + [
            whole((tokens, width)), whole((tokens, width)), whole((8, width)),
            pl.BlockSpec((blocks, width, lanes), lambda i: (i, 0, 0)),
            pl.BlockSpec((blocks, width, lanes), lambda i: (i + steps, 0, 0)),
            pl.BlockSpec((width // lanes, part, lanes), lambda i: (0, i, 0)),
        ],
        out_specs=[whole((local_tokens, width))] * narrow
        + [
            whole((tokens, width)), whole((1, width)),
            pl.BlockSpec((2, half, part), lambda i: (0, 0, i)),
            pl.BlockSpec((2, half, part), lambda i: (0, 0, i)),
            pl.BlockSpec((None, part // 2, width), lambda i: (i, 0, 0)),
            pl.BlockSpec((None, part // 2, width), lambda i: (i, 0, 0)),
        ],
        out_shape=[piece16] * narrow
        + [
            row32, gain_out,
            shape_of((2, half, ff_width), bf16), shape_of((2, half, ff_width), bf16),
            shape_of((steps, part // 2, width), bf16), shape_of((steps, part // 2, width), bf16),
        ],
        scratch_shapes=[
            pltpu.VMEM((tokens, width), f32), pltpu.VMEM((tokens, width), f32),
            pltpu.VMEM((width, tokens), bf16), pltpu.VMEM((width, tokens), bf16),
            pltpu.VMEM((part, width), bf16), pltpu.VMEM((tokens, width), bf16),
        ],
        compiler_params=pltpu.CompilerParams(vmem_limit_bytes=48 * MIB),
        cost_estimate=pl.CostEstimate(
            flops=18 * tokens * width * ff_width, bytes_accessed=20 * MIB, transcendentals=0
        ),
    )(at, *c_pieces, x2, h3, g, w_ffn, w_ffn, w_fout)
    output = to_owners(outs[:narrow])
    dx2, gain3, keep_fin, send_fin, keep_fout, send_fout = outs[narrow:]
    (sum_fin, fin_rows, fin_part), (sum_fout, fout_rows, fout_part) = scattered(
        at, [(keep_fin, send_fin), (keep_fout, send_fout)], fast, narrow
    )

    square = pltpu.VMEM((tokens, tokens), bf16)
    back_scratch = [
        pltpu.VMEM((tokens, width), bf16), pltpu.VMEM((3, tokens, width), bf16),
        pltpu.VMEM((heads, 1, tokens), f32), square, square, pair_t,
        pltpu.VMEM((width, tokens), bf16), pltpu.VMEM((width, tokens), bf16),
    ]
    grads = lambda count: shape_of((count, half, width), bf16)
    outs = call(
        functools.partial(cross_back_kernel, pieces=pieces, narrow=narrow, fold=fast),
        [piece16] * narrow + [row32, gain_out, grads(5), grads(5)],
        back_scratch + [pltpu.VMEM((tokens, width), bf16), weights(5), sems], 52,
        at, *w_second, dx2, o2, h2, m, x1, o1, qkv2, cross_mask, g, peak2, inv2,
        loose=range(1, 1 + pieces),
    )
    grad_memory = to_owners(outs[:narrow])
    dx1, gain2, keep_second, send_second = outs[narrow:]
    ((sum_second, second_rows, second_part),) = scattered(
        at, [(keep_second, send_second)], fast, narrow
    )
    outs = call(
        functools.partial(self_back_kernel, pieces=pieces, narrow=narrow, fold=fast),
        [piece16] * narrow
        + [gain_out, grads(3), grads(3), shape_of((heads, tokens, tokens), bf16)],
        back_scratch + [pltpu.VMEM((tokens, width), f32), weights(3), weights(1), sems, sems], 60,
        at, *w_first, *w_second, dx1, o1, h1, x, qkv1, index, table, g, peak1, inv1,
        loose=range(1, 1 + 2 * pieces),
    )
    grad_targets = to_owners(outs[:narrow])
    gain1, keep_first, send_first, ds = outs[narrow:]
    ((sum_first, first_rows, first_part),) = scattered(
        at, [(keep_first, send_first)], fast, narrow
    )
    (table_part,) = call(
        functools.partial(table_kernel, buckets=bucket_count),
        [shape_of((heads, 128), f32)],
        [pltpu.VMEM((heads * 16, bucket_count * 16), f32)], 32, ds, index, scalars=0,
    )
    table_part = table_part[:, :bucket_count].T

    def regroup(first, second):
        return jnp.concatenate([first, second[1:4]]), jnp.stack([second[0], second[4]])

    sum_in, sum_out = regroup(sum_first, sum_second)
    in_rows, out_rows = regroup(first_rows, second_rows)
    in_part, out_part = regroup(first_part, second_part)
    sum_fout, fout_rows, fout_part = sum_fout[0], fout_rows[0], fout_part[0]
    gain_part = jnp.concatenate([gain1, gain2, gain3])
    in_square = jnp.sum(attn_in * attn_in, axis=(1, 2))
    out_square = jnp.sum(attn_out * attn_out, axis=(1, 2))
    fin_square = jnp.sum(ff_in * ff_in, axis=(1, 2))
    fout_square = jnp.sum(ff_out * ff_out).reshape(1)
    (
        sum_gain, in_cols, out_cols, fin_cols, fout_cols, grad_table,
        in_total, out_total, fin_total, fout_total,
    ) = summed_all(
        (
            gain_part, in_part, out_part, fin_part, fout_part, table_part,
            in_square, out_square, fin_square, fout_square,
        ),
        fast,
    )
    sum_gain = lax.dynamic_slice_in_dim(sum_gain, device * chunk, chunk, 1)
    table_rows, table_cols = local_stats(grad_table)
    in_rms = jnp.sqrt(in_total / (width * width) + 1e-06)[:, None, None]
    out_rms = jnp.sqrt(out_total / (width * width) + 1e-06)[:, None, None]
    fin_rms = jnp.sqrt(fin_total / (width * ff_width) + 1e-06)[:, None, None]
    fout_rms = jnp.sqrt(fout_total[0] / (width * ff_width) + 1e-06)
    table_rms = jnp.sqrt(jnp.mean(bias_table * bias_table) + 1e-06)
    return (
        output, grad_targets, grad_memory,
        sum_in, sum_out, sum_gain, sum_fin, sum_fout, grad_table,
        in_rows, in_cols, out_rows, out_cols, fin_rows, fin_cols, fout_rows, fout_cols,
        adafactor_step(sum_in, attn_in, in_rows, in_cols, in_rms),
        adafactor_step(sum_out, attn_out, out_rows, out_cols, out_rms),
        adafactor_step(sum_fin, ff_in, fin_rows, fin_cols, fin_rms),
        adafactor_step(sum_fout, ff_out, fout_rows, fout_cols, fout_rms),
        adafactor_step(grad_table, bias_table, table_rows, table_cols, table_rms),
    )


def solution(mesh):
    in_specs = (
        P("wide", "narrow", None),
        P("wide", "narrow", None),
        P("wide", "narrow", None),
        P("wide", "narrow"),
        P("wide", "narrow"),
        P("narrow", None),
        P(None, ("wide", "narrow"), None),
        P(None, ("wide", "narrow"), None),
        P(None, ("wide", "narrow")),
        P(None, ("wide", "narrow"), None),
        P(("wide", "narrow"), None),
        P(),
    )
    out_specs = (
        P("wide", "narrow", None),
        P("wide", "narrow", None),
        P("wide", "narrow", None),
        P(None, ("wide", "narrow"), None),
        P(None, ("wide", "narrow"), None),
        P(None, ("wide", "narrow")),
        P(None, ("wide", "narrow"), None),
        P(("wide", "narrow"), None),
        P(),
        P(None, ("wide", "narrow")),
        P(),
        P(None, ("wide", "narrow")),
        P(),
        P(None, ("wide", "narrow")),
        P(),
        P(("wide", "narrow")),
        P(),
        P(None, ("wide", "narrow"), None),
        P(None, ("wide", "narrow"), None),
        P(None, ("wide", "narrow"), None),
        P(("wide", "narrow"), None),
        P(),
    )
    return jax.shard_map(body, mesh=mesh, in_specs=in_specs, out_specs=out_specs, check_vma=False)
```

```python
import functools
import math

import jax
import jax.numpy as jnp
from jax import lax
from jax.experimental import pallas as pl
from jax.experimental.pallas import tpu as pltpu
from jax.sharding import PartitionSpec as P

bf16, f32 = jnp.bfloat16, jnp.float32
BOTH = ("wide", "narrow")
NEG = -1e9
TILE = 256
MIB = 1 << 20


def dot_nn(left, right):
    return lax.dot_general(left, right, (((1,), (0,)), ((), ())), preferred_element_type=f32)


def dot_nt(left, right):
    return lax.dot_general(left, right, (((1,), (1,)), ((), ())), preferred_element_type=f32)


def unit_of(values):
    inv_rms = lax.rsqrt(jnp.mean(values * values, axis=-1, keepdims=True) + 1e-06)
    return values * inv_rms, inv_rms


def norm_back(incoming, values, gain_row):
    unit, inv_rms = unit_of(values)
    scaled = incoming * gain_row
    inner = jnp.mean(scaled * unit, axis=-1, keepdims=True)
    return inv_rms * (scaled - unit * inner), jnp.sum(incoming * unit, axis=0, keepdims=True)


def tiles_of(width):
    return [(start, min(TILE, width - start)) for start in range(0, width, TILE)]


def project(left, w_ref, index, store):
    for start, size in tiles_of(w_ref.shape[2]):
        store(start, size, dot_nn(left, w_ref[index, :, start : start + size]))


def half_lanes(second):
    lane = lax.broadcasted_iota(jnp.int32, (1, 128), 1)
    return ((lane >= 64) == bool(second)).astype(bf16)


def biased(table_row, index):
    spread = jnp.broadcast_to(table_row, (index.shape[0], 128))
    return jnp.concatenate(
        [
            jnp.take_along_axis(
                spread, index[:, at : at + 128], axis=1, mode="promise_in_bounds"
            )
            for at in range(0, index.shape[1], 128)
        ],
        axis=1,
    )


def query_blocks(keys, queries, causal):
    return [
        (at, min(keys, at + TILE) if causal else keys) for at in range(0, queries, TILE)
    ]


def attend(qkv_ref, extra_ref, table_ref, o_ref, peak_ref, inv_ref, ot_ref):
    causal = table_ref is not None
    keys = qkv_ref.shape[1]

    def pair(at_pair, carry):
        lanes = pl.ds(pl.multiple_of(at_pair * 128, 128), 128)
        query, key, value = (qkv_ref[i, :, lanes] for i in range(3))
        value_t = value.T
        for second in range(2):
            head = at_pair * 2 + second
            key_half = key * half_lanes(second)
            for start, last in query_blocks(keys, keys, causal):
                part = slice(start, start + TILE)
                scores = dot_nt(key_half[:last], query[part])
                if causal:
                    scores += biased(table_ref[pl.ds(head, 1), :], extra_ref[:last, part])
                else:
                    scores += extra_ref[:last, part]
                peak = jnp.max(scores, axis=0, keepdims=True)
                grown = jnp.exp(scores - peak)
                inverse = 1.0 / jnp.sum(grown, axis=0, keepdims=True)
                mixed = dot_nn(value_t[second * 64 : second * 64 + 64, :last], grown.astype(bf16))
                ot_ref[second * 64 : second * 64 + 64, part] = mixed * inverse
                peak_ref[head, :, part] = peak
                inv_ref[head, :, part] = inverse
        o_ref[:, lanes] = ot_ref[...].T.astype(bf16)
        return carry

    lax.fori_loop(0, qkv_ref.shape[2] // 128, pair, 0)


def attend_back(
    qkv_ref, extra_ref, table_ref, do_ref, dsum_ref, peak_ref, inv_ref,
    dqkv_ref, p_ref, ds_ref, dqt_ref, ds_out,
):
    causal = table_ref is not None
    keys = qkv_ref.shape[1]
    first_half = lax.broadcasted_iota(jnp.int32, (1, 128), 1) < 64

    def pair(at_pair, carry):
        lanes = pl.ds(pl.multiple_of(at_pair * 128, 128), 128)
        query, key, value = (qkv_ref[i, :, lanes] for i in range(3))
        grad = do_ref[:, lanes]
        key_t = key.T
        for second in range(2):
            head = at_pair * 2 + second
            half = half_lanes(second)
            key_half, value_half = key * half, value * half
            for start, last in query_blocks(keys, keys, causal):
                part = slice(start, start + TILE)
                scores = dot_nt(key_half[:last], query[part])
                if causal:
                    scores += biased(table_ref[pl.ds(head, 1), :], extra_ref[:last, part])
                else:
                    scores += extra_ref[:last, part]
                weights = jnp.exp(scores - peak_ref[head, :, part]) * inv_ref[head, :, part]
                grad_weights = dot_nt(value_half[:last], grad[part])
                grad_scores = (weights * (grad_weights - dsum_ref[head, :, part])).astype(bf16)
                p_ref[:last, part] = weights.astype(bf16)
                ds_ref[:last, part] = grad_scores
                dqt_ref[second * 64 : second * 64 + 64, part] = dot_nn(
                    key_t[second * 64 : second * 64 + 64, :last], grad_scores
                )
            for start in range(0, keys, TILE):
                rows = slice(start, start + TILE)
                begin = start if causal else 0
                d_value = dot_nn(p_ref[rows, begin:], grad[begin:]).astype(bf16)
                d_key = dot_nn(ds_ref[rows, begin:], query[begin:]).astype(bf16)
                if second:
                    d_value = jnp.where(first_half, dqkv_ref[2, rows, lanes], d_value)
                    d_key = jnp.where(first_half, dqkv_ref[1, rows, lanes], d_key)
                dqkv_ref[2, rows, lanes] = d_value
                dqkv_ref[1, rows, lanes] = d_key
            if ds_out is not None:
                ds_out[head] = ds_ref[...]
        dqkv_ref[0, :, lanes] = dqt_ref[...].T.astype(bf16)
        return carry

    if causal:
        p_ref[...] = jnp.zeros_like(p_ref)
        ds_ref[...] = jnp.zeros_like(ds_ref)
    lax.fori_loop(0, qkv_ref.shape[2] // 128, pair, 0)


def head_sums(grad, mixed, dsum_ref):
    heads = dsum_ref.shape[0]
    product = grad.astype(f32) * mixed.astype(f32)
    width = product.shape[1]
    pick = (
        lax.broadcasted_iota(jnp.int32, (16, width), 1) // (width // heads)
        == lax.broadcasted_iota(jnp.int32, (16, width), 0)
    ).astype(f32)
    sums = lax.dot_general(
        pick, product, (((1,), (1,)), ((), ())),
        preferred_element_type=f32, precision=lax.Precision.HIGHEST,
    )
    for head in range(heads):
        dsum_ref[head] = sums[head : head + 1]


def fold_rows(core, turned, turned_ref, out_ref, fold):
    if not fold:
        out_ref[...] = turned
        return
    turned_ref[...] = turned
    total = turned.shape[0]
    size = total // 8
    for group in range(4):
        for place, which in ((0, core), (1, 1 - core)):
            begin = pl.multiple_of(group * 2 * size + which * size, 16)
            to = place * (total // 2) + group * size
            out_ref[to : to + size, :] = turned_ref[pl.ds(begin, size), :]


def weight_grad(left_ref, right_ref, keep_ref, send_ref, index):
    half = left_ref.shape[0] // 2
    for start, size in tiles_of(right_ref.shape[1]):
        part = slice(start, start + size)
        right = right_ref[:, part]
        keep_ref[index, :, part] = dot_nn(left_ref[:half], right).astype(bf16)
        send_ref[index, :, part] = dot_nn(left_ref[half:], right).astype(bf16)


def start_weights(place, pieces, target_ref, sems, only=None):
    rows = target_ref.shape[1] // len(pieces)
    copies = []
    for d, piece in enumerate(pieces):
        begin = pl.multiple_of((place ^ d) * rows, rows) if len(pieces) > 1 else 0
        source = piece if only is None else piece.at[only]
        copies.append(
            pltpu.make_async_copy(source, target_ref.at[:, pl.ds(begin, rows), :], sems.at[d])
        )
        copies[-1].start()
    return copies


def join_rows(place, pieces, which, target_ref):
    rows = pieces[0].shape[1]
    for d, piece in enumerate(pieces):
        target_ref[pl.ds(pl.multiple_of((place ^ d) * rows, 16), rows), :] = piece[which]


def join_blocks(place, pieces, target_ref):
    blocks = target_ref.shape[1] // TILE
    rows = target_ref.shape[0] // len(pieces)
    for d, piece in enumerate(pieces):
        to = pl.ds(pl.multiple_of((place ^ d) * rows, 16), rows)
        for j in range(blocks):
            target_ref[to, j * TILE : (j + 1) * TILE] = piece[j * rows : (j + 1) * rows, :]


def pack_kernel(at_ref, x_ref, m_ref, c_ref, buckets_ref, seg_t_ref, seg_m_ref, *outs, narrow):
    local, width = x_ref.shape[1:]
    for d in range(narrow):
        first, both = outs[d], outs[narrow + d]
        row = at_ref[2] ^ d
        both[0] = m_ref[row]
        both[1] = c_ref[row]
        begin = 0
        for j in range(width // TILE):
            first[begin : begin + local, :] = x_ref[row, :, j * TILE : (j + 1) * TILE]
            begin += local
        for j in range(buckets_ref.shape[1] // TILE):
            part = buckets_ref[:, j * TILE : (j + 1) * TILE]
            first[begin : begin + local, :] = part.astype(f32).astype(bf16)
            begin += local
        for i, ref in enumerate((seg_t_ref, seg_m_ref)):
            seg = jnp.broadcast_to(ref[pl.ds(row, 1), :].astype(f32), (16, local))
            first[begin : begin + 16, i * local : (i + 1) * local] = seg.astype(bf16)


def split_rows(place, source_ref, pieces):
    rows = pieces[0].shape[0]
    for d, piece in enumerate(pieces):
        piece[...] = source_ref[pl.ds(pl.multiple_of((place ^ d) * rows, 16), rows), :].astype(
            piece.dtype
        )


def first_kernel(at_ref, *refs, pieces, narrow, chunk):
    x_refs, refs = refs[:narrow], refs[narrow:]
    w_refs, refs = refs[:pieces], refs[pieces:]
    (extra_ref, table_ref, g_ref, x_ref, h_ref, qkv_ref, o_ref, peak_ref, inv_ref,
     ot_ref, w_ref, sems) = refs
    copies = start_weights(at_ref[3], w_refs, w_ref, sems)
    join_blocks(at_ref[2], x_refs, x_ref)
    width = x_ref.shape[1]
    pick = (
        lax.broadcasted_iota(jnp.int32, (8, width), 1) % chunk
        == lax.broadcasted_iota(jnp.int32, (8, width), 0)
    ).astype(bf16)
    unit, _ = unit_of(x_ref[...].astype(f32))
    for copy in copies:
        copy.wait()
    gains = dot_nn(pick, w_ref[3])
    g_ref[...] = gains
    h_ref[...] = (unit * gains[0:1]).astype(bf16)
    for i in range(3):
        def store(start, size, product, i=i):
            qkv_ref[i, :, start : start + size] = product.astype(bf16)

        project(h_ref[...], w_ref, i, store)
    attend(qkv_ref, extra_ref, table_ref, o_ref, peak_ref, inv_ref, ot_ref)


def second_kernel(at_ref, *refs, pieces, narrow):
    m_refs, refs = refs[:narrow], refs[narrow:]
    w_refs, refs = refs[:pieces], refs[pieces:]
    (x_ref, o1_ref, extra_ref, g_ref, m_ref, c_ref, x1_ref, h_ref, qkv_ref, o_ref, x2_ref, h3_ref,
     peak_ref, inv_ref, ot_ref, w_ref, sems) = refs
    copies = start_weights(at_ref[3], w_refs, w_ref, sems)
    join_rows(at_ref[2], m_refs, 0, m_ref)
    join_rows(at_ref[2], m_refs, 1, c_ref)
    for copy in copies:
        copy.wait()

    def store_x1(start, size, product):
        part = slice(start, start + size)
        x1_ref[:, part] = x_ref[:, part].astype(f32) + product

    project(o1_ref[...], w_ref, 0, store_x1)
    unit, _ = unit_of(x1_ref[...])
    h_ref[...] = (unit * g_ref[1:2, :]).astype(bf16)
    for i in range(3):
        def store(start, size, product, i=i):
            qkv_ref[i, :, start : start + size] = product.astype(bf16)

        project(m_ref[...] if i else h_ref[...], w_ref, i + 1, store)
    attend(qkv_ref, extra_ref, None, o_ref, peak_ref, inv_ref, ot_ref)

    def store_x2(start, size, product):
        part = slice(start, start + size)
        x2_ref[:, part] = x1_ref[:, part] + product

    project(o_ref[...], w_ref, 4, store_x2)
    unit, _ = unit_of(x2_ref[...])
    h3_ref[...] = (unit * g_ref[2:3, :]).astype(bf16)


def prepare_kernel(at_ref, *refs, narrow, bucket_count, skip):
    in_refs, (index_ref, mask_ref, seg_ref, near_ref) = refs[:narrow], refs[narrow:]
    tokens = near_ref.shape[0]
    local = tokens // narrow
    for d, ref in enumerate(in_refs):
        lanes = pl.ds(pl.multiple_of((at_ref[2] ^ d) * local, 128), local)
        begin = skip
        for j in range(tokens // TILE):
            near_ref[j * TILE : (j + 1) * TILE, lanes] = (
                ref[begin : begin + local, :].astype(f32).T
            )
            begin += local
        tail = ref[begin : begin + 16, :].astype(f32)
        seg_ref[0:8, lanes] = tail[:8, :local]
        seg_ref[8:16, lanes] = tail[:8, local : 2 * local]
    seg = seg_ref[...]
    seg_t = seg.T
    key = lax.broadcasted_iota(jnp.int32, (tokens, tokens), 0)
    query = lax.broadcasted_iota(jnp.int32, (tokens, tokens), 1)
    allowed = (key <= query) & (seg_t[:, 0:1] == seg[0:1, :])
    index_ref[...] = jnp.where(allowed, near_ref[...], float(bucket_count)).astype(jnp.int32)
    mask_ref[...] = jnp.where(seg_t[:, 8:9] == seg[0:1, :], 0.0, NEG)


def order_kernel(at_ref, *refs, outs):
    pieces, out_refs = refs[:-outs], refs[-outs:]
    for d, piece in enumerate(pieces):
        if piece.ndim == 2:
            out_refs[0][at_ref[2] ^ d] = piece[...]
            continue
        begin = 0
        for out_ref in out_refs:
            size = out_ref.shape[0]
            out_ref[:, at_ref[2] ^ d] = piece[begin : begin + size]
            begin += size


def read_part(refs, group):
    if len(refs) == 1:
        count, rows, cols = refs[0].shape
        rows //= 4
        part = pl.ds(pl.multiple_of(group * rows, 16), rows)
        return refs[0][:, part, :].astype(f32).reshape(count * rows, cols)
    fin, fout = refs
    rows, rows_out = fin.shape[1] // 4, fout.shape[1] // 4
    part = pl.ds(pl.multiple_of(group * rows, 16), rows)
    part_out = pl.ds(pl.multiple_of(group * rows_out, 16), rows_out)
    pieces = [
        fin[i, part, at : at + TILE].astype(f32)
        for i in range(fin.shape[0])
        for at in range(0, fin.shape[2], TILE)
    ]
    pieces += [
        fout[0, part_out, at : at + TILE].astype(f32) for at in range(0, fout.shape[2], TILE)
    ]
    return jnp.concatenate(pieces, axis=0)


def spread_kernel(at_ref, *refs, count):
    keeps, recvs = refs[:count], refs[count : 2 * count]
    own_ref, kept_x, kept_y, to_x, to_y = refs[2 * count :]
    half = own_ref.shape[0] // 2
    for d in range(4):
        total = read_part(keeps, at_ref[1] ^ d) + read_part(recvs, at_ref[1] ^ d)
        if d == 0:
            own_ref[...] = total
        elif d == 1:
            to_x[0] = total[:half].astype(bf16)
            kept_x[...] = total[half:]
        elif d == 2:
            to_y[0] = total[half:].astype(bf16)
            kept_y[...] = total[:half]
        else:
            to_x[1] = total[:half].astype(bf16)
            to_y[1] = total[half:].astype(bf16)


def middle_kernel(own_ref, kept_x, kept_y, from_x, from_y, sum_ref, to_x, to_y):
    half = own_ref.shape[0] // 2
    sum_ref[:half, :] = own_ref[:half, :] + from_x[0].astype(f32)
    sum_ref[half:, :] = own_ref[half:, :] + from_y[0].astype(f32)
    to_y[...] = (kept_y[...] + from_x[1].astype(f32)).astype(bf16)
    to_x[...] = (kept_x[...] + from_y[1].astype(f32)).astype(bf16)


def narrow_kernel(at_ref, own_ref, from_x, from_y, *refs, narrow, spots):
    outs, sum_ref = refs[:-1], refs[-1]
    half = own_ref.shape[0] // 2
    sum_ref[:half, :] = own_ref[:half, :] + from_y[...].astype(f32)
    sum_ref[half:, :] = own_ref[half:, :] + from_x[...].astype(f32)
    for d, out_ref in enumerate(outs):
        place = at_ref[2] ^ d
        out_ref[...] = jnp.concatenate(
            [
                sum_ref[pl.ds(start + pl.multiple_of(place * rows, 8), rows), :]
                for start, rows in spots
            ],
            axis=0,
        ).astype(out_ref.dtype)


def total_kernel(*refs, narrow):
    total = refs[0][...]
    for ref in refs[1:narrow]:
        total = total + ref[...].astype(f32)
    outs = refs[narrow:]
    at = 0
    for total_ref, rows_ref, cols_ref in zip(*(outs[i::3] for i in range(3))):
        count, rows, cols = total_ref.shape
        block = total.shape[1]
        if cols == block:
            total_ref[...] = total[at : at + count * rows].reshape(count, rows, cols)
            at += count * rows
        else:
            for i in range(count):
                for j in range(cols // block):
                    total_ref[i, :, j * block : (j + 1) * block] = total[at : at + rows]
                    at += rows
        squares = total_ref[...]
        squares = squares * squares + 1e-30
        rows_ref[...] = jnp.sum(squares, axis=-1, keepdims=True)
        cols_ref[...] = jnp.sum(squares, axis=1, keepdims=True)


def ffn_kernel(at_ref, *refs, fold, narrow, pieces, first_out):
    c_ref, refs = refs[0], refs[1:]
    fin_refs, refs = refs[:pieces], refs[pieces:]
    fout_refs, refs = refs[:pieces], refs[pieces:]
    (x2_ref, h_ref, g_ref), refs = refs[:3], refs[3:]
    out_refs, refs = refs[:narrow], refs[narrow:]
    (dx_ref, dg_ref, kin_ref, sin_ref, kout_ref, sout_ref, acc_ref, dh_ref, turned_ref, ht_ref,
     gout_ref, fin_ref, fout_ref, fin_sems, fout_sems) = refs
    step, steps = pl.program_id(0), pl.num_programs(0)
    core = at_ref[0]

    @pl.when(step == 0)
    def _():
        copies = start_weights(at_ref[3], fin_refs, fin_ref, fin_sems, pl.ds(0, fin_ref.shape[0]))
        copies += start_weights(
            at_ref[3], fout_refs, fout_ref, fout_sems, pl.ds(first_out, fout_ref.shape[0])
        )
        acc_ref[...] = x2_ref[...]
        dh_ref[...] = jnp.zeros_like(dh_ref)
        fold_rows(core, h_ref[...].T, turned_ref, ht_ref, fold)
        for copy in copies:
            copy.wait()

    hidden_in, cot = h_ref[...], c_ref[...]
    size = fin_ref.shape[2]
    blocks = gout_ref.shape[0] // size
    for block in range(blocks):
        part = slice(block * size, (block + 1) * size)
        at_gate = step * blocks + block
        at_up = fin_ref.shape[0] // 2 + at_gate
        gate = dot_nn(hidden_in, fin_ref[at_gate])
        up = dot_nn(hidden_in, fin_ref[at_up])
        square = gate * gate
        bent = jnp.tanh(0.7978845608028654 * (gate + 0.044715 * square * gate))
        plus = 0.5 * (1.0 + bent)
        act = gate * plus
        slope = plus + 0.5 * gate * (1.0 - bent * bent) * (
            0.7978845608028654 + (3 * 0.044715 * 0.7978845608028654) * square
        )
        hidden = (act * up).astype(bf16)
        down_rows = pl.ds(pl.multiple_of(at_gate * size, size), size)
        down = jnp.concatenate(
            [fout_ref[i, down_rows, :] for i in range(fout_ref.shape[0])], axis=1
        )
        acc_ref[...] += dot_nn(hidden, down)
        grad = dot_nt(cot, down)
        d_gate = (grad * up * slope).astype(bf16)
        d_up = (grad * act).astype(bf16)
        dh_ref[...] += dot_nt(d_gate, fin_ref[at_gate]) + dot_nt(d_up, fin_ref[at_up])
        half = ht_ref.shape[0] // 2
        for index, right in ((0, d_gate), (1, d_up)):
            product = dot_nn(ht_ref[...], right).astype(bf16)
            kin_ref[index, :, part] = product[:half]
            sin_ref[index, :, part] = product[half:]
        gout_ref[part, :] = dot_nn(hidden.T, cot).astype(bf16)
    rows = gout_ref.shape[0] // 2
    kept = pl.multiple_of(core * rows, 16) if fold else 0
    sent = pl.multiple_of((1 - core) * rows, 16) if fold else rows
    kout_ref[...] = gout_ref[pl.ds(kept, rows), :]
    sout_ref[...] = gout_ref[pl.ds(sent, rows), :]

    @pl.when(step == steps - 1)
    def _():
        split_rows(at_ref[2], acc_ref, out_refs)
        back, d_gain = norm_back(dh_ref[...], x2_ref[...], g_ref[2:3, :])
        dx_ref[...] = cot.astype(f32) + back
        dg_ref[...] = d_gain


def attend_back_kernel(at_ref, *refs, pieces, which, causal):
    w_refs, refs = refs[:pieces], refs[pieces:]
    table_ref = None
    if causal:
        table_ref, refs = refs[0], refs[1:]
    dx_ref, o_ref, qkv_ref, extra_ref, peak_ref, inv_ref, dqkv_ref = refs[:7]
    ds_out, refs = (refs[7], refs[8:]) if causal else (None, refs[7:])
    do_ref, dsum_ref, p_ref, ds_ref, dqt_ref, w_ref, sems = refs
    copies = start_weights(at_ref[3], w_refs, w_ref, sems, pl.ds(which, 1))
    branch = dx_ref[...].astype(bf16)
    for copy in copies:
        copy.wait()
    for start, size in tiles_of(o_ref.shape[1]):
        do_ref[:, start : start + size] = dot_nt(
            branch, w_ref[0, start : start + size, :]
        ).astype(bf16)
    head_sums(do_ref[...], o_ref[...], dsum_ref)
    attend_back(qkv_ref, extra_ref, table_ref, do_ref, dsum_ref, peak_ref, inv_ref, dqkv_ref,
                p_ref, ds_ref, dqt_ref, ds_out)


def second_back_kernel(at_ref, *refs, pieces, narrow, fold):
    w_refs, refs = refs[:pieces], refs[pieces:]
    (dqkv_ref, dx2_ref, o_ref, h_ref, m_ref, x1_ref, o1_ref, g_ref), refs = refs[:8], refs[8:]
    gm_refs, refs = refs[:narrow], refs[narrow:]
    (dx1_ref, dg_ref, keep_ref, send_ref, turned_ref, left_ref, gm_ref, w_ref, sems) = refs
    core = at_ref[0]
    copies = start_weights(at_ref[3], w_refs, w_ref, sems, pl.ds(1, 3))
    gm_ref[...] = dx2_ref[...].astype(bf16)
    fold_rows(core, o_ref[...].T, turned_ref, left_ref, fold)
    for copy in copies:
        copy.wait()
    weight_grad(left_ref, gm_ref, keep_ref, send_ref, 4)
    fold_rows(core, h_ref[...].T, turned_ref, left_ref, fold)
    weight_grad(left_ref, dqkv_ref.at[0], keep_ref, send_ref, 1)
    fold_rows(core, m_ref[...].T, turned_ref, left_ref, fold)
    for i in (1, 2):
        weight_grad(left_ref, dqkv_ref.at[i], keep_ref, send_ref, i + 1)
    for start, size in tiles_of(o_ref.shape[1]):
        rows = slice(start, start + size)
        gm_ref[:, rows] = (
            dot_nt(dqkv_ref[1], w_ref[1, rows, :]) + dot_nt(dqkv_ref[2], w_ref[2, rows, :])
        ).astype(bf16)
        dx1_ref[:, rows] = dot_nt(dqkv_ref[0], w_ref[0, rows, :])
    split_rows(at_ref[2], gm_ref, gm_refs)
    back, d_gain = norm_back(dx1_ref[...], x1_ref[...], g_ref[1:2, :])
    d_x1 = dx2_ref[...] + back
    dx1_ref[...] = d_x1
    dg_ref[...] = d_gain
    gm_ref[...] = d_x1.astype(bf16)
    fold_rows(core, o1_ref[...].T, turned_ref, left_ref, fold)
    weight_grad(left_ref, gm_ref, keep_ref, send_ref, 0)


def first_back_kernel(at_ref, *refs, pieces, narrow, fold):
    w_refs, refs = refs[:pieces], refs[pieces:]
    (dqkv_ref, h_ref, dx1_ref, x_ref, g_ref), refs = refs[:5], refs[5:]
    gx_refs, refs = refs[:narrow], refs[narrow:]
    dg_ref, keep_ref, send_ref, turned_ref, left_ref, dh_ref, w_ref, sems = refs
    copies = start_weights(at_ref[3], w_refs, w_ref, sems, pl.ds(0, 3))
    fold_rows(at_ref[0], h_ref[...].T, turned_ref, left_ref, fold)
    for copy in copies:
        copy.wait()
    for i in range(3):
        weight_grad(left_ref, dqkv_ref.at[i], keep_ref, send_ref, i)
    for start, size in tiles_of(h_ref.shape[1]):
        rows = slice(start, start + size)
        dh_ref[:, rows] = (
            dot_nt(dqkv_ref[0], w_ref[0, rows, :])
            + dot_nt(dqkv_ref[1], w_ref[1, rows, :])
            + dot_nt(dqkv_ref[2], w_ref[2, rows, :])
        )
    back, d_gain = norm_back(dh_ref[...], x_ref[...].astype(f32), g_ref[0:1, :])
    dh_ref[...] = dx1_ref[...] + back
    split_rows(at_ref[2], dh_ref, gx_refs)
    dg_ref[...] = d_gain


def table_kernel(ds_ref, index_ref, out_ref, acc_ref, *, buckets):
    heads, keys, queries = ds_ref.shape
    acc_ref[...] = jnp.zeros_like(acc_ref)

    def group(at, carry):
        rows = pl.ds(pl.multiple_of(at * 16, 16), 16)
        index = index_ref[rows, :]
        grads = ds_ref[:, rows, :].reshape(heads * 16, queries)
        hot = jnp.concatenate(
            [(index == b).astype(f32).astype(bf16) for b in range(buckets)], axis=0
        )
        acc_ref[...] += dot_nt(grads, hot)
        return carry

    lax.fori_loop(0, keys // 16, group, 0)
    shape = acc_ref.shape
    same = (
        lax.broadcasted_iota(jnp.int32, shape, 0) % 16
        == lax.broadcasted_iota(jnp.int32, shape, 1) % 16
    )
    kept = jnp.where(same, acc_ref[...], 0.0).reshape(heads, 16, shape[1]).sum(axis=1)
    gather = (
        lax.broadcasted_iota(jnp.int32, (shape[1], 128), 0) // 16
        == lax.broadcasted_iota(jnp.int32, (shape[1], 128), 1)
    ).astype(f32)
    out_ref[...] = lax.dot_general(
        kept, gather, (((1,), (0,)), ((), ())),
        preferred_element_type=f32, precision=lax.Precision.HIGHEST,
    )


def cost_of(us):
    return pl.CostEstimate(flops=int(us * 1.15e9), bytes_accessed=MIB, transcendentals=0)


def room_for(arrays, scratch):
    size = sum(v.size * v.dtype.itemsize for v in arrays)
    for ref in scratch:
        shape = getattr(ref, "shape", ())
        if ref.memory_space == pltpu.VMEM:
            rows = -(-shape[-2] // 8) * 8
            size += math.prod(shape[:-2]) * rows * shape[-1] * jnp.dtype(ref.dtype).itemsize
    return (size // MIB + 8) * MIB


def call(kernel, outs, scratch, *args, scalars=1, loose=(), us=2, name=None):
    spaces = [
        pltpu.SMEM if i < scalars else pl.ANY if i in loose else pltpu.VMEM
        for i in range(len(args))
    ]
    return pl.pallas_call(
        kernel,
        out_shape=outs,
        in_specs=[pl.BlockSpec(memory_space=space) for space in spaces],
        out_specs=[pl.BlockSpec(memory_space=pltpu.VMEM)] * len(outs),
        scratch_shapes=scratch,
        compiler_params=pltpu.CompilerParams(
            vmem_limit_bytes=room_for(
                [v for v, space in zip(args, spaces) if space == pltpu.VMEM] + list(outs), scratch
            )
        ),
        cost_estimate=cost_of(us),
        name=name,
    )(*args)


def shape_of(shape, dtype):
    return jax.ShapeDtypeStruct(tuple(shape), dtype)


def permuted(value, wide_bits, narrow_bits):
    wide, narrow = lax.axis_size("wide"), lax.axis_size("narrow")
    pairs = [
        (w * narrow + n, (w ^ wide_bits) * narrow + (n ^ narrow_bits))
        for w in range(wide)
        for n in range(narrow)
    ]
    return lax.ppermute(value, BOTH, pairs)


def after(value, *done):
    return lax.optimization_barrier((value, *done))[0]


def ordered(at, pieces, shares=None):
    first = pieces[0]
    if first.ndim == 2:
        shapes = [(len(pieces),) + first.shape]
    else:
        shapes = [(k, len(pieces)) + first.shape[1:] for k in shares]
    outs = [shape_of(shape, first.dtype) for shape in shapes]
    return call(
        functools.partial(order_kernel, outs=len(outs)), outs, [], at, *pieces, us=1, name="order"
    )


def local_stats(gradient):
    squares = gradient * gradient + 1e-30
    return (jnp.sum(squares, axis=-1), jnp.sum(squares, axis=-2))


class Scatter:
    def __init__(self, at, pairs, fast, narrow):
        self.at, self.fast, self.narrow, self.pairs = at, fast, narrow, pairs
        if not fast:
            return
        keeps = [keep.reshape(-1, keep.shape[1], keep.shape[2]) for keep, _ in pairs]
        sends = [send for _, send in pairs]
        if len(pairs) == 2:
            keeps[1] = keeps[1].reshape(1, -1, keeps[1].shape[2])
            sends[1] = sends[1].reshape(keeps[1].shape)
        self.shapes = [(k.shape[0], k.shape[1] // 4, k.shape[2]) for k in keeps]
        size = sum(k.size for k in keeps) // 4
        cols = TILE if len(pairs) == 2 else keeps[0].shape[2]
        self.rows, self.cols = size // cols, cols
        half = (self.rows // 2, cols)
        recvs = [permuted(send, 1, 0) for send in sends]
        self.own, self.kept_x, self.kept_y, to_x, to_y = call(
            functools.partial(spread_kernel, count=len(pairs)),
            [shape_of((self.rows, cols), f32), shape_of(half, f32), shape_of(half, f32),
             shape_of((2,) + half, bf16), shape_of((2,) + half, bf16)],
            [], at, *keeps, *recvs, us=3, name="spread",
        )
        self.out = (to_x, to_y)
        self.done = self.own

    def middle(self, *done):
        if not self.fast:
            return
        self.own = after(self.own, *done)
        half = (self.rows // 2, self.cols)
        from_x, from_y = permuted(self.out[0], 2, 0), permuted(self.out[1], 4, 0)
        self.own, to_x, to_y = call(
            middle_kernel,
            [shape_of((self.rows, self.cols), f32), shape_of(half, bf16), shape_of(half, bf16)],
            [], self.own, self.kept_x, self.kept_y, from_x, from_y, scalars=0, name="middle",
        )
        self.out = (to_x, to_y)
        self.done = self.own

    def narrowed(self, *done):
        if not self.fast:
            return
        self.own = after(self.own, *done)
        from_x, from_y = permuted(self.out[0], 2, 0), permuted(self.out[1], 4, 0)
        if len(self.shapes) == 2:
            (k, rows, cols), (_, rows_out, cols_out) = self.shapes
            sizes = [rows] * (k * cols // TILE) + [rows_out] * (cols_out // TILE)
        else:
            sizes = [self.shapes[0][1]] * self.shapes[0][0]
        spots, begin = [], 0
        for size in sizes:
            spots.append((begin, size // self.narrow))
            begin += size
        share = (self.rows // self.narrow, self.cols)
        self.out = call(
            functools.partial(narrow_kernel, narrow=self.narrow, spots=spots),
            [shape_of(share, bf16 if d else f32) for d in range(self.narrow)],
            [pltpu.VMEM((self.rows, self.cols), f32)], self.at, self.own, from_x, from_y,
            name="narrow",
        )
        self.done = self.out[0]

    def total(self, *done):
        if not self.fast:
            results = []
            for keep, send in self.pairs:
                whole = jnp.concatenate([keep, send], axis=1)
                if keep.shape[0] == 4:
                    whole = whole.reshape(1, -1, whole.shape[2])
                total = lax.psum_scatter(whole, BOTH, scatter_dimension=1, tiled=True).astype(f32)
                results.append((total, *local_stats(total)))
            return results
        parts = [permuted(v, 0, d) if d else v for d, v in enumerate(self.out)]
        parts[0] = after(parts[0], *done)
        outs = []
        for k, rows, cols in self.shapes:
            rows //= self.narrow
            outs += [
                shape_of((k, rows, cols), f32), shape_of((k, rows, 1), f32),
                shape_of((k, 1, cols), f32),
            ]
        flat = call(
            functools.partial(total_kernel, narrow=self.narrow), outs, [], *parts, scalars=0,
            name="total",
        )
        return [
            (flat[3 * i], flat[3 * i + 1][:, :, 0], flat[3 * i + 2][:, 0])
            for i in range(len(self.shapes))
        ]


def summed_all(parts, fast):
    if not fast:
        return lax.psum(parts, BOTH)
    sizes = [v.size for v in parts]
    flat = jnp.concatenate([v.reshape(-1) for v in parts])
    flat = jnp.pad(flat, (0, -flat.size % 1024)).reshape(-1, 128)
    for bits in (1, 2, 4):
        flat = flat + permuted(flat, bits, 0)
    flat = (flat + permuted(flat, 0, 1)) + (permuted(flat, 0, 2) + permuted(flat, 0, 3))
    flat = flat.reshape(-1)
    results, at = [], 0
    for part, size in zip(parts, sizes):
        results.append(flat[at : at + size].reshape(part.shape))
        at += size
    return results


def adafactor_step(gradient, weight, rows_stat, cols_stat, weight_rms):
    overall = jnp.sum(cols_stat, axis=-1)[..., None, None]
    estimate = rows_stat[..., :, None] * cols_stat[..., None, :] / overall
    return weight - 0.3 * weight_rms * gradient * lax.rsqrt(estimate)


def body(
    targets, memory, cotangent, target_segments, memory_segments, buckets,
    attn_in, attn_out, gains, ff_in, ff_out, bias_table,
):
    wide, narrow = lax.axis_size("wide"), lax.axis_size("narrow")
    at_wide, at_narrow = lax.axis_index("wide"), lax.axis_index("narrow")
    fast = wide == 8 and narrow == 4
    at = jnp.stack([at_wide % 2, at_wide // 2, at_narrow, at_wide]).astype(jnp.int32)
    width, ff_width = attn_in.shape[2], ff_in.shape[2]
    bucket_count, heads = bias_table.shape
    chunk = gains.shape[1]
    local_tokens = targets.shape[1]
    tokens = local_tokens * narrow
    assert targets.shape[0] == narrow

    def over_narrow(pieces):
        return [permuted(v, 0, d) if d else v for d, v in enumerate(pieces)]

    def to_owners(pieces, *done):
        pieces = over_narrow(pieces)
        return ordered(at, [after(pieces[0], *done)] + pieces[1:])[0]

    device = at_wide * narrow + at_narrow
    gain_rows = lax.dynamic_update_slice(
        jnp.zeros((chunk, width), bf16), gains.astype(bf16), (0, device * chunk)
    )
    local_weights = jnp.concatenate(
        [
            attn_in[:3].astype(bf16), gain_rows[None], attn_out[:1].astype(bf16),
            attn_in[3:].astype(bf16), attn_out[1:].astype(bf16),
        ]
    )
    piece16 = shape_of((local_tokens, width), bf16)
    near_rows = local_tokens * (width + tokens) // TILE + 16
    packed = call(
        functools.partial(pack_kernel, narrow=narrow),
        [shape_of((near_rows, TILE), bf16)] * narrow
        + [shape_of((2, local_tokens, width), bf16)] * narrow,
        [], at, targets, memory, cotangent, buckets, target_segments, memory_segments,
        us=4, name="pack",
    )
    near, later = packed[:narrow], packed[narrow:]
    lanes = TILE
    fin_blocks = ff_in.astype(bf16).reshape(2, chunk, ff_width // lanes, lanes)
    fin_blocks = fin_blocks.transpose(0, 2, 1, 3).reshape(-1, chunk, lanes)
    out_rows_here = ff_out.shape[0]
    fout_blocks = ff_out.astype(bf16).reshape(out_rows_here, width // lanes, lanes)
    fout_blocks = fout_blocks.transpose(1, 0, 2).reshape(-1, chunk, lanes)
    fin_count, fout_count = fin_blocks.shape[0], fout_blocks.shape[0]
    ffn_local = jnp.concatenate([fin_blocks, fout_blocks])

    def regroup_out(stack, owners):
        stack = stack.reshape(fout_count, owners, chunk, lanes).transpose(1, 0, 2, 3)
        stack = stack.reshape(owners, width // lanes, out_rows_here, lanes)
        return stack.transpose(1, 0, 2, 3).reshape(width // lanes, -1, lanes)

    def over_plane(stack):
        return [stack] + [permuted(stack, 2 * d, 0) for d in range(1, 4)]

    def with_other_core(plane, *done):
        return [
            piece for part in plane for piece in (part, permuted(after(part, *done), 1, 0))
        ]

    if fast:
        stacks = ordered(at, over_narrow([local_weights] * narrow), (4, 5))
        stacks = [v.reshape(v.shape[0], -1, width) for v in stacks]
        near = [near[0]] + [after(v, stacks[0]) for v in near[1:]]
        plane_first = over_plane(stacks[0])
        w_first = with_other_core(plane_first)
        plane_second = over_plane(after(stacks[1], *plane_first[1:]))
    else:
        every = lax.all_gather(local_weights, BOTH, axis=1, tiled=True)
        w_first, w_second = [every[:4]], [every[4:]]
    near = over_narrow(near)
    index, cross_mask = call(
        functools.partial(
            prepare_kernel, narrow=narrow, bucket_count=bucket_count,
            skip=local_tokens * width // TILE,
        ),
        [shape_of((tokens, tokens), jnp.int32), shape_of((tokens, tokens), f32)],
        [pltpu.VMEM((16, tokens), f32), pltpu.VMEM((tokens, tokens), f32)],
        at, *near, us=3, name="prepare",
    )
    if fast:
        ffn_local = after(ffn_local, index)
        ffn_near = over_narrow([ffn_local] * narrow)
    table = jnp.concatenate(
        [bias_table.T, jnp.full((heads, 128 - bucket_count), NEG, f32)], axis=1
    )
    row16 = shape_of((tokens, width), bf16)
    row32 = shape_of((tokens, width), f32)
    three = shape_of((3, tokens, width), bf16)
    stat = shape_of((heads, 1, tokens), f32)
    gain_out = shape_of((1, width), f32)
    pair_t = pltpu.VMEM((128, tokens), f32)
    pieces = len(w_first)
    weights = lambda count: pltpu.VMEM((count, width, width), bf16)
    sems = pltpu.SemaphoreType.DMA((pieces,))
    g, x, h1, qkv1, o1, peak1, inv1 = call(
        functools.partial(first_kernel, pieces=pieces, narrow=narrow, chunk=chunk),
        [shape_of((8, width), f32), row16, row16, three, row16, stat, stat],
        [pair_t, weights(4), sems],
        at, *near, *w_first, index, table,
        loose=range(1 + narrow, 1 + narrow + pieces), us=16, name="first",
    )
    if fast:
        w_second = with_other_core(plane_second, h1)
        ffn_near[0] = after(ffn_near[0], h1)
        (stack,) = ordered(at, ffn_near, (fin_count + fout_count,))
        stack = stack.reshape(fin_count + fout_count, -1, lanes)
        stack_out = regroup_out(stack[fin_count:], narrow).reshape(fout_count, -1, lanes)
        stack = jnp.concatenate([stack[:fin_count], stack_out])
        later = [later[0]] + [after(v, stack) for v in later[1:]]
        plane_ffn = over_plane(after(stack, *plane_second[1:]))
        o1 = after(o1, plane_ffn[1], plane_ffn[2])
    later = over_narrow(later)
    m, c, x1, h2, qkv2, o2, x2, h3, peak2, inv2 = call(
        functools.partial(second_kernel, pieces=pieces, narrow=narrow),
        [row16, row16, row32, row16, three, row16, row32, row16, stat, stat],
        [pair_t, weights(5), sems],
        at, *later, *w_second, x, o1, cross_mask, g,
        loose=range(1 + narrow, 1 + narrow + pieces), us=21, name="second",
    )

    if fast:
        ffn_pieces = with_other_core(plane_ffn, x2)
        w_fin = ffn_pieces
        w_fout = [v.reshape(-1, narrow * out_rows_here, lanes) for v in ffn_pieces]
    else:
        every = lax.all_gather(ffn_local, BOTH, axis=1, tiled=True)
        w_fin, w_fout = [every], [regroup_out(every[fin_count:], wide * narrow)]
    steps = 4
    part = ff_width // steps
    half = width // 2
    whole = lambda shape: pl.BlockSpec(shape, lambda i: (0,) * len(shape))
    outs = pl.pallas_call(
        functools.partial(
            ffn_kernel, fold=fast, narrow=narrow, pieces=pieces,
            first_out=w_fout[0].shape[0] - width // lanes,
        ),
        grid=(steps,),
        in_specs=[pl.BlockSpec(memory_space=pltpu.SMEM)]
        + [whole((tokens, width))]
        + [pl.BlockSpec(memory_space=pl.ANY)] * (2 * pieces)
        + [whole((tokens, width)), whole((tokens, width)), whole((8, width))],
        out_specs=[whole((local_tokens, width))] * narrow
        + [
            whole((tokens, width)), whole((1, width)),
            pl.BlockSpec((2, half, part), lambda i: (0, 0, i)),
            pl.BlockSpec((2, half, part), lambda i: (0, 0, i)),
            pl.BlockSpec((None, part // 2, width), lambda i: (i, 0, 0)),
            pl.BlockSpec((None, part // 2, width), lambda i: (i, 0, 0)),
        ],
        out_shape=[piece16] * narrow
        + [
            row32, gain_out,
            shape_of((2, half, ff_width), bf16), shape_of((2, half, ff_width), bf16),
            shape_of((steps, part // 2, width), bf16), shape_of((steps, part // 2, width), bf16),
        ],
        scratch_shapes=[
            pltpu.VMEM((tokens, width), f32), pltpu.VMEM((tokens, width), f32),
            pltpu.VMEM((width, tokens), bf16), pltpu.VMEM((width, tokens), bf16),
            pltpu.VMEM((part, width), bf16),
            pltpu.VMEM((fin_count, width, lanes), bf16),
            pltpu.VMEM((width // lanes, ff_width, lanes), bf16), sems, sems,
        ],
        compiler_params=pltpu.CompilerParams(vmem_limit_bytes=40 * MIB),
        cost_estimate=cost_of(24),
        name="ffn",
    )(at, c, *w_fin, *w_fout, x2, h3, g)
    out_pieces = outs[:narrow]
    dx2, gain3, keep_fin, send_fin, keep_fout, send_fout = outs[narrow:]
    ffn_sum = Scatter(at, [(keep_fin, send_fin), (keep_fout, send_fout)], fast, narrow)
    if fast:
        dx2 = after(dx2, ffn_sum.done)
    square = pltpu.VMEM((tokens, tokens), bf16)
    attend_scratch = [
        pltpu.VMEM((tokens, width), bf16), pltpu.VMEM((heads, 1, tokens), f32), square, square,
        pair_t, weights(1), sems,
    ]
    turned = pltpu.VMEM((width, tokens), bf16)
    grads = lambda count: shape_of((count, half, width), bf16)
    (dqkv2,) = call(
        functools.partial(attend_back_kernel, pieces=pieces, which=4, causal=False),
        [three], attend_scratch,
        at, *w_second, dx2, o2, qkv2, cross_mask, peak2, inv2,
        loose=range(1, 1 + pieces), us=18, name="cross_back",
    )
    output = to_owners(out_pieces, dqkv2)
    ffn_sum.middle(dqkv2)
    if fast:
        dqkv2 = after(dqkv2, ffn_sum.done, output)
    outs = call(
        functools.partial(second_back_kernel, pieces=pieces, narrow=narrow, fold=fast),
        [piece16] * narrow + [row32, gain_out, grads(5), grads(5)],
        [turned, turned, pltpu.VMEM((tokens, width), bf16), weights(3), sems],
        at, *w_second, dqkv2, dx2, o2, h2, m, x1, o1, g,
        loose=range(1, 1 + pieces), us=12, name="second_back",
    )
    gm_pieces = outs[:narrow]
    dx1, gain2, keep_second, send_second = outs[narrow:]
    ffn_sum.narrowed(gain2)
    if fast:
        send_second = after(send_second, ffn_sum.done)
    second_sum = Scatter(at, [(keep_second, send_second)], fast, narrow)
    if fast:
        dx1 = after(dx1, second_sum.done, ffn_sum.done)
    dqkv1, ds = call(
        functools.partial(attend_back_kernel, pieces=pieces, which=0, causal=True),
        [three, shape_of((heads, tokens, tokens), bf16)], attend_scratch,
        at, *w_second, table, dx1, o1, qkv1, index, peak1, inv1,
        loose=range(1, 1 + pieces), us=20, name="self_back",
    )
    (sum_fin, fin_rows, fin_part), (sum_fout, fout_rows, fout_part) = ffn_sum.total(dqkv1)
    second_sum.middle(dqkv1)
    if fast:
        dqkv1 = after(dqkv1, sum_fin, second_sum.done)
    outs = call(
        functools.partial(first_back_kernel, pieces=pieces, narrow=narrow, fold=fast),
        [piece16] * narrow + [gain_out, grads(3), grads(3)],
        [turned, turned, pltpu.VMEM((tokens, width), f32), weights(3), sems],
        at, *w_first, dqkv1, h1, dx1, x, g,
        loose=range(1, 1 + pieces), us=9, name="first_back",
    )
    gx_pieces = outs[:narrow]
    gain1, keep_first, send_first = outs[narrow:]
    grad_memory = to_owners(gm_pieces, gain1)
    second_sum.narrowed(gain1, grad_memory)
    if fast:
        send_first = after(send_first, second_sum.done)
    first_sum = Scatter(at, [(keep_first, send_first)], fast, narrow)
    if fast:
        ds = after(ds, first_sum.done, second_sum.done, grad_memory)
    (table_part,) = call(
        functools.partial(table_kernel, buckets=bucket_count),
        [shape_of((heads, 128), f32)],
        [pltpu.VMEM((heads * 16, bucket_count * 16), f32)], ds, index, scalars=0, us=11,
        name="table",
    )
    first_sum.middle(table_part)
    ((sum_second, second_rows, second_part),) = second_sum.total(table_part)
    if fast:
        gx_pieces = [after(v, sum_second) for v in gx_pieces]
    grad_targets = to_owners(gx_pieces)
    first_sum.narrowed()
    ((sum_first, first_rows, first_part),) = first_sum.total()
    table_part = table_part[:, :bucket_count].T


    def regroup(first, second):
        return jnp.concatenate([first, second[1:4]]), jnp.stack([second[0], second[4]])

    sum_in, sum_out = regroup(sum_first, sum_second)
    in_rows, out_rows = regroup(first_rows, second_rows)
    in_part, out_part = regroup(first_part, second_part)
    sum_fout, fout_rows, fout_part = sum_fout[0], fout_rows[0], fout_part[0]
    gain_part = jnp.concatenate([gain1, gain2, gain3])
    in_square = jnp.sum(attn_in * attn_in, axis=(1, 2))
    out_square = jnp.sum(attn_out * attn_out, axis=(1, 2))
    fin_square = jnp.sum(ff_in * ff_in, axis=(1, 2))
    fout_square = jnp.sum(ff_out * ff_out).reshape(1)
    (
        sum_gain, in_cols, out_cols, fin_cols, fout_cols, grad_table,
        in_total, out_total, fin_total, fout_total,
    ) = summed_all(
        (
            gain_part, in_part, out_part, fin_part, fout_part, table_part,
            in_square, out_square, fin_square, fout_square,
        ),
        fast,
    )
    sum_gain = lax.dynamic_slice_in_dim(sum_gain, device * chunk, chunk, 1)
    table_rows, table_cols = local_stats(grad_table)
    in_rms = jnp.sqrt(in_total / (width * width) + 1e-06)[:, None, None]
    out_rms = jnp.sqrt(out_total / (width * width) + 1e-06)[:, None, None]
    fin_rms = jnp.sqrt(fin_total / (width * ff_width) + 1e-06)[:, None, None]
    fout_rms = jnp.sqrt(fout_total[0] / (width * ff_width) + 1e-06)
    table_rms = jnp.sqrt(jnp.mean(bias_table * bias_table) + 1e-06)
    return (
        output, grad_targets, grad_memory,
        sum_in, sum_out, sum_gain, sum_fin, sum_fout, grad_table,
        in_rows, in_cols, out_rows, out_cols, fin_rows, fin_cols, fout_rows, fout_cols,
        adafactor_step(sum_in, attn_in, in_rows, in_cols, in_rms),
        adafactor_step(sum_out, attn_out, out_rows, out_cols, out_rms),
        adafactor_step(sum_fin, ff_in, fin_rows, fin_cols, fin_rms),
        adafactor_step(sum_fout, ff_out, fout_rows, fout_cols, fout_rms),
        adafactor_step(grad_table, bias_table, table_rows, table_cols, table_rms),
    )


def solution(mesh):
    in_specs = (
        P("wide", "narrow", None),
        P("wide", "narrow", None),
        P("wide", "narrow", None),
        P("wide", "narrow"),
        P("wide", "narrow"),
        P("narrow", None),
        P(None, ("wide", "narrow"), None),
        P(None, ("wide", "narrow"), None),
        P(None, ("wide", "narrow")),
        P(None, ("wide", "narrow"), None),
        P(("wide", "narrow"), None),
        P(),
    )
    out_specs = (
        P("wide", "narrow", None),
        P("wide", "narrow", None),
        P("wide", "narrow", None),
        P(None, ("wide", "narrow"), None),
        P(None, ("wide", "narrow"), None),
        P(None, ("wide", "narrow")),
        P(None, ("wide", "narrow"), None),
        P(("wide", "narrow"), None),
        P(),
        P(None, ("wide", "narrow")),
        P(),
        P(None, ("wide", "narrow")),
        P(),
        P(None, ("wide", "narrow")),
        P(),
        P(("wide", "narrow")),
        P(),
        P(None, ("wide", "narrow"), None),
        P(None, ("wide", "narrow"), None),
        P(None, ("wide", "narrow"), None),
        P(("wide", "narrow"), None),
        P(),
    )
    return jax.shard_map(body, mesh=mesh, in_specs=in_specs, out_specs=out_specs, check_vma=False)
```

```python
import functools
import math

import jax
import jax.numpy as jnp
from jax import lax
from jax.experimental import pallas as pl
from jax.experimental.pallas import tpu as pltpu
from jax.sharding import PartitionSpec as P

bf16, f32 = jnp.bfloat16, jnp.float32
BOTH = ("wide", "narrow")
NEG = -1e9
TILE = 256
MIB = 1 << 20


def dot_nn(left, right):
    return lax.dot_general(left, right, (((1,), (0,)), ((), ())), preferred_element_type=f32)


def dot_nt(left, right):
    return lax.dot_general(left, right, (((1,), (1,)), ((), ())), preferred_element_type=f32)


def unit_of(values):
    inv_rms = lax.rsqrt(jnp.mean(values * values, axis=-1, keepdims=True) + 1e-06)
    return values * inv_rms, inv_rms


def norm_back(incoming, values, gain_row):
    unit, inv_rms = unit_of(values)
    scaled = incoming * gain_row
    inner = jnp.mean(scaled * unit, axis=-1, keepdims=True)
    return inv_rms * (scaled - unit * inner), jnp.sum(incoming * unit, axis=0, keepdims=True)


def tiles_of(width):
    return [(start, min(TILE, width - start)) for start in range(0, width, TILE)]


def project(left, w_ref, index, store):
    for start, size in tiles_of(w_ref.shape[2]):
        store(start, size, dot_nn(left, w_ref[index, :, start : start + size]))


def half_lanes(second):
    lane = lax.broadcasted_iota(jnp.int32, (1, 128), 1)
    return ((lane >= 64) == bool(second)).astype(bf16)


def biased(table_row, index):
    spread = jnp.broadcast_to(table_row, (index.shape[0], 128))
    return jnp.concatenate(
        [
            jnp.take_along_axis(
                spread, index[:, at : at + 128], axis=1, mode="promise_in_bounds"
            )
            for at in range(0, index.shape[1], 128)
        ],
        axis=1,
    )


def query_blocks(keys, queries, causal):
    return [
        (at, min(keys, at + TILE) if causal else keys) for at in range(0, queries, TILE)
    ]


def attend(qkv_ref, extra_ref, table_ref, o_ref, peak_ref, inv_ref, ot_ref):
    causal = table_ref is not None
    keys = qkv_ref.shape[1]

    def pair(at_pair, carry):
        lanes = pl.ds(pl.multiple_of(at_pair * 128, 128), 128)
        query, key, value = (qkv_ref[i, :, lanes] for i in range(3))
        value_t = value.T
        for second in range(2):
            head = at_pair * 2 + second
            key_half = key * half_lanes(second)
            for start, last in query_blocks(keys, keys, causal):
                part = slice(start, start + TILE)
                scores = dot_nt(key_half[:last], query[part])
                if causal:
                    scores += biased(table_ref[pl.ds(head, 1), :], extra_ref[:last, part])
                else:
                    scores += extra_ref[:last, part]
                peak = jnp.max(scores, axis=0, keepdims=True)
                grown = jnp.exp(scores - peak)
                inverse = 1.0 / jnp.sum(grown, axis=0, keepdims=True)
                mixed = dot_nn(value_t[second * 64 : second * 64 + 64, :last], grown.astype(bf16))
                ot_ref[second * 64 : second * 64 + 64, part] = mixed * inverse
                peak_ref[head, :, part] = peak
                inv_ref[head, :, part] = inverse
        o_ref[:, lanes] = ot_ref[...].T.astype(bf16)
        return carry

    lax.fori_loop(0, qkv_ref.shape[2] // 128, pair, 0)


def attend_back(
    qkv_ref, extra_ref, table_ref, do_ref, dsum_ref, peak_ref, inv_ref,
    dqkv_ref, p_ref, ds_ref, dqt_ref, ds_out,
):
    causal = table_ref is not None
    keys = qkv_ref.shape[1]
    first_half = lax.broadcasted_iota(jnp.int32, (1, 128), 1) < 64

    def pair(at_pair, carry):
        lanes = pl.ds(pl.multiple_of(at_pair * 128, 128), 128)
        query, key, value = (qkv_ref[i, :, lanes] for i in range(3))
        grad = do_ref[:, lanes]
        key_t = key.T
        for second in range(2):
            head = at_pair * 2 + second
            half = half_lanes(second)
            key_half, value_half = key * half, value * half
            for start, last in query_blocks(keys, keys, causal):
                part = slice(start, start + TILE)
                scores = dot_nt(key_half[:last], query[part])
                if causal:
                    scores += biased(table_ref[pl.ds(head, 1), :], extra_ref[:last, part])
                else:
                    scores += extra_ref[:last, part]
                weights = jnp.exp(scores - peak_ref[head, :, part]) * inv_ref[head, :, part]
                grad_weights = dot_nt(value_half[:last], grad[part])
                grad_scores = (weights * (grad_weights - dsum_ref[head, :, part])).astype(bf16)
                p_ref[:last, part] = weights.astype(bf16)
                ds_ref[:last, part] = grad_scores
                dqt_ref[second * 64 : second * 64 + 64, part] = dot_nn(
                    key_t[second * 64 : second * 64 + 64, :last], grad_scores
                )
            for start in range(0, keys, TILE):
                rows = slice(start, start + TILE)
                begin = start if causal else 0
                d_value = dot_nn(p_ref[rows, begin:], grad[begin:]).astype(bf16)
                d_key = dot_nn(ds_ref[rows, begin:], query[begin:]).astype(bf16)
                if second:
                    d_value = jnp.where(first_half, dqkv_ref[2, rows, lanes], d_value)
                    d_key = jnp.where(first_half, dqkv_ref[1, rows, lanes], d_key)
                dqkv_ref[2, rows, lanes] = d_value
                dqkv_ref[1, rows, lanes] = d_key
            if ds_out is not None:
                ds_out[head] = ds_ref[...]
        dqkv_ref[0, :, lanes] = dqt_ref[...].T.astype(bf16)
        return carry

    if causal:
        p_ref[...] = jnp.zeros_like(p_ref)
        ds_ref[...] = jnp.zeros_like(ds_ref)
    lax.fori_loop(0, qkv_ref.shape[2] // 128, pair, 0)


def head_sums(grad, mixed, dsum_ref):
    heads = dsum_ref.shape[0]
    product = grad.astype(f32) * mixed.astype(f32)
    width = product.shape[1]
    pick = (
        lax.broadcasted_iota(jnp.int32, (16, width), 1) // (width // heads)
        == lax.broadcasted_iota(jnp.int32, (16, width), 0)
    ).astype(f32)
    sums = lax.dot_general(
        pick, product, (((1,), (1,)), ((), ())),
        preferred_element_type=f32, precision=lax.Precision.HIGHEST,
    )
    for head in range(heads):
        dsum_ref[head] = sums[head : head + 1]


def square_kernel(*refs):
    row = 0
    for ref in refs[:-1]:
        parts = [ref[i] for i in range(ref.shape[0])] if len(ref.shape) == 3 else [ref[...]]
        for part in parts:
            total = jnp.sum(jnp.sum(part * part, axis=1, keepdims=True), axis=0, keepdims=True)
            refs[-1][row : row + 1, :] = jnp.broadcast_to(total, (1, 128))
            row += 1
    refs[-1][row:, :] = jnp.zeros((refs[-1].shape[0] - row, 128), f32)


def tally_kernel(gain1, gain2, gain3, first, second, fin, fout, table, squares, out_ref):
    at = 0
    rows = [ref[...] for ref in (gain1, gain2, gain3)]
    rows += [ref[i] for ref in (first, second, fin, fout) for i in range(ref.shape[0])]
    for row in rows:
        for start in range(0, row.shape[1], 128):
            out_ref[at : at + 1, :] = row[:, start : start + 128]
            at += 1
    for ref in (table, squares):
        out_ref[at : at + ref.shape[0], :] = ref[...]
        at += ref.shape[0]
    out_ref[at:, :] = jnp.zeros((out_ref.shape[0] - at, 128), f32)


def update_kernel(tally, first, second, fin, fout, first_rows, second_rows, fin_rows, fout_rows,
                  attn_in, attn_out, ff_in, ff_out, table, g_in, g_out, new_in, new_out, new_fin,
                  new_fout, gains, in_cols, out_cols, fin_cols, fout_cols, g_table, new_table,
                  *, buckets):
    at = 0

    def row(width):
        nonlocal at
        parts = [tally[at + i : at + i + 1, :] for i in range(width // 128)]
        at += width // 128
        return jnp.concatenate(parts, axis=1)

    width, ff_width = attn_in.shape[2], ff_in.shape[2]
    for i in range(3):
        gains[i : i + 1, :] = row(width)
    cols = [row(width) for _ in range(8)]
    cols += [row(ff_width), row(ff_width), row(width)]
    heads = table.shape[0]
    grad_t = tally[at : at + heads, :][:, :buckets]
    squares = at + heads
    sizes = [width * width] * 8 + [width * ff_width] * 3

    def step(grad, weight, rows, col, square, size):
        overall = jnp.sum(col, axis=1, keepdims=True)
        rms = jnp.sqrt(tally[squares + square : squares + square + 1, 0:1] / size + 1e-06)
        return weight - 0.3 * rms * grad * lax.rsqrt(rows * col / overall)

    places = [(first, first_rows, i, col) for i, col in enumerate(cols[:3])]
    places += [(second, second_rows, i, cols[3 + i]) for i in (1, 2, 3)]
    for i, (grad, rows, j, col) in enumerate(places):
        g_in[i] = grad[j]
        in_cols[i : i + 1, :] = col
        new_in[i] = step(grad[j], attn_in[i], rows[j], col, i, sizes[0])
    for i, j in ((0, 0), (1, 4)):
        col = cols[3 + j]
        g_out[i] = second[j]
        out_cols[i : i + 1, :] = col
        new_out[i] = step(second[j], attn_out[i], second_rows[j], col, 6 + i, sizes[0])
    for i in range(2):
        fin_cols[i : i + 1, :] = cols[8 + i]
        new_fin[i] = step(fin[i], ff_in[i], fin_rows[i], cols[8 + i], 8 + i, sizes[8])
    fout_cols[...] = cols[10]
    new_fout[...] = step(fout[0], ff_out[...], fout_rows[0], cols[10], 10, sizes[8])
    weight = table[:, :buckets]
    square = grad_t * grad_t + 1e-30
    by_bucket = jnp.sum(square, axis=0, keepdims=True)
    by_head = jnp.sum(square, axis=1, keepdims=True)
    overall = jnp.sum(by_head, axis=0, keepdims=True)
    mean = jnp.sum(jnp.sum(weight * weight, axis=1, keepdims=True), axis=0, keepdims=True)
    rms = jnp.sqrt(mean / (heads * buckets) + 1e-06)
    new_t = weight - 0.3 * rms * grad_t * lax.rsqrt(by_bucket * by_head / overall)
    g_table[...] = grad_t.T
    new_table[...] = new_t.T


def fold_rows(core, turned, turned_ref, out_ref, fold):
    if not fold:
        out_ref[...] = turned
        return
    turned_ref[...] = turned
    total = turned.shape[0]
    size = total // 8
    for group in range(4):
        for place, which in ((0, core), (1, 1 - core)):
            begin = pl.multiple_of(group * 2 * size + which * size, 16)
            to = place * (total // 2) + group * size
            out_ref[to : to + size, :] = turned_ref[pl.ds(begin, size), :]


def weight_grad(left_ref, right_ref, keep_ref, send_ref, index):
    half = left_ref.shape[0] // 2
    for start, size in tiles_of(right_ref.shape[1]):
        part = slice(start, start + size)
        right = right_ref[:, part]
        keep_ref[index, :, part] = dot_nn(left_ref[:half], right).astype(bf16)
        send_ref[index, :, part] = dot_nn(left_ref[half:], right).astype(bf16)


def start_weights(place, pieces, target_ref, sems, only=None):
    if len(pieces) == 5:
        size = pieces[0].shape[0]
        pieces = [
            piece
            for d in range(4)
            for piece in (pieces[d], pieces[4].at[pl.ds(d * size, size)])
        ]
    rows = target_ref.shape[1] // len(pieces)
    copies = []
    for d, piece in enumerate(pieces):
        begin = pl.multiple_of((place ^ d) * rows, rows) if len(pieces) > 1 else 0
        source = piece if only is None else piece.at[only]
        copies.append(
            pltpu.make_async_copy(source, target_ref.at[:, pl.ds(begin, rows), :], sems.at[d])
        )
        copies[-1].start()
    return copies


def join_rows(place, pieces, target_ref):
    rows = pieces[0].shape[0]
    for d, piece in enumerate(pieces):
        target_ref[pl.ds(pl.multiple_of((place ^ d) * rows, 16), rows), :] = piece[...]


def join_blocks(place, pieces, target_ref):
    blocks = target_ref.shape[1] // TILE
    rows = target_ref.shape[0] // len(pieces)
    for d, piece in enumerate(pieces):
        to = pl.ds(pl.multiple_of((place ^ d) * rows, 16), rows)
        for j in range(blocks):
            target_ref[to, j * TILE : (j + 1) * TILE] = piece[j * rows : (j + 1) * rows, :]


def pack_kernel(at_ref, x_ref, m_ref, c_ref, seg_t_ref, seg_m_ref, *outs, narrow):
    local, width = x_ref.shape[1:]
    for d in range(narrow):
        first, memory, cot = outs[d], outs[narrow + d], outs[2 * narrow + d]
        row = at_ref[2] ^ d
        memory[...] = m_ref[row]
        cot[...] = c_ref[row]
        begin = 0
        for j in range(width // TILE):
            first[begin : begin + local, :] = x_ref[row, :, j * TILE : (j + 1) * TILE]
            begin += local
        for i, ref in enumerate((seg_t_ref, seg_m_ref)):
            seg = jnp.broadcast_to(ref[pl.ds(row, 1), :].astype(f32), (16, local))
            first[begin : begin + 16, i * local : (i + 1) * local] = seg.astype(bf16)


def split_rows(place, source_ref, pieces):
    rows = pieces[0].shape[0]
    for d, piece in enumerate(pieces):
        piece[...] = source_ref[pl.ds(pl.multiple_of((place ^ d) * rows, 16), rows), :].astype(
            piece.dtype
        )


def first_kernel(at_ref, *refs, pieces, narrow, chunk, bucket_count):
    x_refs, refs = refs[:narrow], refs[narrow:]
    w_refs, refs = refs[:pieces], refs[pieces:]
    near_ref = None
    if pieces == 1:
        near_ref, refs = refs[0], refs[1:]
    (allowed_ref, table_ref, w_ref, extra_ref, g_ref, x_ref, h_ref, qkv_ref, o_ref, peak_ref,
     inv_ref, ot_ref, sems) = refs
    copies = start_weights(at_ref[3], w_refs, w_ref, sems)
    join_blocks(at_ref[2], x_refs, x_ref)
    width = x_ref.shape[1]
    pick = (
        lax.broadcasted_iota(jnp.int32, (8, width), 1) % chunk
        == lax.broadcasted_iota(jnp.int32, (8, width), 0)
    ).astype(bf16)
    unit, _ = unit_of(x_ref[...].astype(f32))
    for copy in copies:
        copy.wait()
    gains = dot_nn(pick, w_ref[3])
    g_ref[...] = gains
    if near_ref is None:
        tokens = extra_ref.shape[0]
        held = w_ref[3, :, :tokens].astype(f32)
        groups = width // (narrow * chunk)
        share = tokens // (narrow * groups)
        near = jnp.concatenate(
            [
                held[(w * narrow + n + 1) * chunk - share : (w * narrow + n + 1) * chunk]
                for n in range(narrow)
                for w in range(groups)
            ],
            axis=0,
        ).T
    else:
        near = near_ref[...].astype(f32)
    extra_ref[...] = jnp.where(
        allowed_ref[...] > 0.0, near, float(bucket_count)
    ).astype(jnp.int32)
    h_ref[...] = (unit * gains[0:1]).astype(bf16)
    for i in range(3):
        def store(start, size, product, i=i):
            qkv_ref[i, :, start : start + size] = product.astype(bf16)

        project(h_ref[...], w_ref, i, store)
    attend(qkv_ref, extra_ref, table_ref, o_ref, peak_ref, inv_ref, ot_ref)


def second_kernel(at_ref, *refs, pieces, narrow):
    m_refs, refs = refs[:narrow], refs[narrow:]
    w_refs, refs = refs[:pieces], refs[pieces:]
    (x_ref, o1_ref, extra_ref, g_ref, w_ref, m_ref, x1_ref, h_ref, qkv_ref, o_ref, x2_ref, h3_ref,
     peak_ref, inv_ref, ot_ref, sems) = refs
    copies = start_weights(at_ref[3], w_refs, w_ref, sems)
    join_rows(at_ref[2], m_refs, m_ref)
    for copy in copies:
        copy.wait()

    def store_x1(start, size, product):
        part = slice(start, start + size)
        x1_ref[:, part] = x_ref[:, part].astype(f32) + product

    project(o1_ref[...], w_ref, 0, store_x1)
    unit, _ = unit_of(x1_ref[...])
    h_ref[...] = (unit * g_ref[1:2, :]).astype(bf16)
    for i in range(3):
        def store(start, size, product, i=i):
            qkv_ref[i, :, start : start + size] = product.astype(bf16)

        project(m_ref[...] if i else h_ref[...], w_ref, i + 1, store)
    attend(qkv_ref, extra_ref, None, o_ref, peak_ref, inv_ref, ot_ref)

    def store_x2(start, size, product):
        part = slice(start, start + size)
        x2_ref[:, part] = x1_ref[:, part] + product

    project(o_ref[...], w_ref, 4, store_x2)
    unit, _ = unit_of(x2_ref[...])
    h3_ref[...] = (unit * g_ref[2:3, :]).astype(bf16)


def prepare_kernel(at_ref, *refs, narrow, skip):
    in_refs, (allowed_ref, mask_ref, seg_ref) = refs[:narrow], refs[narrow:]
    tokens = mask_ref.shape[0]
    local = tokens // narrow
    for d, ref in enumerate(in_refs):
        lanes = pl.ds(pl.multiple_of((at_ref[2] ^ d) * local, 128), local)
        tail = ref[skip : skip + 16, :].astype(f32)
        seg_ref[0:8, lanes] = tail[:8, :local]
        seg_ref[8:16, lanes] = tail[:8, local : 2 * local]
    seg = seg_ref[...]
    seg_t = seg.T
    key = lax.broadcasted_iota(jnp.int32, (tokens, tokens), 0)
    query = lax.broadcasted_iota(jnp.int32, (tokens, tokens), 1)
    allowed = (key <= query) & (seg_t[:, 0:1] == seg[0:1, :])
    allowed_ref[...] = jnp.where(allowed, 1.0, 0.0)
    mask_ref[...] = jnp.where(seg_t[:, 8:9] == seg[0:1, :], 0.0, NEG)


def order_kernel(at_ref, *refs, outs):
    pieces, out_refs = refs[:-outs], refs[-outs:]
    for d, piece in enumerate(pieces):
        if piece.ndim == 2:
            out_refs[0][at_ref[2] ^ d] = piece[...]
            continue
        begin = 0
        for out_ref in out_refs:
            size = out_ref.shape[0]
            out_ref[:, at_ref[2] ^ d] = piece[begin : begin + size]
            begin += size


def read_part(refs, group):
    if len(refs) == 1:
        count, rows, cols = refs[0].shape
        rows //= 4
        part = pl.ds(pl.multiple_of(group * rows, 16), rows)
        return refs[0][:, part, :].astype(f32).reshape(count * rows, cols)
    fin, fout = refs
    rows, rows_out = fin.shape[1] // 4, fout.shape[1] // 4
    part = pl.ds(pl.multiple_of(group * rows, 16), rows)
    part_out = pl.ds(pl.multiple_of(group * rows_out, 16), rows_out)
    pieces = [
        fin[i, part, at : at + TILE].astype(f32)
        for i in range(fin.shape[0])
        for at in range(0, fin.shape[2], TILE)
    ]
    pieces += [
        fout[0, part_out, at : at + TILE].astype(f32) for at in range(0, fout.shape[2], TILE)
    ]
    return jnp.concatenate(pieces, axis=0)


def spread_kernel(at_ref, *refs, count):
    keeps, recvs = refs[:count], refs[count : 2 * count]
    own_ref, kept_x, kept_y, to_x, to_y = refs[2 * count :]
    half = own_ref.shape[0] // 2
    for d in range(4):
        total = read_part(keeps, at_ref[1] ^ d) + read_part(recvs, at_ref[1] ^ d)
        if d == 0:
            own_ref[...] = total
        elif d == 1:
            to_x[0] = total[:half].astype(bf16)
            kept_x[...] = total[half:]
        elif d == 2:
            to_y[0] = total[half:].astype(bf16)
            kept_y[...] = total[:half]
        else:
            to_x[1] = total[:half].astype(bf16)
            to_y[1] = total[half:].astype(bf16)


def middle_kernel(own_ref, kept_x, kept_y, from_x, from_y, sum_ref, to_x, to_y):
    half = own_ref.shape[0] // 2
    sum_ref[:half, :] = own_ref[:half, :] + from_x[0].astype(f32)
    sum_ref[half:, :] = own_ref[half:, :] + from_y[0].astype(f32)
    to_y[...] = (kept_y[...] + from_x[1].astype(f32)).astype(bf16)
    to_x[...] = (kept_x[...] + from_y[1].astype(f32)).astype(bf16)


def narrow_kernel(at_ref, own_ref, from_x, from_y, *refs, narrow, spots):
    riders, outs, sum_ref = refs[: -narrow - 1], refs[-narrow - 1 : -1], refs[-1]
    half = own_ref.shape[0] // 2
    sum_ref[:half, :] = own_ref[:half, :] + from_y[...].astype(f32)
    sum_ref[half:, :] = own_ref[half:, :] + from_x[...].astype(f32)
    for d, out_ref in enumerate(outs):
        place = at_ref[2] ^ d
        share = jnp.concatenate(
            [
                sum_ref[pl.ds(start + pl.multiple_of(place * rows, 8), rows), :]
                for start, rows in spots
            ],
            axis=0,
        ).astype(out_ref.dtype)
        ahead = out_ref.shape[0] - share.shape[0]
        if ahead:
            rider, cols = riders[d - 1], out_ref.shape[1]
            rows = rider.shape[0]
            for j in range(rider.shape[1] // cols):
                out_ref[j * rows : (j + 1) * rows, :] = rider[:, j * cols : (j + 1) * cols]
        out_ref[ahead:, :] = share


def join_kernel(at_ref, *refs):
    own, pieces, out_ref = refs[0], refs[1:-1], refs[-1]
    out_ref[at_ref[2]] = own[...]
    rows, width = own.shape
    for d, piece in enumerate(pieces):
        cols = piece.shape[1]
        for j in range(width // cols):
            out_ref[at_ref[2] ^ (d + 1), :, j * cols : (j + 1) * cols] = piece[
                j * rows : (j + 1) * rows, :
            ]


def total_kernel(*refs, narrow):
    total = refs[0][...]
    for ref in refs[1:narrow]:
        total = total + ref[ref.shape[0] - total.shape[0] :, :].astype(f32)
    outs = refs[narrow:]
    at = 0
    for total_ref, rows_ref, cols_ref in zip(*(outs[i::3] for i in range(3))):
        count, rows, cols = total_ref.shape
        block = total.shape[1]
        if cols == block:
            total_ref[...] = total[at : at + count * rows].reshape(count, rows, cols)
            at += count * rows
        else:
            for i in range(count):
                for j in range(cols // block):
                    total_ref[i, :, j * block : (j + 1) * block] = total[at : at + rows]
                    at += rows
        squares = total_ref[...]
        squares = squares * squares + 1e-30
        rows_ref[...] = jnp.sum(squares, axis=-1, keepdims=True)
        cols_ref[...] = jnp.sum(squares, axis=1, keepdims=True)


def ffn_kernel(at_ref, *refs, fold, narrow, pieces, first_out):
    c_refs, refs = refs[:narrow], refs[narrow:]
    fin_refs, refs = refs[:pieces], refs[pieces:]
    fout_refs, refs = refs[:pieces], refs[pieces:]
    (x2_ref, h_ref, g_ref), refs = refs[:3], refs[3:]
    out_refs, refs = refs[:narrow], refs[narrow:]
    (dx_ref, dg_ref, kin_ref, sin_ref, kout_ref, sout_ref, acc_ref, dh_ref, turned_ref, ht_ref,
     gout_ref, c_ref, fin_ref, fout_ref, fin_sems, fout_sems) = refs
    step, steps = pl.program_id(0), pl.num_programs(0)
    core = at_ref[0]

    @pl.when(step == 0)
    def _():
        copies = start_weights(at_ref[3], fin_refs, fin_ref, fin_sems, pl.ds(0, fin_ref.shape[0]))
        copies += start_weights(
            at_ref[3], fout_refs, fout_ref, fout_sems, pl.ds(first_out, fout_ref.shape[0])
        )
        join_rows(at_ref[2], c_refs, c_ref)
        acc_ref[...] = x2_ref[...]
        dh_ref[...] = jnp.zeros_like(dh_ref)
        fold_rows(core, h_ref[...].T, turned_ref, ht_ref, fold)
        for copy in copies:
            copy.wait()

    hidden_in, cot = h_ref[...], c_ref[...]
    size = fin_ref.shape[2]
    blocks = gout_ref.shape[0] // size
    for block in range(blocks):
        part = slice(block * size, (block + 1) * size)
        at_gate = step * blocks + block
        at_up = fin_ref.shape[0] // 2 + at_gate
        gate = dot_nn(hidden_in, fin_ref[at_gate])
        up = dot_nn(hidden_in, fin_ref[at_up])
        square = gate * gate
        bent = jnp.tanh(0.7978845608028654 * (gate + 0.044715 * square * gate))
        plus = 0.5 * (1.0 + bent)
        act = gate * plus
        slope = plus + 0.5 * gate * (1.0 - bent * bent) * (
            0.7978845608028654 + (3 * 0.044715 * 0.7978845608028654) * square
        )
        hidden = (act * up).astype(bf16)
        down_rows = pl.ds(pl.multiple_of(at_gate * size, size), size)
        down = jnp.concatenate(
            [fout_ref[i, down_rows, :] for i in range(fout_ref.shape[0])], axis=1
        )
        acc_ref[...] += dot_nn(hidden, down)
        grad = dot_nt(cot, down)
        d_gate = (grad * up * slope).astype(bf16)
        d_up = (grad * act).astype(bf16)
        dh_ref[...] += dot_nt(d_gate, fin_ref[at_gate]) + dot_nt(d_up, fin_ref[at_up])
        half = ht_ref.shape[0] // 2
        for index, right in ((0, d_gate), (1, d_up)):
            product = dot_nn(ht_ref[...], right).astype(bf16)
            kin_ref[index, :, part] = product[:half]
            sin_ref[index, :, part] = product[half:]
        gout_ref[part, :] = dot_nn(hidden.T, cot).astype(bf16)
    rows = gout_ref.shape[0] // 2
    kept = pl.multiple_of(core * rows, 16) if fold else 0
    sent = pl.multiple_of((1 - core) * rows, 16) if fold else rows
    kout_ref[...] = gout_ref[pl.ds(kept, rows), :]
    sout_ref[...] = gout_ref[pl.ds(sent, rows), :]

    @pl.when(step == steps - 1)
    def _():
        split_rows(at_ref[2], acc_ref, out_refs)
        back, d_gain = norm_back(dh_ref[...], x2_ref[...], g_ref[2:3, :])
        dx_ref[...] = cot.astype(f32) + back
        dg_ref[...] = d_gain


def attend_back_kernel(at_ref, *refs, pieces, which, causal):
    w_refs, refs = refs[:pieces], refs[pieces:]
    table_ref = None
    if causal:
        table_ref, refs = refs[0], refs[1:]
    dx_ref, o_ref, qkv_ref, extra_ref, peak_ref, inv_ref, dqkv_ref = refs[:7]
    ds_out, refs = (refs[7], refs[8:]) if causal else (None, refs[7:])
    do_ref, dsum_ref, p_ref, ds_ref, dqt_ref, w_ref, sems = refs
    copies = start_weights(at_ref[3], w_refs, w_ref, sems, pl.ds(which, 1))
    branch = dx_ref[...].astype(bf16)
    for copy in copies:
        copy.wait()
    for start, size in tiles_of(o_ref.shape[1]):
        do_ref[:, start : start + size] = dot_nt(
            branch, w_ref[0, start : start + size, :]
        ).astype(bf16)
    head_sums(do_ref[...], o_ref[...], dsum_ref)
    attend_back(qkv_ref, extra_ref, table_ref, do_ref, dsum_ref, peak_ref, inv_ref, dqkv_ref,
                p_ref, ds_ref, dqt_ref, ds_out)


def second_back_kernel(at_ref, *refs, pieces, narrow, fold):
    w_refs, refs = refs[:pieces], refs[pieces:]
    (dqkv_ref, dx2_ref, o_ref, h_ref, m_ref, x1_ref, o1_ref, g_ref), refs = refs[:8], refs[8:]
    gm_refs, refs = refs[:narrow], refs[narrow:]
    (dx1_ref, dg_ref, keep_ref, send_ref, turned_ref, left_ref, gm_ref, w_ref, sems) = refs
    core = at_ref[0]
    copies = start_weights(at_ref[3], w_refs, w_ref, sems, pl.ds(1, 3))
    gm_ref[...] = dx2_ref[...].astype(bf16)
    fold_rows(core, o_ref[...].T, turned_ref, left_ref, fold)
    for copy in copies:
        copy.wait()
    weight_grad(left_ref, gm_ref, keep_ref, send_ref, 4)
    fold_rows(core, h_ref[...].T, turned_ref, left_ref, fold)
    weight_grad(left_ref, dqkv_ref.at[0], keep_ref, send_ref, 1)
    fold_rows(core, m_ref[...].T, turned_ref, left_ref, fold)
    for i in (1, 2):
        weight_grad(left_ref, dqkv_ref.at[i], keep_ref, send_ref, i + 1)
    for start, size in tiles_of(o_ref.shape[1]):
        rows = slice(start, start + size)
        gm_ref[:, rows] = (
            dot_nt(dqkv_ref[1], w_ref[1, rows, :]) + dot_nt(dqkv_ref[2], w_ref[2, rows, :])
        ).astype(bf16)
        dx1_ref[:, rows] = dot_nt(dqkv_ref[0], w_ref[0, rows, :])
    split_rows(at_ref[2], gm_ref, gm_refs)
    back, d_gain = norm_back(dx1_ref[...], x1_ref[...], g_ref[1:2, :])
    d_x1 = dx2_ref[...] + back
    dx1_ref[...] = d_x1
    dg_ref[...] = d_gain
    gm_ref[...] = d_x1.astype(bf16)
    fold_rows(core, o1_ref[...].T, turned_ref, left_ref, fold)
    weight_grad(left_ref, gm_ref, keep_ref, send_ref, 0)


def first_back_kernel(at_ref, *refs, pieces, narrow, fold):
    w_refs, refs = refs[:pieces], refs[pieces:]
    (dqkv_ref, h_ref, dx1_ref, x_ref, g_ref), refs = refs[:5], refs[5:]
    gx_refs, refs = refs[:narrow], refs[narrow:]
    dg_ref, keep_ref, send_ref, turned_ref, left_ref, dh_ref, w_ref, sems = refs
    copies = start_weights(at_ref[3], w_refs, w_ref, sems, pl.ds(0, 3))
    fold_rows(at_ref[0], h_ref[...].T, turned_ref, left_ref, fold)
    for copy in copies:
        copy.wait()
    for i in range(3):
        weight_grad(left_ref, dqkv_ref.at[i], keep_ref, send_ref, i)
    for start, size in tiles_of(h_ref.shape[1]):
        rows = slice(start, start + size)
        dh_ref[:, rows] = (
            dot_nt(dqkv_ref[0], w_ref[0, rows, :])
            + dot_nt(dqkv_ref[1], w_ref[1, rows, :])
            + dot_nt(dqkv_ref[2], w_ref[2, rows, :])
        )
    back, d_gain = norm_back(dh_ref[...], x_ref[...].astype(f32), g_ref[0:1, :])
    dh_ref[...] = dx1_ref[...] + back
    split_rows(at_ref[2], dh_ref, gx_refs)
    dg_ref[...] = d_gain


def table_kernel(ds_ref, index_ref, out_ref, acc_ref, *, buckets):
    heads, keys, queries = ds_ref.shape
    acc_ref[...] = jnp.zeros_like(acc_ref)

    def group(at, carry):
        rows = pl.ds(pl.multiple_of(at * 16, 16), 16)
        index = index_ref[rows, :]
        grads = ds_ref[:, rows, :].reshape(heads * 16, queries)
        hot = jnp.concatenate(
            [(index == b).astype(f32).astype(bf16) for b in range(buckets)], axis=0
        )
        acc_ref[...] += dot_nt(grads, hot)
        return carry

    lax.fori_loop(0, keys // 16, group, 0)
    shape = acc_ref.shape
    same = (
        lax.broadcasted_iota(jnp.int32, shape, 0) % 16
        == lax.broadcasted_iota(jnp.int32, shape, 1) % 16
    )
    kept = jnp.where(same, acc_ref[...], 0.0).reshape(heads, 16, shape[1]).sum(axis=1)
    gather = (
        lax.broadcasted_iota(jnp.int32, (shape[1], 128), 0) // 16
        == lax.broadcasted_iota(jnp.int32, (shape[1], 128), 1)
    ).astype(f32)
    out_ref[...] = lax.dot_general(
        kept, gather, (((1,), (0,)), ((), ())),
        preferred_element_type=f32, precision=lax.Precision.HIGHEST,
    )


def cost_of(us):
    return pl.CostEstimate(flops=int(us * 1.15e9), bytes_accessed=MIB, transcendentals=0)


def room_for(arrays, scratch):
    size = sum(v.size * v.dtype.itemsize for v in arrays)
    for ref in scratch:
        shape = getattr(ref, "shape", ())
        if ref.memory_space == pltpu.VMEM:
            rows = -(-shape[-2] // 8) * 8
            size += math.prod(shape[:-2]) * rows * shape[-1] * jnp.dtype(ref.dtype).itemsize
    return (size // MIB + 8) * MIB


def call(kernel, outs, scratch, *args, scalars=1, loose=(), us=2, name=None):
    spaces = [
        pltpu.SMEM if i < scalars else pl.ANY if i in loose else pltpu.VMEM
        for i in range(len(args))
    ]
    return pl.pallas_call(
        kernel,
        out_shape=outs,
        in_specs=[pl.BlockSpec(memory_space=space) for space in spaces],
        out_specs=[pl.BlockSpec(memory_space=pltpu.VMEM)] * len(outs),
        scratch_shapes=scratch,
        compiler_params=pltpu.CompilerParams(
            vmem_limit_bytes=room_for(
                [v for v, space in zip(args, spaces) if space == pltpu.VMEM] + list(outs), scratch
            )
        ),
        cost_estimate=cost_of(us),
        name=name,
    )(*args)


def shape_of(shape, dtype):
    return jax.ShapeDtypeStruct(tuple(shape), dtype)


def permuted(value, wide_bits, narrow_bits):
    wide, narrow = lax.axis_size("wide"), lax.axis_size("narrow")
    pairs = [
        (w * narrow + n, (w ^ wide_bits) * narrow + (n ^ narrow_bits))
        for w in range(wide)
        for n in range(narrow)
    ]
    return lax.ppermute(value, BOTH, pairs)


def after(value, *done):
    return lax.optimization_barrier((value, *done))[0]


def ordered(at, pieces, shares=None):
    first = pieces[0]
    if first.ndim == 2:
        shapes = [(len(pieces),) + first.shape]
    else:
        shapes = [(k, len(pieces)) + first.shape[1:] for k in shares]
    outs = [shape_of(shape, first.dtype) for shape in shapes]
    return call(
        functools.partial(order_kernel, outs=len(outs)), outs, [], at, *pieces, us=1, name="order"
    )


def local_stats(gradient):
    squares = gradient * gradient + 1e-30
    return (jnp.sum(squares, axis=-1, keepdims=True), jnp.sum(squares, axis=-2, keepdims=True))


class Scatter:
    def __init__(self, at, pairs, fast, narrow):
        self.at, self.fast, self.narrow, self.pairs = at, fast, narrow, pairs
        self.done = pairs[0][0]
        if not fast:
            return
        keeps = [keep.reshape(-1, keep.shape[1], keep.shape[2]) for keep, _ in pairs]
        sends = [send for _, send in pairs]
        if len(pairs) == 2:
            keeps[1] = keeps[1].reshape(1, -1, keeps[1].shape[2])
            sends[1] = sends[1].reshape(keeps[1].shape)
        self.shapes = [(k.shape[0], k.shape[1] // 4, k.shape[2]) for k in keeps]
        size = sum(k.size for k in keeps) // 4
        cols = TILE if len(pairs) == 2 else keeps[0].shape[2]
        self.rows, self.cols = size // cols, cols
        half = (self.rows // 2, cols)
        recvs = [permuted(send, 1, 0) for send in sends]
        self.own, self.kept_x, self.kept_y, to_x, to_y = call(
            functools.partial(spread_kernel, count=len(pairs)),
            [shape_of((self.rows, cols), f32), shape_of(half, f32), shape_of(half, f32),
             shape_of((2,) + half, bf16), shape_of((2,) + half, bf16)],
            [], at, *keeps, *recvs, us=3, name="spread",
        )
        self.out = (to_x, to_y)
        self.done = self.own

    def middle(self, *done):
        if not self.fast:
            return
        self.own = after(self.own, *done)
        half = (self.rows // 2, self.cols)
        from_x, from_y = permuted(self.out[0], 2, 0), permuted(self.out[1], 4, 0)
        self.own, to_x, to_y = call(
            middle_kernel,
            [shape_of((self.rows, self.cols), f32), shape_of(half, bf16), shape_of(half, bf16)],
            [], self.own, self.kept_x, self.kept_y, from_x, from_y, scalars=0, name="middle",
        )
        self.out = (to_x, to_y)
        self.done = self.own

    def narrowed(self, riders, *done):
        self.riders = riders
        if not self.fast:
            return
        self.own = after(self.own, *done)
        from_x, from_y = permuted(self.out[0], 2, 0), permuted(self.out[1], 4, 0)
        if len(self.shapes) == 2:
            (k, rows, cols), (_, rows_out, cols_out) = self.shapes
            sizes = [rows] * (k * cols // TILE) + [rows_out] * (cols_out // TILE)
        else:
            sizes = [self.shapes[0][1]] * self.shapes[0][0]
        spots, begin = [], 0
        for size in sizes:
            spots.append((begin, size // self.narrow))
            begin += size
        share = self.rows // self.narrow
        ahead = riders[0].size // self.cols if riders else 0
        self.out = call(
            functools.partial(narrow_kernel, narrow=self.narrow, spots=spots),
            [
                shape_of((share + ahead, self.cols) if d else (share, self.cols), bf16 if d else f32)
                for d in range(self.narrow)
            ],
            [pltpu.VMEM((self.rows, self.cols), f32)], self.at, self.own, from_x, from_y,
            *riders[1:], name="narrow",
        )
        self.done = self.out[0]

    def total(self, *done):
        if not self.fast:
            results = []
            for keep, send in self.pairs:
                whole = jnp.concatenate([keep, send], axis=1)
                if keep.shape[0] == 4:
                    whole = whole.reshape(1, -1, whole.shape[2])
                total = lax.psum_scatter(whole, BOTH, scatter_dimension=1, tiled=True).astype(f32)
                results.append((total, *local_stats(total)))
            return results
        parts = [permuted(v, 0, d) if d else v for d, v in enumerate(self.out)]
        parts[0] = after(parts[0], *done)
        if self.riders:
            rider = self.riders[0]
            (self.ridden,) = call(
                join_kernel, [shape_of((self.narrow,) + rider.shape, bf16)], [], self.at,
                after(rider, *done), *parts[1:], name="join",
            )
        outs = []
        for k, rows, cols in self.shapes:
            rows //= self.narrow
            outs += [
                shape_of((k, rows, cols), f32), shape_of((k, rows, 1), f32),
                shape_of((k, 1, cols), f32),
            ]
        flat = call(
            functools.partial(total_kernel, narrow=self.narrow), outs, [], *parts, scalars=0,
            name="total",
        )
        return [
            tuple(flat[3 * i : 3 * i + 3])
            for i in range(len(self.shapes))
        ]


def summed_all(flat, fast):
    if not fast:
        return lax.psum(flat, BOTH)
    flat = flat + permuted(flat, 1, 0)
    flat = (flat + permuted(flat, 2, 0)) + (permuted(flat, 4, 0) + permuted(flat, 6, 0))
    return (flat + permuted(flat, 0, 1)) + (permuted(flat, 0, 2) + permuted(flat, 0, 3))


def body(
    targets, memory, cotangent, target_segments, memory_segments, buckets,
    attn_in, attn_out, gains, ff_in, ff_out, bias_table,
):
    wide, narrow = lax.axis_size("wide"), lax.axis_size("narrow")
    at_wide, at_narrow = lax.axis_index("wide"), lax.axis_index("narrow")
    fast = wide == 8 and narrow == 4
    at = jnp.stack([at_wide % 2, at_wide // 2, at_narrow, at_wide]).astype(jnp.int32)
    width, ff_width = attn_in.shape[2], ff_in.shape[2]
    bucket_count, heads = bias_table.shape
    chunk = gains.shape[1]
    local_tokens = targets.shape[1]
    tokens = local_tokens * narrow
    assert targets.shape[0] == narrow

    def over_narrow(pieces):
        return [permuted(v, 0, d) if d else v for d, v in enumerate(pieces)]

    def to_owners(pieces, *done):
        pieces = over_narrow(pieces)
        return ordered(at, [after(pieces[0], *done)] + pieces[1:])[0]

    device = at_wide * narrow + at_narrow
    gain_rows = lax.dynamic_update_slice(
        jnp.zeros((chunk, width), bf16), gains.astype(bf16), (0, device * chunk)
    )
    if fast:
        share = local_tokens // wide
        held = lax.dynamic_slice_in_dim(buckets, at_wide * share, share, 0).astype(bf16)
        gain_rows = lax.dynamic_update_slice(gain_rows, held, (chunk - share, 0))
    first_local = jnp.concatenate([attn_in[:3].astype(bf16), gain_rows[None]])
    second_local = jnp.concatenate([attn_out[:1], attn_in[3:], attn_out[1:]]).astype(bf16)
    piece16 = shape_of((local_tokens, width), bf16)
    near_rows = local_tokens * width // TILE + 16
    packed = call(
        functools.partial(pack_kernel, narrow=narrow),
        [shape_of((near_rows, TILE), bf16)] * narrow
        + [piece16] * (2 * narrow),
        [], at, targets, memory, cotangent, target_segments, memory_segments,
        us=4, name="pack",
    )
    near, m_out, c_out = packed[:narrow], packed[narrow : 2 * narrow], packed[2 * narrow :]
    lanes = TILE
    fin_blocks = ff_in.astype(bf16).reshape(2, chunk, ff_width // lanes, lanes)
    fin_blocks = fin_blocks.transpose(0, 2, 1, 3).reshape(-1, chunk, lanes)
    out_rows_here = ff_out.shape[0]
    fout_blocks = ff_out.astype(bf16).reshape(out_rows_here, width // lanes, lanes)
    fout_blocks = fout_blocks.transpose(1, 0, 2).reshape(-1, chunk, lanes)
    fin_count, fout_count = fin_blocks.shape[0], fout_blocks.shape[0]
    ffn_local = jnp.concatenate([fin_blocks, fout_blocks])

    def regroup_out(stack, owners):
        stack = stack.reshape(fout_count, owners, chunk, lanes).transpose(1, 0, 2, 3)
        stack = stack.reshape(owners, width // lanes, out_rows_here, lanes)
        return stack.transpose(1, 0, 2, 3).reshape(width // lanes, -1, lanes)

    def over_plane(stack, diagonal_last=True):
        near = [stack] + [permuted(stack, 2 * d, 0) for d in (1, 2)]
        last = after(stack, *near[1:]) if diagonal_last else stack
        return near + [permuted(last, 6, 0)]

    def with_other_core(plane, *done):
        return plane + [permuted(jnp.concatenate([after(plane[0], *done)] + plane[1:]), 1, 0)]

    if fast:
        first_near = over_narrow([first_local] * narrow)
        first_near[0] = after(first_near[0], near[0])
        (stack,) = ordered(at, first_near, (4,))
        near = [near[0]] + [after(v, stack) for v in near[1:]]
        plane_first = over_plane(stack.reshape(4, -1, width), False)
        held_out = []
    else:
        w_first = [lax.all_gather(first_local, BOTH, axis=1, tiled=True)]
        w_second = [lax.all_gather(second_local, BOTH, axis=1, tiled=True)]
        held_out = [lax.all_gather(buckets.astype(bf16), "narrow", axis=0, tiled=True).T]
    near = over_narrow(near)
    allowed, cross_mask = call(
        functools.partial(
            prepare_kernel, narrow=narrow, skip=local_tokens * width // TILE,
        ),
        [shape_of((tokens, tokens), f32), shape_of((tokens, tokens), f32)],
        [pltpu.VMEM((16, tokens), f32)],
        at, *near, us=2, name="prepare",
    )
    (squares,) = call(
        square_kernel, [shape_of((16, 128), f32)], [],
        *(after(v, allowed) for v in (attn_in, attn_out, ff_in, ff_out)), scalars=0, name="squares",
    )
    if fast:
        w_first = with_other_core(plane_first, allowed)
        second_near = over_narrow([after(second_local, allowed)] * narrow)
    table = jnp.concatenate(
        [bias_table.T, jnp.full((heads, 128 - bucket_count), NEG, f32)], axis=1
    )
    row16 = shape_of((tokens, width), bf16)
    row32 = shape_of((tokens, width), f32)
    three = shape_of((3, tokens, width), bf16)
    stat = shape_of((heads, 1, tokens), f32)
    gain_out = shape_of((1, width), f32)
    pair_t = pltpu.VMEM((128, tokens), f32)
    pieces = len(w_first)
    weights = lambda count: pltpu.VMEM((count, width, width), bf16)
    sems = pltpu.SemaphoreType.DMA((8,))
    stack_of = lambda count: shape_of((count, width, width), bf16)
    w_first, index, g, x, h1, qkv1, o1, peak1, inv1 = call(
        functools.partial(
            first_kernel, pieces=pieces, narrow=narrow, chunk=chunk, bucket_count=bucket_count
        ),
        [stack_of(4), shape_of((tokens, tokens), jnp.int32), shape_of((8, width), f32), row16,
         row16, three, row16, stat, stat],
        [pair_t, sems],
        at, *near, *w_first, *held_out, allowed, table,
        loose=range(1 + narrow, 1 + narrow + pieces), us=16, name="first",
    )
    if fast:
        second_near[0] = after(second_near[0], h1)
        (stack,) = ordered(at, second_near, (5,))
        plane_second = over_plane(stack.reshape(5, -1, width))
        ffn_near = over_narrow([after(ffn_local, stack)] * narrow)
        ffn_near[0] = after(ffn_near[0], plane_second[1], plane_second[2])
        (stack,) = ordered(at, ffn_near, (fin_count + fout_count,))
        stack = stack.reshape(fin_count + fout_count, -1, lanes)
        stack_out = regroup_out(stack[fin_count:], narrow).reshape(fout_count, -1, lanes)
        stack = jnp.concatenate([stack[:fin_count], stack_out])
        w_second = with_other_core(plane_second, stack)
        m_out = [m_out[0]] + [after(v, stack) for v in m_out[1:]]
        plane_ffn = over_plane(after(stack, *plane_second[1:]))
        o1 = after(o1, plane_ffn[1], plane_ffn[2], squares)
    m_pieces = over_narrow(m_out)
    if fast:
        c_out = [c_out[0]] + [after(v, *m_pieces[1:]) for v in c_out[1:]]
    c_pieces = over_narrow(c_out)
    w_second, m, x1, h2, qkv2, o2, x2, h3, peak2, inv2 = call(
        functools.partial(second_kernel, pieces=pieces, narrow=narrow),
        [stack_of(5), row16, row32, row16, three, row16, row32, row16, stat, stat],
        [pair_t, sems],
        at, *m_pieces, *w_second, x, o1, cross_mask, g,
        loose=range(1 + narrow, 1 + narrow + pieces), us=21, name="second",
    )

    if fast:
        ffn_pieces = with_other_core(plane_ffn, x2, *c_pieces[1:])
        w_fin = ffn_pieces
        w_fout = [v.reshape(-1, narrow * out_rows_here, lanes) for v in ffn_pieces]
    else:
        every = lax.all_gather(ffn_local, BOTH, axis=1, tiled=True)
        w_fin, w_fout = [every], [regroup_out(every[fin_count:], wide * narrow)]
    steps = 4
    part = ff_width // steps
    half = width // 2
    whole = lambda shape: pl.BlockSpec(shape, lambda i: (0,) * len(shape))
    outs = pl.pallas_call(
        functools.partial(
            ffn_kernel, fold=fast, narrow=narrow, pieces=pieces,
            first_out=w_fout[0].shape[0] - width // lanes if fast else 0,
        ),
        grid=(steps,),
        in_specs=[pl.BlockSpec(memory_space=pltpu.SMEM)]
        + [whole((local_tokens, width))] * narrow
        + [pl.BlockSpec(memory_space=pl.ANY)] * (2 * pieces)
        + [whole((tokens, width)), whole((tokens, width)), whole((8, width))],
        out_specs=[whole((local_tokens, width))] * narrow
        + [
            whole((tokens, width)), whole((1, width)),
            pl.BlockSpec((2, half, part), lambda i: (0, 0, i)),
            pl.BlockSpec((2, half, part), lambda i: (0, 0, i)),
            pl.BlockSpec((None, part // 2, width), lambda i: (i, 0, 0)),
            pl.BlockSpec((None, part // 2, width), lambda i: (i, 0, 0)),
        ],
        out_shape=[piece16] * narrow
        + [
            row32, gain_out,
            shape_of((2, half, ff_width), bf16), shape_of((2, half, ff_width), bf16),
            shape_of((steps, part // 2, width), bf16), shape_of((steps, part // 2, width), bf16),
        ],
        scratch_shapes=[
            pltpu.VMEM((tokens, width), f32), pltpu.VMEM((tokens, width), f32),
            pltpu.VMEM((width, tokens), bf16), pltpu.VMEM((width, tokens), bf16),
            pltpu.VMEM((part, width), bf16), pltpu.VMEM((tokens, width), bf16),
            pltpu.VMEM((fin_count, width, lanes), bf16),
            pltpu.VMEM((width // lanes, ff_width, lanes), bf16), sems, sems,
        ],
        compiler_params=pltpu.CompilerParams(vmem_limit_bytes=40 * MIB),
        cost_estimate=cost_of(24),
        name="ffn",
    )(at, *c_pieces, *w_fin, *w_fout, x2, h3, g)
    out_pieces = outs[:narrow]
    dx2, gain3, keep_fin, send_fin, keep_fout, send_fout = outs[narrow:]
    ffn_sum = Scatter(at, [(keep_fin, send_fin), (keep_fout, send_fout)], fast, narrow)
    if fast:
        dx2 = after(dx2, ffn_sum.done)
    square = pltpu.VMEM((tokens, tokens), bf16)
    attend_scratch = [
        pltpu.VMEM((tokens, width), bf16), pltpu.VMEM((heads, 1, tokens), f32), square, square,
        pair_t, weights(1), sems,
    ]
    turned = pltpu.VMEM((width, tokens), bf16)
    grads = lambda count: shape_of((count, half, width), bf16)
    (dqkv2,) = call(
        functools.partial(attend_back_kernel, pieces=1, which=4, causal=False),
        [three], attend_scratch,
        at, w_second, dx2, o2, qkv2, cross_mask, peak2, inv2,
        loose=(1,), us=18, name="cross_back",
    )
    output = to_owners(out_pieces, dqkv2)
    ffn_sum.middle(dqkv2)
    if fast:
        dqkv2 = after(dqkv2, ffn_sum.done, output)
    outs = call(
        functools.partial(second_back_kernel, pieces=1, narrow=narrow, fold=fast),
        [piece16] * narrow + [row32, gain_out, grads(5), grads(5)],
        [turned, turned, pltpu.VMEM((tokens, width), bf16), weights(3), sems],
        at, w_second, dqkv2, dx2, o2, h2, m, x1, o1, g,
        loose=(1,), us=12, name="second_back",
    )
    gm_pieces = outs[:narrow]
    dx1, gain2, keep_second, send_second = outs[narrow:]
    ffn_sum.narrowed([], gain2)
    if fast:
        send_second = after(send_second, ffn_sum.done)
    second_sum = Scatter(at, [(keep_second, send_second)], fast, narrow)
    if fast:
        dx1 = after(dx1, second_sum.done, ffn_sum.done)
    dqkv1, ds = call(
        functools.partial(attend_back_kernel, pieces=1, which=0, causal=True),
        [three, shape_of((heads, tokens, tokens), bf16)], attend_scratch,
        at, w_second, table, dx1, o1, qkv1, index, peak1, inv1,
        loose=(1,), us=20, name="self_back",
    )
    (sum_fin, fin_rows, fin_part), (sum_fout, fout_rows, fout_part) = ffn_sum.total(dqkv1)
    second_sum.middle(dqkv1)
    if fast:
        dqkv1 = after(dqkv1, sum_fin, second_sum.done)
    outs = call(
        functools.partial(first_back_kernel, pieces=1, narrow=narrow, fold=fast),
        [piece16] * narrow + [gain_out, grads(3), grads(3)],
        [turned, turned, pltpu.VMEM((tokens, width), f32), weights(3), sems],
        at, w_first, dqkv1, h1, dx1, x, g,
        loose=(1,), us=9, name="first_back",
    )
    gx_pieces = outs[:narrow]
    gain1, keep_first, send_first = outs[narrow:]
    grad_memory = to_owners(gm_pieces, gain1)
    second_sum.narrowed(gx_pieces, gain1, grad_memory)
    if fast:
        send_first = after(send_first, second_sum.done)
    first_sum = Scatter(at, [(keep_first, send_first)], fast, narrow)
    if fast:
        ds = after(ds, first_sum.done, second_sum.done)
    (table_part,) = call(
        functools.partial(table_kernel, buckets=bucket_count),
        [shape_of((heads, 128), f32)],
        [pltpu.VMEM((heads * 16, bucket_count * 16), f32)], ds, index, scalars=0, us=11,
        name="table",
    )
    first_sum.middle(table_part)
    first_sum.narrowed([])
    ((sum_second, second_rows, second_part),) = second_sum.total(first_sum.done)
    ((sum_first, first_rows, first_part),) = first_sum.total()
    grad_targets = second_sum.ridden if fast else to_owners(gx_pieces)
    parts = (gain1, gain2, gain3, first_part, second_part, fin_part, fout_part, table_part, squares)
    rows = sum(v.size for v in parts) // 128
    (tally,) = call(
        tally_kernel, [shape_of((-(-rows // 8) * 8, 128), f32)], [], *parts, scalars=0, us=1,
        name="tally",
    )
    tally = summed_all(tally, fast)
    (
        sum_in, sum_out, new_in, new_out, new_fin, new_fout, sum_gain, in_cols, out_cols, fin_cols,
        fout_cols, grad_table, new_table,
    ) = call(
        functools.partial(update_kernel, buckets=bucket_count),
        [
            shape_of(attn_in.shape, f32), shape_of(attn_out.shape, f32), shape_of(attn_in.shape, f32),
            shape_of(attn_out.shape, f32), shape_of(ff_in.shape, f32), shape_of(ff_out.shape, f32),
            shape_of((3, width), f32), shape_of((6, width), f32), shape_of((2, width), f32),
            shape_of((2, ff_width), f32), shape_of((1, width), f32),
            shape_of(bias_table.shape, f32), shape_of(bias_table.shape, f32),
        ],
        [], tally, sum_first, sum_second, sum_fin, sum_fout, first_rows, second_rows, fin_rows,
        fout_rows, attn_in, attn_out, ff_in, ff_out, table, scalars=0, us=3, name="update",
    )
    sum_gain = lax.dynamic_slice_in_dim(sum_gain, device * chunk, chunk, 1)
    in_rows = jnp.concatenate([first_rows, second_rows[1:4]])[:, :, 0]
    out_rows = jnp.stack([second_rows[0], second_rows[4]])[:, :, 0]
    return (
        output, grad_targets, grad_memory,
        sum_in, sum_out, sum_gain, sum_fin, sum_fout[0], grad_table,
        in_rows, in_cols, out_rows, out_cols, fin_rows[:, :, 0], fin_cols, fout_rows[0, :, 0],
        fout_cols[0], new_in, new_out, new_fin, new_fout, new_table,
    )


def solution(mesh):
    in_specs = (
        P("wide", "narrow", None),
        P("wide", "narrow", None),
        P("wide", "narrow", None),
        P("wide", "narrow"),
        P("wide", "narrow"),
        P("narrow", None),
        P(None, ("wide", "narrow"), None),
        P(None, ("wide", "narrow"), None),
        P(None, ("wide", "narrow")),
        P(None, ("wide", "narrow"), None),
        P(("wide", "narrow"), None),
        P(),
    )
    out_specs = (
        P("wide", "narrow", None),
        P("wide", "narrow", None),
        P("wide", "narrow", None),
        P(None, ("wide", "narrow"), None),
        P(None, ("wide", "narrow"), None),
        P(None, ("wide", "narrow")),
        P(None, ("wide", "narrow"), None),
        P(("wide", "narrow"), None),
        P(),
        P(None, ("wide", "narrow")),
        P(),
        P(None, ("wide", "narrow")),
        P(),
        P(None, ("wide", "narrow")),
        P(),
        P(("wide", "narrow")),
        P(),
        P(None, ("wide", "narrow"), None),
        P(None, ("wide", "narrow"), None),
        P(None, ("wide", "narrow"), None),
        P(("wide", "narrow"), None),
        P(),
    )
    return jax.shard_map(body, mesh=mesh, in_specs=in_specs, out_specs=out_specs, check_vma=False)
```

```python
import functools
import math

import jax
import jax.numpy as jnp
from jax import lax
from jax.experimental import pallas as pl
from jax.experimental.pallas import tpu as pltpu
from jax.sharding import PartitionSpec as P

bf16, f32 = jnp.bfloat16, jnp.float32
BOTH = ("wide", "narrow")
NEG = -1e9
TILE = 256
MIB = 1 << 20


def dot_nn(left, right):
    return lax.dot_general(left, right, (((1,), (0,)), ((), ())), preferred_element_type=f32)


def dot_nt(left, right):
    return lax.dot_general(left, right, (((1,), (1,)), ((), ())), preferred_element_type=f32)


def unit_of(values):
    inv_rms = lax.rsqrt(jnp.mean(values * values, axis=-1, keepdims=True) + 1e-06)
    return values * inv_rms, inv_rms


def norm_back(incoming, values, gain_row):
    unit, inv_rms = unit_of(values)
    scaled = incoming * gain_row
    inner = jnp.mean(scaled * unit, axis=-1, keepdims=True)
    return inv_rms * (scaled - unit * inner), jnp.sum(incoming * unit, axis=0, keepdims=True)


def tiles_of(width):
    return [(start, min(TILE, width - start)) for start in range(0, width, TILE)]


def project(left, w_ref, index, store):
    for start, size in tiles_of(w_ref.shape[2]):
        store(start, size, dot_nn(left, w_ref[index, :, start : start + size]))


def half_lanes(second):
    lane = lax.broadcasted_iota(jnp.int32, (1, 128), 1)
    return ((lane >= 64) == bool(second)).astype(bf16)


def biased(table_row, index):
    spread = jnp.broadcast_to(table_row, (index.shape[0], 128))
    return jnp.concatenate(
        [
            jnp.take_along_axis(
                spread, index[:, at : at + 128], axis=1, mode="promise_in_bounds"
            )
            for at in range(0, index.shape[1], 128)
        ],
        axis=1,
    )


def query_blocks(keys, queries, causal):
    return [
        (at, min(keys, at + TILE) if causal else keys) for at in range(0, queries, TILE)
    ]


def attend(qkv_ref, extra_ref, table_ref, o_ref, peak_ref, inv_ref, ot_ref):
    causal = table_ref is not None
    keys = qkv_ref.shape[1]

    def pair(at_pair, carry):
        lanes = pl.ds(pl.multiple_of(at_pair * 128, 128), 128)
        query, key, value = (qkv_ref[i, :, lanes] for i in range(3))
        value_t = value.T
        for second in range(2):
            head = at_pair * 2 + second
            key_half = key * half_lanes(second)
            for start, last in query_blocks(keys, keys, causal):
                part = slice(start, start + TILE)
                scores = dot_nt(key_half[:last], query[part])
                if causal:
                    scores += biased(table_ref[pl.ds(head, 1), :], extra_ref[:last, part])
                else:
                    scores += extra_ref[:last, part]
                peak = jnp.max(scores, axis=0, keepdims=True)
                grown = jnp.exp(scores - peak)
                inverse = 1.0 / jnp.sum(grown, axis=0, keepdims=True)
                mixed = dot_nn(value_t[second * 64 : second * 64 + 64, :last], grown.astype(bf16))
                ot_ref[second * 64 : second * 64 + 64, part] = mixed * inverse
                peak_ref[head, :, part] = peak
                inv_ref[head, :, part] = inverse
        o_ref[:, lanes] = ot_ref[...].T.astype(bf16)
        return carry

    lax.fori_loop(0, qkv_ref.shape[2] // 128, pair, 0)


def attend_back(
    qkv_ref, extra_ref, table_ref, do_ref, dsum_ref, peak_ref, inv_ref,
    dqkv_ref, p_ref, ds_ref, dqt_ref, ds_out,
):
    causal = table_ref is not None
    keys = qkv_ref.shape[1]
    first_half = lax.broadcasted_iota(jnp.int32, (1, 128), 1) < 64

    def pair(at_pair, carry):
        lanes = pl.ds(pl.multiple_of(at_pair * 128, 128), 128)
        query, key, value = (qkv_ref[i, :, lanes] for i in range(3))
        grad = do_ref[:, lanes]
        key_t = key.T
        for second in range(2):
            head = at_pair * 2 + second
            half = half_lanes(second)
            key_half, value_half = key * half, value * half
            for start, last in query_blocks(keys, keys, causal):
                part = slice(start, start + TILE)
                scores = dot_nt(key_half[:last], query[part])
                if causal:
                    scores += biased(table_ref[pl.ds(head, 1), :], extra_ref[:last, part])
                else:
                    scores += extra_ref[:last, part]
                weights = jnp.exp(scores - peak_ref[head, :, part]) * inv_ref[head, :, part]
                grad_weights = dot_nt(value_half[:last], grad[part])
                grad_scores = (weights * (grad_weights - dsum_ref[head, :, part])).astype(bf16)
                p_ref[:last, part] = weights.astype(bf16)
                ds_ref[:last, part] = grad_scores
                dqt_ref[second * 64 : second * 64 + 64, part] = dot_nn(
                    key_t[second * 64 : second * 64 + 64, :last], grad_scores
                )
            for start in range(0, keys, TILE):
                rows = slice(start, start + TILE)
                begin = start if causal else 0
                d_value = dot_nn(p_ref[rows, begin:], grad[begin:]).astype(bf16)
                d_key = dot_nn(ds_ref[rows, begin:], query[begin:]).astype(bf16)
                if second:
                    d_value = jnp.where(first_half, dqkv_ref[2, rows, lanes], d_value)
                    d_key = jnp.where(first_half, dqkv_ref[1, rows, lanes], d_key)
                dqkv_ref[2, rows, lanes] = d_value
                dqkv_ref[1, rows, lanes] = d_key
            if ds_out is not None:
                ds_out[head] = ds_ref[...]
        dqkv_ref[0, :, lanes] = dqt_ref[...].T.astype(bf16)
        return carry

    if causal:
        p_ref[...] = jnp.zeros_like(p_ref)
        ds_ref[...] = jnp.zeros_like(ds_ref)
    lax.fori_loop(0, qkv_ref.shape[2] // 128, pair, 0)


def head_sums(grad, mixed, dsum_ref):
    heads = dsum_ref.shape[0]
    product = grad.astype(f32) * mixed.astype(f32)
    width = product.shape[1]
    pick = (
        lax.broadcasted_iota(jnp.int32, (16, width), 1) // (width // heads)
        == lax.broadcasted_iota(jnp.int32, (16, width), 0)
    ).astype(f32)
    sums = lax.dot_general(
        pick, product, (((1,), (1,)), ((), ())),
        preferred_element_type=f32, precision=lax.Precision.HIGHEST,
    )
    for head in range(heads):
        dsum_ref[head] = sums[head : head + 1]


def square_kernel(*refs):
    row = 0
    for ref in refs[:-1]:
        parts = [ref[i] for i in range(ref.shape[0])] if len(ref.shape) == 3 else [ref[...]]
        for part in parts:
            total = jnp.sum(jnp.sum(part * part, axis=1, keepdims=True), axis=0, keepdims=True)
            refs[-1][row : row + 1, :] = jnp.broadcast_to(total, (1, 128))
            row += 1
    refs[-1][row:, :] = jnp.zeros((refs[-1].shape[0] - row, 128), f32)


def tally_kernel(gain1, gain2, gain3, first, second, fin, fout, table, squares, out_ref):
    at = 0
    rows = [ref[...] for ref in (gain1, gain2, gain3)]
    rows += [ref[i] for ref in (first, second, fin, fout) for i in range(ref.shape[0])]
    for row in rows:
        for start in range(0, row.shape[1], 128):
            out_ref[at : at + 1, :] = row[:, start : start + 128]
            at += 1
    for ref in (table, squares):
        out_ref[at : at + ref.shape[0], :] = ref[...]
        at += ref.shape[0]
    out_ref[at:, :] = jnp.zeros((out_ref.shape[0] - at, 128), f32)


def update_kernel(tally, first, second, fin, fout, first_rows, second_rows, fin_rows, fout_rows,
                  attn_in, attn_out, ff_in, ff_out, table, g_in, g_out, new_in, new_out, new_fin,
                  new_fout, gains, in_cols, out_cols, fin_cols, fout_cols, g_table, new_table,
                  *, buckets):
    at = 0

    def row(width):
        nonlocal at
        parts = [tally[at + i : at + i + 1, :] for i in range(width // 128)]
        at += width // 128
        return jnp.concatenate(parts, axis=1)

    width, ff_width = attn_in.shape[2], ff_in.shape[2]
    for i in range(3):
        gains[i : i + 1, :] = row(width)
    cols = [row(width) for _ in range(8)]
    cols += [row(ff_width), row(ff_width), row(width)]
    heads = table.shape[0]
    grad_t = tally[at : at + heads, :][:, :buckets]
    squares = at + heads
    sizes = [width * width] * 8 + [width * ff_width] * 3

    def step(grad, weight, rows, col, square, size):
        overall = jnp.sum(col, axis=1, keepdims=True)
        rms = jnp.sqrt(tally[squares + square : squares + square + 1, 0:1] / size + 1e-06)
        return weight - 0.3 * rms * grad * lax.rsqrt(rows * col / overall)

    places = [(first, first_rows, i, col) for i, col in enumerate(cols[:3])]
    places += [(second, second_rows, i, cols[3 + i]) for i in (1, 2, 3)]
    for i, (grad, rows, j, col) in enumerate(places):
        g_in[i] = grad[j]
        in_cols[i : i + 1, :] = col
        new_in[i] = step(grad[j], attn_in[i], rows[j], col, i, sizes[0])
    for i, j in ((0, 0), (1, 4)):
        col = cols[3 + j]
        g_out[i] = second[j]
        out_cols[i : i + 1, :] = col
        new_out[i] = step(second[j], attn_out[i], second_rows[j], col, 6 + i, sizes[0])
    for i in range(2):
        fin_cols[i : i + 1, :] = cols[8 + i]
        new_fin[i] = step(fin[i], ff_in[i], fin_rows[i], cols[8 + i], 8 + i, sizes[8])
    fout_cols[...] = cols[10]
    new_fout[...] = step(fout[0], ff_out[...], fout_rows[0], cols[10], 10, sizes[8])
    weight = table[:, :buckets]
    square = grad_t * grad_t + 1e-30
    by_bucket = jnp.sum(square, axis=0, keepdims=True)
    by_head = jnp.sum(square, axis=1, keepdims=True)
    overall = jnp.sum(by_head, axis=0, keepdims=True)
    mean = jnp.sum(jnp.sum(weight * weight, axis=1, keepdims=True), axis=0, keepdims=True)
    rms = jnp.sqrt(mean / (heads * buckets) + 1e-06)
    new_t = weight - 0.3 * rms * grad_t * lax.rsqrt(by_bucket * by_head / overall)
    g_table[...] = grad_t.T
    new_table[...] = new_t.T


def fold_rows(core, turned, turned_ref, out_ref, fold):
    if not fold:
        out_ref[...] = turned
        return
    turned_ref[...] = turned
    total = turned.shape[0]
    size = total // 8
    for group in range(4):
        for place, which in ((0, core), (1, 1 - core)):
            begin = pl.multiple_of(group * 2 * size + which * size, 16)
            to = place * (total // 2) + group * size
            out_ref[to : to + size, :] = turned_ref[pl.ds(begin, size), :]


def weight_grad(left_ref, right_ref, keep_ref, send_ref, index):
    half = left_ref.shape[0] // 2
    for start, size in tiles_of(right_ref.shape[1]):
        part = slice(start, start + size)
        right = right_ref[:, part]
        keep_ref[index, :, part] = dot_nn(left_ref[:half], right).astype(bf16)
        send_ref[index, :, part] = dot_nn(left_ref[half:], right).astype(bf16)


def start_weights(place, pieces, target_ref, sems, only=None):
    if len(pieces) == 2:
        size = pieces[0].shape[0] // 4
        pieces = [piece.at[pl.ds(d * size, size)] for d in range(4) for piece in pieces]
    rows = target_ref.shape[1] // len(pieces)
    copies = []
    for d, piece in enumerate(pieces):
        begin = pl.multiple_of((place ^ d) * rows, rows) if len(pieces) > 1 else 0
        source = piece if only is None else piece.at[only]
        copies.append(
            pltpu.make_async_copy(source, target_ref.at[:, pl.ds(begin, rows), :], sems.at[d])
        )
        copies[-1].start()
    return copies


def join_rows(place, pieces, target_ref):
    rows = pieces[0].shape[0]
    for d, piece in enumerate(pieces):
        target_ref[pl.ds(pl.multiple_of((place ^ d) * rows, 16), rows), :] = piece[...]


def join_blocks(place, pieces, target_ref):
    blocks = target_ref.shape[1] // TILE
    rows = target_ref.shape[0] // len(pieces)
    for d, piece in enumerate(pieces):
        to = pl.ds(pl.multiple_of((place ^ d) * rows, 16), rows)
        for j in range(blocks):
            target_ref[to, j * TILE : (j + 1) * TILE] = piece[j * rows : (j + 1) * rows, :]


def pack_kernel(at_ref, x_ref, m_ref, c_ref, seg_t_ref, seg_m_ref, *outs, narrow):
    local, width = x_ref.shape[1:]
    for d in range(narrow):
        first, memory, cot = outs[d], outs[narrow + d], outs[2 * narrow + d]
        row = at_ref[2] ^ d
        memory[...] = m_ref[row]
        cot[...] = c_ref[row]
        begin = 0
        for j in range(width // TILE):
            first[begin : begin + local, :] = x_ref[row, :, j * TILE : (j + 1) * TILE]
            begin += local
        for i, ref in enumerate((seg_t_ref, seg_m_ref)):
            seg = jnp.broadcast_to(ref[pl.ds(row, 1), :].astype(f32), (16, local))
            first[begin : begin + 16, i * local : (i + 1) * local] = seg.astype(bf16)


def split_rows(place, source_ref, pieces):
    rows = pieces[0].shape[0]
    for d, piece in enumerate(pieces):
        piece[...] = source_ref[pl.ds(pl.multiple_of((place ^ d) * rows, 16), rows), :].astype(
            piece.dtype
        )


def first_kernel(at_ref, *refs, pieces, narrow, chunk, bucket_count):
    x_refs, refs = refs[:narrow], refs[narrow:]
    w_refs, refs = refs[:pieces], refs[pieces:]
    near_ref = None
    if pieces == 1:
        near_ref, refs = refs[0], refs[1:]
    (allowed_ref, table_ref, w_ref, extra_ref, g_ref, x_ref, h_ref, qkv_ref, o_ref, peak_ref,
     inv_ref, ot_ref, sems) = refs
    copies = start_weights(at_ref[3], w_refs, w_ref, sems)
    join_blocks(at_ref[2], x_refs, x_ref)
    width = x_ref.shape[1]
    pick = (
        lax.broadcasted_iota(jnp.int32, (8, width), 1) % chunk
        == lax.broadcasted_iota(jnp.int32, (8, width), 0)
    ).astype(bf16)
    unit, _ = unit_of(x_ref[...].astype(f32))
    for copy in copies:
        copy.wait()
    gains = dot_nn(pick, w_ref[3])
    g_ref[...] = gains
    if near_ref is None:
        tokens = extra_ref.shape[0]
        held = w_ref[3, :, :tokens].astype(f32)
        groups = width // (narrow * chunk)
        share = tokens // (narrow * groups)
        near = jnp.concatenate(
            [
                held[(w * narrow + n + 1) * chunk - share : (w * narrow + n + 1) * chunk]
                for n in range(narrow)
                for w in range(groups)
            ],
            axis=0,
        ).T
    else:
        near = near_ref[...].astype(f32)
    extra_ref[...] = jnp.where(
        allowed_ref[...] > 0.0, near, float(bucket_count)
    ).astype(jnp.int32)
    h_ref[...] = (unit * gains[0:1]).astype(bf16)
    for i in range(3):
        def store(start, size, product, i=i):
            qkv_ref[i, :, start : start + size] = product.astype(bf16)

        project(h_ref[...], w_ref, i, store)
    attend(qkv_ref, extra_ref, table_ref, o_ref, peak_ref, inv_ref, ot_ref)


def second_kernel(at_ref, *refs, pieces, narrow):
    m_refs, refs = refs[:narrow], refs[narrow:]
    w_refs, refs = refs[:pieces], refs[pieces:]
    (x_ref, o1_ref, extra_ref, g_ref, w_ref, m_ref, x1_ref, h_ref, qkv_ref, o_ref, x2_ref, h3_ref,
     peak_ref, inv_ref, ot_ref, sems) = refs
    copies = start_weights(at_ref[3], w_refs, w_ref, sems)
    join_rows(at_ref[2], m_refs, m_ref)
    for copy in copies:
        copy.wait()

    def store_x1(start, size, product):
        part = slice(start, start + size)
        x1_ref[:, part] = x_ref[:, part].astype(f32) + product

    project(o1_ref[...], w_ref, 0, store_x1)
    unit, _ = unit_of(x1_ref[...])
    h_ref[...] = (unit * g_ref[1:2, :]).astype(bf16)
    for i in range(3):
        def store(start, size, product, i=i):
            qkv_ref[i, :, start : start + size] = product.astype(bf16)

        project(m_ref[...] if i else h_ref[...], w_ref, i + 1, store)
    attend(qkv_ref, extra_ref, None, o_ref, peak_ref, inv_ref, ot_ref)

    def store_x2(start, size, product):
        part = slice(start, start + size)
        x2_ref[:, part] = x1_ref[:, part] + product

    project(o_ref[...], w_ref, 4, store_x2)
    unit, _ = unit_of(x2_ref[...])
    h3_ref[...] = (unit * g_ref[2:3, :]).astype(bf16)


def prepare_kernel(at_ref, *refs, narrow, skip):
    in_refs, (allowed_ref, mask_ref, seg_ref) = refs[:narrow], refs[narrow:]
    tokens = mask_ref.shape[0]
    local = tokens // narrow
    for d, ref in enumerate(in_refs):
        lanes = pl.ds(pl.multiple_of((at_ref[2] ^ d) * local, 128), local)
        tail = ref[skip : skip + 16, :].astype(f32)
        seg_ref[0:8, lanes] = tail[:8, :local]
        seg_ref[8:16, lanes] = tail[:8, local : 2 * local]
    seg = seg_ref[...]
    seg_t = seg.T
    key = lax.broadcasted_iota(jnp.int32, (tokens, tokens), 0)
    query = lax.broadcasted_iota(jnp.int32, (tokens, tokens), 1)
    allowed = (key <= query) & (seg_t[:, 0:1] == seg[0:1, :])
    allowed_ref[...] = jnp.where(allowed, 1.0, 0.0)
    mask_ref[...] = jnp.where(seg_t[:, 8:9] == seg[0:1, :], 0.0, NEG)


def order_kernel(at_ref, *refs, outs):
    pieces, out_refs = refs[:-outs], refs[-outs:]
    for d, piece in enumerate(pieces):
        if piece.ndim == 2:
            out_refs[0][at_ref[2] ^ d] = piece[...]
            continue
        begin = 0
        for out_ref in out_refs:
            size = out_ref.shape[0]
            out_ref[:, at_ref[2] ^ d] = piece[begin : begin + size]
            begin += size


def read_part(refs, group):
    if len(refs) == 1:
        count, rows, cols = refs[0].shape
        rows //= 4
        part = pl.ds(pl.multiple_of(group * rows, 16), rows)
        return refs[0][:, part, :].astype(f32).reshape(count * rows, cols)
    fin, fout = refs
    rows, rows_out = fin.shape[1] // 4, fout.shape[1] // 4
    part = pl.ds(pl.multiple_of(group * rows, 16), rows)
    part_out = pl.ds(pl.multiple_of(group * rows_out, 16), rows_out)
    pieces = [
        fin[i, part, at : at + TILE].astype(f32)
        for i in range(fin.shape[0])
        for at in range(0, fin.shape[2], TILE)
    ]
    pieces += [
        fout[0, part_out, at : at + TILE].astype(f32) for at in range(0, fout.shape[2], TILE)
    ]
    return jnp.concatenate(pieces, axis=0)


def spread_kernel(at_ref, *refs, count):
    keeps, recvs = refs[:count], refs[count : 2 * count]
    own_ref, kept_x, kept_y, to_x, to_y = refs[2 * count :]
    half = own_ref.shape[0] // 2
    for d in range(4):
        total = read_part(keeps, at_ref[1] ^ d) + read_part(recvs, at_ref[1] ^ d)
        if d == 0:
            own_ref[...] = total
        elif d == 1:
            to_x[0] = total[:half].astype(bf16)
            kept_x[...] = total[half:]
        elif d == 2:
            to_y[0] = total[half:].astype(bf16)
            kept_y[...] = total[:half]
        else:
            to_x[1] = total[:half].astype(bf16)
            to_y[1] = total[half:].astype(bf16)


def middle_kernel(own_ref, kept_x, kept_y, from_x, from_y, sum_ref, to_x, to_y):
    half = own_ref.shape[0] // 2
    sum_ref[:half, :] = own_ref[:half, :] + from_x[0].astype(f32)
    sum_ref[half:, :] = own_ref[half:, :] + from_y[0].astype(f32)
    to_y[...] = (kept_y[...] + from_x[1].astype(f32)).astype(bf16)
    to_x[...] = (kept_x[...] + from_y[1].astype(f32)).astype(bf16)


def narrow_kernel(at_ref, own_ref, from_x, from_y, *refs, narrow, spots):
    riders, outs, sum_ref = refs[: -narrow - 1], refs[-narrow - 1 : -1], refs[-1]
    half = own_ref.shape[0] // 2
    sum_ref[:half, :] = own_ref[:half, :] + from_y[...].astype(f32)
    sum_ref[half:, :] = own_ref[half:, :] + from_x[...].astype(f32)
    for d, out_ref in enumerate(outs):
        place = at_ref[2] ^ d
        share = jnp.concatenate(
            [
                sum_ref[pl.ds(start + pl.multiple_of(place * rows, 8), rows), :]
                for start, rows in spots
            ],
            axis=0,
        ).astype(out_ref.dtype)
        ahead = out_ref.shape[0] - share.shape[0]
        if ahead:
            rider, cols = riders[d - 1], out_ref.shape[1]
            rows = rider.shape[0]
            for j in range(rider.shape[1] // cols):
                out_ref[j * rows : (j + 1) * rows, :] = rider[:, j * cols : (j + 1) * cols]
        out_ref[ahead:, :] = share


def join_kernel(at_ref, *refs):
    own, pieces, out_ref = refs[0], refs[1:-1], refs[-1]
    out_ref[at_ref[2]] = own[...]
    rows, width = own.shape
    for d, piece in enumerate(pieces):
        cols = piece.shape[1]
        for j in range(width // cols):
            out_ref[at_ref[2] ^ (d + 1), :, j * cols : (j + 1) * cols] = piece[
                j * rows : (j + 1) * rows, :
            ]


def total_kernel(*refs, narrow):
    total = refs[0][...]
    for ref in refs[1:narrow]:
        total = total + ref[ref.shape[0] - total.shape[0] :, :].astype(f32)
    outs = refs[narrow:]
    at = 0
    for total_ref, rows_ref, cols_ref in zip(*(outs[i::3] for i in range(3))):
        count, rows, cols = total_ref.shape
        block = total.shape[1]
        if cols == block:
            total_ref[...] = total[at : at + count * rows].reshape(count, rows, cols)
            at += count * rows
        else:
            for i in range(count):
                for j in range(cols // block):
                    total_ref[i, :, j * block : (j + 1) * block] = total[at : at + rows]
                    at += rows
        squares = total_ref[...]
        squares = squares * squares + 1e-30
        rows_ref[...] = jnp.sum(squares, axis=-1, keepdims=True)
        cols_ref[...] = jnp.sum(squares, axis=1, keepdims=True)


def ffn_kernel(at_ref, *refs, fold, narrow, pieces, first_out):
    c_refs, refs = refs[:narrow], refs[narrow:]
    fin_refs, refs = refs[:pieces], refs[pieces:]
    fout_refs, refs = refs[:pieces], refs[pieces:]
    (x2_ref, h_ref, g_ref), refs = refs[:3], refs[3:]
    out_refs, refs = refs[:narrow], refs[narrow:]
    (dx_ref, dg_ref, kin_ref, sin_ref, kout_ref, sout_ref, acc_ref, dh_ref, turned_ref, ht_ref,
     gout_ref, c_ref, fin_ref, fout_ref, fin_sems, fout_sems) = refs
    step, steps = pl.program_id(0), pl.num_programs(0)
    core = at_ref[0]

    @pl.when(step == 0)
    def _():
        copies = start_weights(at_ref[3], fin_refs, fin_ref, fin_sems, pl.ds(0, fin_ref.shape[0]))
        copies += start_weights(
            at_ref[3], fout_refs, fout_ref, fout_sems, pl.ds(first_out, fout_ref.shape[0])
        )
        join_rows(at_ref[2], c_refs, c_ref)
        acc_ref[...] = x2_ref[...]
        dh_ref[...] = jnp.zeros_like(dh_ref)
        fold_rows(core, h_ref[...].T, turned_ref, ht_ref, fold)
        for copy in copies:
            copy.wait()

    hidden_in, cot = h_ref[...], c_ref[...]
    size = fin_ref.shape[2]
    blocks = gout_ref.shape[0] // size
    for block in range(blocks):
        part = slice(block * size, (block + 1) * size)
        at_gate = step * blocks + block
        at_up = fin_ref.shape[0] // 2 + at_gate
        gate = dot_nn(hidden_in, fin_ref[at_gate])
        up = dot_nn(hidden_in, fin_ref[at_up])
        square = gate * gate
        bent = jnp.tanh(0.7978845608028654 * (gate + 0.044715 * square * gate))
        plus = 0.5 * (1.0 + bent)
        act = gate * plus
        slope = plus + 0.5 * gate * (1.0 - bent * bent) * (
            0.7978845608028654 + (3 * 0.044715 * 0.7978845608028654) * square
        )
        hidden = (act * up).astype(bf16)
        down_rows = pl.ds(pl.multiple_of(at_gate * size, size), size)
        down = jnp.concatenate(
            [fout_ref[i, down_rows, :] for i in range(fout_ref.shape[0])], axis=1
        )
        acc_ref[...] += dot_nn(hidden, down)
        grad = dot_nt(cot, down)
        d_gate = (grad * up * slope).astype(bf16)
        d_up = (grad * act).astype(bf16)
        dh_ref[...] += dot_nt(d_gate, fin_ref[at_gate]) + dot_nt(d_up, fin_ref[at_up])
        half = ht_ref.shape[0] // 2
        for index, right in ((0, d_gate), (1, d_up)):
            product = dot_nn(ht_ref[...], right).astype(bf16)
            kin_ref[index, :, part] = product[:half]
            sin_ref[index, :, part] = product[half:]
        gout_ref[part, :] = dot_nn(hidden.T, cot).astype(bf16)
    rows = gout_ref.shape[0] // 2
    kept = pl.multiple_of(core * rows, 16) if fold else 0
    sent = pl.multiple_of((1 - core) * rows, 16) if fold else rows
    kout_ref[...] = gout_ref[pl.ds(kept, rows), :]
    sout_ref[...] = gout_ref[pl.ds(sent, rows), :]

    @pl.when(step == steps - 1)
    def _():
        split_rows(at_ref[2], acc_ref, out_refs)
        back, d_gain = norm_back(dh_ref[...], x2_ref[...], g_ref[2:3, :])
        dx_ref[...] = cot.astype(f32) + back
        dg_ref[...] = d_gain


def attend_back_kernel(at_ref, *refs, pieces, which, causal):
    w_refs, refs = refs[:pieces], refs[pieces:]
    table_ref = None
    if causal:
        table_ref, refs = refs[0], refs[1:]
    dx_ref, o_ref, qkv_ref, extra_ref, peak_ref, inv_ref, dqkv_ref = refs[:7]
    ds_out, refs = (refs[7], refs[8:]) if causal else (None, refs[7:])
    do_ref, dsum_ref, p_ref, ds_ref, dqt_ref, w_ref, sems = refs
    copies = start_weights(at_ref[3], w_refs, w_ref, sems, pl.ds(which, 1))
    branch = dx_ref[...].astype(bf16)
    for copy in copies:
        copy.wait()
    for start, size in tiles_of(o_ref.shape[1]):
        do_ref[:, start : start + size] = dot_nt(
            branch, w_ref[0, start : start + size, :]
        ).astype(bf16)
    head_sums(do_ref[...], o_ref[...], dsum_ref)
    attend_back(qkv_ref, extra_ref, table_ref, do_ref, dsum_ref, peak_ref, inv_ref, dqkv_ref,
                p_ref, ds_ref, dqt_ref, ds_out)


def second_back_kernel(at_ref, *refs, pieces, narrow, fold):
    w_refs, refs = refs[:pieces], refs[pieces:]
    (dqkv_ref, dx2_ref, o_ref, h_ref, m_ref, x1_ref, o1_ref, g_ref), refs = refs[:8], refs[8:]
    gm_refs, refs = refs[:narrow], refs[narrow:]
    (dx1_ref, dg_ref, keep_ref, send_ref, turned_ref, left_ref, gm_ref, w_ref, sems) = refs
    core = at_ref[0]
    copies = start_weights(at_ref[3], w_refs, w_ref, sems, pl.ds(1, 3))
    gm_ref[...] = dx2_ref[...].astype(bf16)
    fold_rows(core, o_ref[...].T, turned_ref, left_ref, fold)
    for copy in copies:
        copy.wait()
    weight_grad(left_ref, gm_ref, keep_ref, send_ref, 4)
    fold_rows(core, h_ref[...].T, turned_ref, left_ref, fold)
    weight_grad(left_ref, dqkv_ref.at[0], keep_ref, send_ref, 1)
    fold_rows(core, m_ref[...].T, turned_ref, left_ref, fold)
    for i in (1, 2):
        weight_grad(left_ref, dqkv_ref.at[i], keep_ref, send_ref, i + 1)
    for start, size in tiles_of(o_ref.shape[1]):
        rows = slice(start, start + size)
        gm_ref[:, rows] = (
            dot_nt(dqkv_ref[1], w_ref[1, rows, :]) + dot_nt(dqkv_ref[2], w_ref[2, rows, :])
        ).astype(bf16)
        dx1_ref[:, rows] = dot_nt(dqkv_ref[0], w_ref[0, rows, :])
    split_rows(at_ref[2], gm_ref, gm_refs)
    back, d_gain = norm_back(dx1_ref[...], x1_ref[...], g_ref[1:2, :])
    d_x1 = dx2_ref[...] + back
    dx1_ref[...] = d_x1
    dg_ref[...] = d_gain
    gm_ref[...] = d_x1.astype(bf16)
    fold_rows(core, o1_ref[...].T, turned_ref, left_ref, fold)
    weight_grad(left_ref, gm_ref, keep_ref, send_ref, 0)


def first_back_kernel(at_ref, *refs, pieces, narrow, fold):
    w_refs, refs = refs[:pieces], refs[pieces:]
    (dqkv_ref, h_ref, dx1_ref, x_ref, g_ref), refs = refs[:5], refs[5:]
    gx_refs, refs = refs[:narrow], refs[narrow:]
    dg_ref, keep_ref, send_ref, turned_ref, left_ref, dh_ref, w_ref, sems = refs
    copies = start_weights(at_ref[3], w_refs, w_ref, sems, pl.ds(0, 3))
    fold_rows(at_ref[0], h_ref[...].T, turned_ref, left_ref, fold)
    for copy in copies:
        copy.wait()
    for i in range(3):
        weight_grad(left_ref, dqkv_ref.at[i], keep_ref, send_ref, i)
    for start, size in tiles_of(h_ref.shape[1]):
        rows = slice(start, start + size)
        dh_ref[:, rows] = (
            dot_nt(dqkv_ref[0], w_ref[0, rows, :])
            + dot_nt(dqkv_ref[1], w_ref[1, rows, :])
            + dot_nt(dqkv_ref[2], w_ref[2, rows, :])
        )
    back, d_gain = norm_back(dh_ref[...], x_ref[...].astype(f32), g_ref[0:1, :])
    dh_ref[...] = dx1_ref[...] + back
    split_rows(at_ref[2], dh_ref, gx_refs)
    dg_ref[...] = d_gain


def table_kernel(ds_ref, index_ref, out_ref, acc_ref, *, buckets):
    heads, keys, queries = ds_ref.shape
    acc_ref[...] = jnp.zeros_like(acc_ref)

    def group(at, carry):
        rows = pl.ds(pl.multiple_of(at * 16, 16), 16)
        index = index_ref[rows, :]
        grads = ds_ref[:, rows, :].reshape(heads * 16, queries)
        hot = jnp.concatenate(
            [(index == b).astype(f32).astype(bf16) for b in range(buckets)], axis=0
        )
        acc_ref[...] += dot_nt(grads, hot)
        return carry

    lax.fori_loop(0, keys // 16, group, 0)
    shape = acc_ref.shape
    same = (
        lax.broadcasted_iota(jnp.int32, shape, 0) % 16
        == lax.broadcasted_iota(jnp.int32, shape, 1) % 16
    )
    kept = jnp.where(same, acc_ref[...], 0.0).reshape(heads, 16, shape[1]).sum(axis=1)
    gather = (
        lax.broadcasted_iota(jnp.int32, (shape[1], 128), 0) // 16
        == lax.broadcasted_iota(jnp.int32, (shape[1], 128), 1)
    ).astype(f32)
    out_ref[...] = lax.dot_general(
        kept, gather, (((1,), (0,)), ((), ())),
        preferred_element_type=f32, precision=lax.Precision.HIGHEST,
    )


def cost_of(us):
    return pl.CostEstimate(flops=int(us * 1.15e9), bytes_accessed=MIB, transcendentals=0)


def room_for(arrays, scratch):
    size = sum(v.size * v.dtype.itemsize for v in arrays)
    for ref in scratch:
        shape = getattr(ref, "shape", ())
        if ref.memory_space == pltpu.VMEM:
            rows = -(-shape[-2] // 8) * 8
            size += math.prod(shape[:-2]) * rows * shape[-1] * jnp.dtype(ref.dtype).itemsize
    return (size // MIB + 8) * MIB


def call(kernel, outs, scratch, *args, scalars=1, loose=(), us=2, name=None):
    spaces = [
        pltpu.SMEM if i < scalars else pl.ANY if i in loose else pltpu.VMEM
        for i in range(len(args))
    ]
    return pl.pallas_call(
        kernel,
        out_shape=outs,
        in_specs=[pl.BlockSpec(memory_space=space) for space in spaces],
        out_specs=[pl.BlockSpec(memory_space=pltpu.VMEM)] * len(outs),
        scratch_shapes=scratch,
        compiler_params=pltpu.CompilerParams(
            vmem_limit_bytes=room_for(
                [v for v, space in zip(args, spaces) if space == pltpu.VMEM] + list(outs), scratch
            )
        ),
        cost_estimate=cost_of(us),
        name=name,
    )(*args)


def shape_of(shape, dtype):
    return jax.ShapeDtypeStruct(tuple(shape), dtype)


def permuted(value, wide_bits, narrow_bits):
    wide, narrow = lax.axis_size("wide"), lax.axis_size("narrow")
    pairs = [
        (w * narrow + n, (w ^ wide_bits) * narrow + (n ^ narrow_bits))
        for w in range(wide)
        for n in range(narrow)
    ]
    return lax.ppermute(value, BOTH, pairs)


def after(value, *done):
    return lax.optimization_barrier((value, *done))[0]


def ordered(at, pieces, shares=None):
    first = pieces[0]
    if first.ndim == 2:
        shapes = [(len(pieces),) + first.shape]
    else:
        shapes = [(k, len(pieces)) + first.shape[1:] for k in shares]
    outs = [shape_of(shape, first.dtype) for shape in shapes]
    return call(
        functools.partial(order_kernel, outs=len(outs)), outs, [], at, *pieces, us=1, name="order"
    )


def local_stats(gradient):
    squares = gradient * gradient + 1e-30
    return (jnp.sum(squares, axis=-1, keepdims=True), jnp.sum(squares, axis=-2, keepdims=True))


class Scatter:
    def __init__(self, at, pairs, fast, narrow):
        self.at, self.fast, self.narrow, self.pairs = at, fast, narrow, pairs
        self.done = pairs[0][0]
        if not fast:
            return
        keeps = [keep.reshape(-1, keep.shape[1], keep.shape[2]) for keep, _ in pairs]
        sends = [send for _, send in pairs]
        if len(pairs) == 2:
            keeps[1] = keeps[1].reshape(1, -1, keeps[1].shape[2])
            sends[1] = sends[1].reshape(keeps[1].shape)
        self.shapes = [(k.shape[0], k.shape[1] // 4, k.shape[2]) for k in keeps]
        size = sum(k.size for k in keeps) // 4
        cols = TILE if len(pairs) == 2 else keeps[0].shape[2]
        self.rows, self.cols = size // cols, cols
        half = (self.rows // 2, cols)
        recvs = [permuted(send, 1, 0) for send in sends]
        self.own, self.kept_x, self.kept_y, to_x, to_y = call(
            functools.partial(spread_kernel, count=len(pairs)),
            [shape_of((self.rows, cols), f32), shape_of(half, f32), shape_of(half, f32),
             shape_of((2,) + half, bf16), shape_of((2,) + half, bf16)],
            [], at, *keeps, *recvs, us=3, name="spread",
        )
        self.out = (to_x, to_y)
        self.done = self.own

    def middle(self, *done):
        if not self.fast:
            return
        self.own = after(self.own, *done)
        half = (self.rows // 2, self.cols)
        from_x, from_y = permuted(self.out[0], 2, 0), permuted(self.out[1], 4, 0)
        self.own, to_x, to_y = call(
            middle_kernel,
            [shape_of((self.rows, self.cols), f32), shape_of(half, bf16), shape_of(half, bf16)],
            [], self.own, self.kept_x, self.kept_y, from_x, from_y, scalars=0, name="middle",
        )
        self.out = (to_x, to_y)
        self.done = self.own

    def narrowed(self, riders, *done):
        self.riders = riders
        if not self.fast:
            return
        self.own = after(self.own, *done)
        from_x, from_y = permuted(self.out[0], 2, 0), permuted(self.out[1], 4, 0)
        if len(self.shapes) == 2:
            (k, rows, cols), (_, rows_out, cols_out) = self.shapes
            sizes = [rows] * (k * cols // TILE) + [rows_out] * (cols_out // TILE)
        else:
            sizes = [self.shapes[0][1]] * self.shapes[0][0]
        spots, begin = [], 0
        for size in sizes:
            spots.append((begin, size // self.narrow))
            begin += size
        share = self.rows // self.narrow
        ahead = riders[0].size // self.cols if riders else 0
        self.out = call(
            functools.partial(narrow_kernel, narrow=self.narrow, spots=spots),
            [
                shape_of((share + ahead, self.cols) if d else (share, self.cols), bf16 if d else f32)
                for d in range(self.narrow)
            ],
            [pltpu.VMEM((self.rows, self.cols), f32)], self.at, self.own, from_x, from_y,
            *riders[1:], name="narrow",
        )
        self.done = self.out[0]

    def total(self, *done):
        if not self.fast:
            results = []
            for keep, send in self.pairs:
                whole = jnp.concatenate([keep, send], axis=1)
                if keep.shape[0] == 4:
                    whole = whole.reshape(1, -1, whole.shape[2])
                total = lax.psum_scatter(whole, BOTH, scatter_dimension=1, tiled=True).astype(f32)
                results.append((total, *local_stats(total)))
            return results
        parts = [permuted(v, 0, d) if d else v for d, v in enumerate(self.out)]
        parts[0] = after(parts[0], *done)
        if self.riders:
            rider = self.riders[0]
            (self.ridden,) = call(
                join_kernel, [shape_of((self.narrow,) + rider.shape, bf16)], [], self.at,
                after(rider, *done), *parts[1:], name="join",
            )
        outs = []
        for k, rows, cols in self.shapes:
            rows //= self.narrow
            outs += [
                shape_of((k, rows, cols), f32), shape_of((k, rows, 1), f32),
                shape_of((k, 1, cols), f32),
            ]
        flat = call(
            functools.partial(total_kernel, narrow=self.narrow), outs, [], *parts, scalars=0,
            name="total",
        )
        return [
            tuple(flat[3 * i : 3 * i + 3])
            for i in range(len(self.shapes))
        ]


def summed_all(flat, fast):
    if not fast:
        return lax.psum(flat, BOTH)
    flat = flat + permuted(flat, 1, 0)
    flat = (flat + permuted(flat, 2, 0)) + (permuted(flat, 4, 0) + permuted(flat, 6, 0))
    return (flat + permuted(flat, 0, 1)) + (permuted(flat, 0, 2) + permuted(flat, 0, 3))


def body(
    targets, memory, cotangent, target_segments, memory_segments, buckets,
    attn_in, attn_out, gains, ff_in, ff_out, bias_table,
):
    wide, narrow = lax.axis_size("wide"), lax.axis_size("narrow")
    at_wide, at_narrow = lax.axis_index("wide"), lax.axis_index("narrow")
    fast = wide == 8 and narrow == 4
    at = jnp.stack([at_wide % 2, at_wide // 2, at_narrow, at_wide]).astype(jnp.int32)
    width, ff_width = attn_in.shape[2], ff_in.shape[2]
    bucket_count, heads = bias_table.shape
    chunk = gains.shape[1]
    local_tokens = targets.shape[1]
    tokens = local_tokens * narrow
    assert targets.shape[0] == narrow

    def over_narrow(pieces):
        return [permuted(v, 0, d) if d else v for d, v in enumerate(pieces)]

    def to_owners(pieces, *done):
        pieces = over_narrow(pieces)
        return ordered(at, [after(pieces[0], *done)] + pieces[1:])[0]

    device = at_wide * narrow + at_narrow
    gain_rows = lax.dynamic_update_slice(
        jnp.zeros((chunk, width), bf16), gains.astype(bf16), (0, device * chunk)
    )
    if fast:
        share = local_tokens // wide
        held = lax.dynamic_slice_in_dim(buckets, at_wide * share, share, 0).astype(bf16)
        gain_rows = lax.dynamic_update_slice(gain_rows, held, (chunk - share, 0))
    first_local = jnp.concatenate([attn_in[:3].astype(bf16), gain_rows[None]])
    second_local = jnp.concatenate([attn_out[:1], attn_in[3:], attn_out[1:]]).astype(bf16)
    piece16 = shape_of((local_tokens, width), bf16)
    near_rows = local_tokens * width // TILE + 16
    packed = call(
        functools.partial(pack_kernel, narrow=narrow),
        [shape_of((near_rows, TILE), bf16)] * narrow
        + [piece16] * (2 * narrow),
        [], at, targets, memory, cotangent, target_segments, memory_segments,
        us=4, name="pack",
    )
    near, m_out, c_out = packed[:narrow], packed[narrow : 2 * narrow], packed[2 * narrow :]
    lanes = TILE
    fin_blocks = ff_in.astype(bf16).reshape(2, chunk, ff_width // lanes, lanes)
    fin_blocks = fin_blocks.transpose(0, 2, 1, 3).reshape(-1, chunk, lanes)
    out_rows_here = ff_out.shape[0]
    fout_blocks = ff_out.astype(bf16).reshape(out_rows_here, width // lanes, lanes)
    fout_blocks = fout_blocks.transpose(1, 0, 2).reshape(-1, chunk, lanes)
    fin_count, fout_count = fin_blocks.shape[0], fout_blocks.shape[0]
    ffn_local = jnp.concatenate([fin_blocks, fout_blocks])

    def regroup_out(stack, owners):
        stack = stack.reshape(fout_count, owners, chunk, lanes).transpose(1, 0, 2, 3)
        stack = stack.reshape(owners, width // lanes, out_rows_here, lanes)
        return stack.transpose(1, 0, 2, 3).reshape(width // lanes, -1, lanes)

    def over_plane(stack):
        from_x, from_y = permuted(stack, 2, 0), permuted(stack, 4, 0)
        half = stack.shape[0] // 2
        begin, end = from_x[:half], from_y[half:]
        return [stack, from_x, from_y, permuted(begin, 4, 0), permuted(end, 2, 0)]

    def with_other_core(plane, *done):
        own = jnp.concatenate([after(plane[0], *done)] + plane[1:])
        return [own, permuted(own, 1, 0)]

    if fast:
        first_near = over_narrow([first_local] * narrow)
        first_near[0] = after(first_near[0], near[0])
        (stack,) = ordered(at, first_near, (4,))
        near = [near[0]] + [after(v, stack) for v in near[1:]]
        stack = stack.reshape(4, -1, width)
        plane_first = [stack] + [permuted(stack, 2 * d, 0) for d in (1, 2, 3)]
        held_out = []
    else:
        w_first = [lax.all_gather(first_local, BOTH, axis=1, tiled=True)]
        w_second = [lax.all_gather(second_local, BOTH, axis=1, tiled=True)]
        held_out = [lax.all_gather(buckets.astype(bf16), "narrow", axis=0, tiled=True).T]
    near = over_narrow(near)
    allowed, cross_mask = call(
        functools.partial(
            prepare_kernel, narrow=narrow, skip=local_tokens * width // TILE,
        ),
        [shape_of((tokens, tokens), f32), shape_of((tokens, tokens), f32)],
        [pltpu.VMEM((16, tokens), f32)],
        at, *near, us=2, name="prepare",
    )
    if fast:
        w_first = with_other_core(plane_first, allowed)
        ffn_near = over_narrow([after(ffn_local, allowed)] * narrow)
    table = jnp.concatenate(
        [bias_table.T, jnp.full((heads, 128 - bucket_count), NEG, f32)], axis=1
    )
    row16 = shape_of((tokens, width), bf16)
    row32 = shape_of((tokens, width), f32)
    three = shape_of((3, tokens, width), bf16)
    stat = shape_of((heads, 1, tokens), f32)
    gain_out = shape_of((1, width), f32)
    pair_t = pltpu.VMEM((128, tokens), f32)
    pieces = len(w_first)
    weights = lambda count: pltpu.VMEM((count, width, width), bf16)
    sems = pltpu.SemaphoreType.DMA((8,))
    stack_of = lambda count: shape_of((count, width, width), bf16)
    w_first, index, g, x, h1, qkv1, o1, peak1, inv1 = call(
        functools.partial(
            first_kernel, pieces=pieces, narrow=narrow, chunk=chunk, bucket_count=bucket_count
        ),
        [stack_of(4), shape_of((tokens, tokens), jnp.int32), shape_of((8, width), f32), row16,
         row16, three, row16, stat, stat],
        [pair_t, sems],
        at, *near, *w_first, *held_out, allowed, table,
        loose=range(1 + narrow, 1 + narrow + pieces), us=16, name="first",
    )
    if fast:
        ffn_near[0] = after(ffn_near[0], h1)
        (stack,) = ordered(at, ffn_near, (fin_count + fout_count,))
        second_near = over_narrow([after(second_local, stack)] * narrow)
        stack = stack.reshape(fin_count + fout_count, -1, lanes)
        stack_out = regroup_out(stack[fin_count:], narrow).reshape(fout_count, -1, lanes)
        stack = jnp.concatenate([stack[:fin_count], stack_out])
        plane_ffn = over_plane(stack)
        second_near[0] = after(second_near[0], plane_ffn[1], plane_ffn[2])
        (stack,) = ordered(at, second_near, (5,))
        m_out = [m_out[0]] + [after(v, *second_near[1:]) for v in m_out[1:]]
        plane_second = over_plane(stack.reshape(5, -1, width))
    m_pieces = over_narrow(m_out)
    if fast:
        w_second = with_other_core(plane_second, *m_pieces[1:])
        c_out = [c_out[0]] + [after(v, *m_pieces[1:]) for v in c_out[1:]]
    c_pieces = over_narrow(c_out)
    w_second, m, x1, h2, qkv2, o2, x2, h3, peak2, inv2 = call(
        functools.partial(second_kernel, pieces=pieces, narrow=narrow),
        [stack_of(5), row16, row32, row16, three, row16, row32, row16, stat, stat],
        [pair_t, sems],
        at, *m_pieces, *w_second, x, o1, cross_mask, g,
        loose=range(1 + narrow, 1 + narrow + pieces), us=21, name="second",
    )

    if fast:
        ffn_pieces = with_other_core(plane_ffn, x2, *c_pieces[1:])
        w_fin = ffn_pieces
        w_fout = [v.reshape(-1, narrow * out_rows_here, lanes) for v in ffn_pieces]
    else:
        every = lax.all_gather(ffn_local, BOTH, axis=1, tiled=True)
        w_fin, w_fout = [every], [regroup_out(every[fin_count:], wide * narrow)]
    steps = 4
    part = ff_width // steps
    half = width // 2
    whole = lambda shape: pl.BlockSpec(shape, lambda i: (0,) * len(shape))
    outs = pl.pallas_call(
        functools.partial(
            ffn_kernel, fold=fast, narrow=narrow, pieces=pieces,
            first_out=w_fout[0].shape[0] // 4 - width // lanes if fast else 0,
        ),
        grid=(steps,),
        in_specs=[pl.BlockSpec(memory_space=pltpu.SMEM)]
        + [whole((local_tokens, width))] * narrow
        + [pl.BlockSpec(memory_space=pl.ANY)] * (2 * pieces)
        + [whole((tokens, width)), whole((tokens, width)), whole((8, width))],
        out_specs=[whole((local_tokens, width))] * narrow
        + [
            whole((tokens, width)), whole((1, width)),
            pl.BlockSpec((2, half, part), lambda i: (0, 0, i)),
            pl.BlockSpec((2, half, part), lambda i: (0, 0, i)),
            pl.BlockSpec((None, part // 2, width), lambda i: (i, 0, 0)),
            pl.BlockSpec((None, part // 2, width), lambda i: (i, 0, 0)),
        ],
        out_shape=[piece16] * narrow
        + [
            row32, gain_out,
            shape_of((2, half, ff_width), bf16), shape_of((2, half, ff_width), bf16),
            shape_of((steps, part // 2, width), bf16), shape_of((steps, part // 2, width), bf16),
        ],
        scratch_shapes=[
            pltpu.VMEM((tokens, width), f32), pltpu.VMEM((tokens, width), f32),
            pltpu.VMEM((width, tokens), bf16), pltpu.VMEM((width, tokens), bf16),
            pltpu.VMEM((part, width), bf16), pltpu.VMEM((tokens, width), bf16),
            pltpu.VMEM((fin_count, width, lanes), bf16),
            pltpu.VMEM((width // lanes, ff_width, lanes), bf16), sems, sems,
        ],
        compiler_params=pltpu.CompilerParams(vmem_limit_bytes=40 * MIB),
        cost_estimate=cost_of(24),
        name="ffn",
    )(at, *c_pieces, *w_fin, *w_fout, x2, h3, g)
    out_pieces = outs[:narrow]
    dx2, gain3, keep_fin, send_fin, keep_fout, send_fout = outs[narrow:]
    ffn_sum = Scatter(at, [(keep_fin, send_fin), (keep_fout, send_fout)], fast, narrow)
    if fast:
        dx2 = after(dx2, ffn_sum.done)
    square = pltpu.VMEM((tokens, tokens), bf16)
    attend_scratch = [
        pltpu.VMEM((tokens, width), bf16), pltpu.VMEM((heads, 1, tokens), f32), square, square,
        pair_t, weights(1), sems,
    ]
    turned = pltpu.VMEM((width, tokens), bf16)
    grads = lambda count: shape_of((count, half, width), bf16)
    (dqkv2,) = call(
        functools.partial(attend_back_kernel, pieces=1, which=4, causal=False),
        [three], attend_scratch,
        at, w_second, dx2, o2, qkv2, cross_mask, peak2, inv2,
        loose=(1,), us=18, name="cross_back",
    )
    output = to_owners(out_pieces, dqkv2)
    ffn_sum.middle(dqkv2)
    if fast:
        dqkv2 = after(dqkv2, ffn_sum.done, output)
    outs = call(
        functools.partial(second_back_kernel, pieces=1, narrow=narrow, fold=fast),
        [piece16] * narrow + [row32, gain_out, grads(5), grads(5)],
        [turned, turned, pltpu.VMEM((tokens, width), bf16), weights(3), sems],
        at, w_second, dqkv2, dx2, o2, h2, m, x1, o1, g,
        loose=(1,), us=12, name="second_back",
    )
    gm_pieces = outs[:narrow]
    dx1, gain2, keep_second, send_second = outs[narrow:]
    ffn_sum.narrowed([], gain2)
    if fast:
        send_second = after(send_second, ffn_sum.done)
    second_sum = Scatter(at, [(keep_second, send_second)], fast, narrow)
    if fast:
        dx1 = after(dx1, second_sum.done, ffn_sum.done)
    dqkv1, ds = call(
        functools.partial(attend_back_kernel, pieces=1, which=0, causal=True),
        [three, shape_of((heads, tokens, tokens), bf16)], attend_scratch,
        at, w_second, table, dx1, o1, qkv1, index, peak1, inv1,
        loose=(1,), us=20, name="self_back",
    )
    (sum_fin, fin_rows, fin_part), (sum_fout, fout_rows, fout_part) = ffn_sum.total(dqkv1)
    second_sum.middle(dqkv1)
    if fast:
        dqkv1 = after(dqkv1, sum_fin, second_sum.done)
    outs = call(
        functools.partial(first_back_kernel, pieces=1, narrow=narrow, fold=fast),
        [piece16] * narrow + [gain_out, grads(3), grads(3)],
        [turned, turned, pltpu.VMEM((tokens, width), f32), weights(3), sems],
        at, w_first, dqkv1, h1, dx1, x, g,
        loose=(1,), us=9, name="first_back",
    )
    gx_pieces = outs[:narrow]
    gain1, keep_first, send_first = outs[narrow:]
    grad_memory = to_owners(gm_pieces, gain1)
    second_sum.narrowed(gx_pieces, gain1, grad_memory)
    (squares,) = call(
        square_kernel, [shape_of((16, 128), f32)], [],
        *(after(v, second_sum.done) for v in (attn_in, attn_out, ff_in, ff_out)), scalars=0,
        us=1, name="squares",
    )
    if fast:
        send_first = after(send_first, second_sum.done)
        keep_first = after(keep_first, squares)
    first_sum = Scatter(at, [(keep_first, send_first)], fast, narrow)
    if fast:
        ds = after(ds, first_sum.done, second_sum.done)
    (table_part,) = call(
        functools.partial(table_kernel, buckets=bucket_count),
        [shape_of((heads, 128), f32)],
        [pltpu.VMEM((heads * 16, bucket_count * 16), f32)], ds, index, scalars=0, us=11,
        name="table",
    )
    first_sum.middle(table_part)
    first_sum.narrowed([])
    ((sum_second, second_rows, second_part),) = second_sum.total(table_part)
    ((sum_first, first_rows, first_part),) = first_sum.total()
    grad_targets = second_sum.ridden if fast else to_owners(gx_pieces)
    parts = (gain1, gain2, gain3, first_part, second_part, fin_part, fout_part, table_part, squares)
    rows = sum(v.size for v in parts) // 128
    (tally,) = call(
        tally_kernel, [shape_of((-(-rows // 8) * 8, 128), f32)], [], *parts, scalars=0, us=1,
        name="tally",
    )
    tally = summed_all(tally, fast)
    (
        sum_in, sum_out, new_in, new_out, new_fin, new_fout, sum_gain, in_cols, out_cols, fin_cols,
        fout_cols, grad_table, new_table,
    ) = call(
        functools.partial(update_kernel, buckets=bucket_count),
        [
            shape_of(attn_in.shape, f32), shape_of(attn_out.shape, f32), shape_of(attn_in.shape, f32),
            shape_of(attn_out.shape, f32), shape_of(ff_in.shape, f32), shape_of(ff_out.shape, f32),
            shape_of((3, width), f32), shape_of((6, width), f32), shape_of((2, width), f32),
            shape_of((2, ff_width), f32), shape_of((1, width), f32),
            shape_of(bias_table.shape, f32), shape_of(bias_table.shape, f32),
        ],
        [], tally, sum_first, sum_second, sum_fin, sum_fout, first_rows, second_rows, fin_rows,
        fout_rows, attn_in, attn_out, ff_in, ff_out, table, scalars=0, us=3, name="update",
    )
    sum_gain = lax.dynamic_slice_in_dim(sum_gain, device * chunk, chunk, 1)
    in_rows = jnp.concatenate([first_rows, second_rows[1:4]])[:, :, 0]
    out_rows = jnp.stack([second_rows[0], second_rows[4]])[:, :, 0]
    return (
        output, grad_targets, grad_memory,
        sum_in, sum_out, sum_gain, sum_fin, sum_fout[0], grad_table,
        in_rows, in_cols, out_rows, out_cols, fin_rows[:, :, 0], fin_cols, fout_rows[0, :, 0],
        fout_cols[0], new_in, new_out, new_fin, new_fout, new_table,
    )


def solution(mesh):
    in_specs = (
        P("wide", "narrow", None),
        P("wide", "narrow", None),
        P("wide", "narrow", None),
        P("wide", "narrow"),
        P("wide", "narrow"),
        P("narrow", None),
        P(None, ("wide", "narrow"), None),
        P(None, ("wide", "narrow"), None),
        P(None, ("wide", "narrow")),
        P(None, ("wide", "narrow"), None),
        P(("wide", "narrow"), None),
        P(),
    )
    out_specs = (
        P("wide", "narrow", None),
        P("wide", "narrow", None),
        P("wide", "narrow", None),
        P(None, ("wide", "narrow"), None),
        P(None, ("wide", "narrow"), None),
        P(None, ("wide", "narrow")),
        P(None, ("wide", "narrow"), None),
        P(("wide", "narrow"), None),
        P(),
        P(None, ("wide", "narrow")),
        P(),
        P(None, ("wide", "narrow")),
        P(),
        P(None, ("wide", "narrow")),
        P(),
        P(("wide", "narrow")),
        P(),
        P(None, ("wide", "narrow"), None),
        P(None, ("wide", "narrow"), None),
        P(None, ("wide", "narrow"), None),
        P(("wide", "narrow"), None),
        P(),
    )
    return jax.shard_map(body, mesh=mesh, in_specs=in_specs, out_specs=out_specs, check_vma=False)
```

```python
import functools
import math

import jax
import jax.numpy as jnp
from jax import lax
from jax.experimental import pallas as pl
from jax.experimental.pallas import tpu as pltpu
from jax.sharding import PartitionSpec as P

bf16, f32 = jnp.bfloat16, jnp.float32
BOTH = ("wide", "narrow")
NEG = -1e9
TILE = 256
MIB = 1 << 20


def dot_nn(left, right):
    return lax.dot_general(left, right, (((1,), (0,)), ((), ())), preferred_element_type=f32)


def dot_nt(left, right):
    return lax.dot_general(left, right, (((1,), (1,)), ((), ())), preferred_element_type=f32)


def unit_of(values):
    inv_rms = lax.rsqrt(jnp.mean(values * values, axis=-1, keepdims=True) + 1e-06)
    return values * inv_rms, inv_rms


def norm_back(incoming, values, gain_row):
    unit, inv_rms = unit_of(values)
    scaled = incoming * gain_row
    inner = jnp.mean(scaled * unit, axis=-1, keepdims=True)
    return inv_rms * (scaled - unit * inner), jnp.sum(incoming * unit, axis=0, keepdims=True)


def tiles_of(width):
    return [(start, min(TILE, width - start)) for start in range(0, width, TILE)]


def project(left, w_ref, index, store):
    for start, size in tiles_of(w_ref.shape[2]):
        store(start, size, dot_nn(left, w_ref[index, :, start : start + size]))


def half_lanes(second):
    lane = lax.broadcasted_iota(jnp.int32, (1, 128), 1)
    return ((lane >= 64) == bool(second)).astype(bf16)


def biased(table_row, index):
    spread = jnp.broadcast_to(table_row, (index.shape[0], 128))
    return jnp.concatenate(
        [
            jnp.take_along_axis(
                spread, index[:, at : at + 128], axis=1, mode="promise_in_bounds"
            )
            for at in range(0, index.shape[1], 128)
        ],
        axis=1,
    )


def query_blocks(keys, queries, causal):
    return [
        (at, min(keys, at + TILE) if causal else keys) for at in range(0, queries, TILE)
    ]


def attend(qkv_ref, extra_ref, table_ref, o_ref, peak_ref, inv_ref, ot_ref):
    causal = table_ref is not None
    keys = qkv_ref.shape[1]

    def pair(at_pair, carry):
        lanes = pl.ds(pl.multiple_of(at_pair * 128, 128), 128)
        query, key, value = (qkv_ref[i, :, lanes] for i in range(3))
        value_t = value.T
        for second in range(2):
            head = at_pair * 2 + second
            key_half = key * half_lanes(second)
            for start, last in query_blocks(keys, keys, causal):
                part = slice(start, start + TILE)
                scores = dot_nt(key_half[:last], query[part])
                if causal:
                    scores += biased(table_ref[pl.ds(head, 1), :], extra_ref[:last, part])
                else:
                    scores += extra_ref[:last, part]
                peak = jnp.max(scores, axis=0, keepdims=True)
                grown = jnp.exp(scores - peak)
                inverse = 1.0 / jnp.sum(grown, axis=0, keepdims=True)
                mixed = dot_nn(value_t[second * 64 : second * 64 + 64, :last], grown.astype(bf16))
                ot_ref[second * 64 : second * 64 + 64, part] = mixed * inverse
                peak_ref[head, :, part] = peak
                inv_ref[head, :, part] = inverse
        o_ref[:, lanes] = ot_ref[...].T.astype(bf16)
        return carry

    lax.fori_loop(0, qkv_ref.shape[2] // 128, pair, 0)


def attend_back(
    qkv_ref, extra_ref, table_ref, do_ref, dsum_ref, peak_ref, inv_ref,
    dqkv_ref, p_ref, ds_ref, dqt_ref, ds_out,
):
    causal = table_ref is not None
    keys = qkv_ref.shape[1]
    first_half = lax.broadcasted_iota(jnp.int32, (1, 128), 1) < 64

    def pair(at_pair, carry):
        lanes = pl.ds(pl.multiple_of(at_pair * 128, 128), 128)
        query, key, value = (qkv_ref[i, :, lanes] for i in range(3))
        grad = do_ref[:, lanes]
        key_t = key.T
        for second in range(2):
            head = at_pair * 2 + second
            half = half_lanes(second)
            key_half, value_half = key * half, value * half
            for start, last in query_blocks(keys, keys, causal):
                part = slice(start, start + TILE)
                scores = dot_nt(key_half[:last], query[part])
                if causal:
                    scores += biased(table_ref[pl.ds(head, 1), :], extra_ref[:last, part])
                else:
                    scores += extra_ref[:last, part]
                weights = jnp.exp(scores - peak_ref[head, :, part]) * inv_ref[head, :, part]
                grad_weights = dot_nt(value_half[:last], grad[part])
                grad_scores = (weights * (grad_weights - dsum_ref[head, :, part])).astype(bf16)
                p_ref[:last, part] = weights.astype(bf16)
                ds_ref[:last, part] = grad_scores
                dqt_ref[second * 64 : second * 64 + 64, part] = dot_nn(
                    key_t[second * 64 : second * 64 + 64, :last], grad_scores
                )
            for start in range(0, keys, TILE):
                rows = slice(start, start + TILE)
                begin = start if causal else 0
                d_value = dot_nn(p_ref[rows, begin:], grad[begin:]).astype(bf16)
                d_key = dot_nn(ds_ref[rows, begin:], query[begin:]).astype(bf16)
                if second:
                    d_value = jnp.where(first_half, dqkv_ref[2, rows, lanes], d_value)
                    d_key = jnp.where(first_half, dqkv_ref[1, rows, lanes], d_key)
                dqkv_ref[2, rows, lanes] = d_value
                dqkv_ref[1, rows, lanes] = d_key
            if ds_out is not None:
                ds_out[head] = ds_ref[...]
        dqkv_ref[0, :, lanes] = dqt_ref[...].T.astype(bf16)
        return carry

    if causal:
        p_ref[...] = jnp.zeros_like(p_ref)
        ds_ref[...] = jnp.zeros_like(ds_ref)
    lax.fori_loop(0, qkv_ref.shape[2] // 128, pair, 0)


def head_sums(grad, mixed, dsum_ref):
    heads = dsum_ref.shape[0]
    product = grad.astype(f32) * mixed.astype(f32)
    width = product.shape[1]
    pick = (
        lax.broadcasted_iota(jnp.int32, (16, width), 1) // (width // heads)
        == lax.broadcasted_iota(jnp.int32, (16, width), 0)
    ).astype(f32)
    sums = lax.dot_general(
        pick, product, (((1,), (1,)), ((), ())),
        preferred_element_type=f32, precision=lax.Precision.HIGHEST,
    )
    for head in range(heads):
        dsum_ref[head] = sums[head : head + 1]


def square_kernel(*refs):
    row = 0
    for ref in refs[:-1]:
        parts = [ref[i] for i in range(ref.shape[0])] if len(ref.shape) == 3 else [ref[...]]
        for part in parts:
            total = jnp.sum(jnp.sum(part * part, axis=1, keepdims=True), axis=0, keepdims=True)
            refs[-1][row : row + 1, :] = jnp.broadcast_to(total, (1, 128))
            row += 1
    refs[-1][row:, :] = jnp.zeros((refs[-1].shape[0] - row, 128), f32)


def tally_kernel(gain1, gain2, gain3, first, second, fin, fout, table, squares, out_ref):
    at = 0
    rows = [ref[...] for ref in (gain1, gain2, gain3)]
    rows += [ref[i] for ref in (first, second, fin, fout) for i in range(ref.shape[0])]
    for row in rows:
        for start in range(0, row.shape[1], 128):
            out_ref[at : at + 1, :] = row[:, start : start + 128]
            at += 1
    for ref in (table, squares):
        out_ref[at : at + ref.shape[0], :] = ref[...]
        at += ref.shape[0]
    out_ref[at:, :] = jnp.zeros((out_ref.shape[0] - at, 128), f32)


def update_kernel(tally, first, second, fin, fout, first_rows, second_rows, fin_rows, fout_rows,
                  attn_in, attn_out, ff_in, ff_out, table, g_in, g_out, new_in, new_out, new_fin,
                  new_fout, gains, in_cols, out_cols, fin_cols, fout_cols, g_table, new_table,
                  *, buckets):
    at = 0

    def row(width):
        nonlocal at
        parts = [tally[at + i : at + i + 1, :] for i in range(width // 128)]
        at += width // 128
        return jnp.concatenate(parts, axis=1)

    width, ff_width = attn_in.shape[2], ff_in.shape[2]
    for i in range(3):
        gains[i : i + 1, :] = row(width)
    cols = [row(width) for _ in range(8)]
    cols += [row(ff_width), row(ff_width), row(width)]
    heads = table.shape[0]
    grad_t = tally[at : at + heads, :][:, :buckets]
    squares = at + heads
    sizes = [width * width] * 8 + [width * ff_width] * 3

    def step(grad, weight, rows, col, square, size):
        overall = jnp.sum(col, axis=1, keepdims=True)
        rms = jnp.sqrt(tally[squares + square : squares + square + 1, 0:1] / size + 1e-06)
        return weight - 0.3 * rms * grad * lax.rsqrt(rows * col / overall)

    places = [(first, first_rows, i, col) for i, col in enumerate(cols[:3])]
    places += [(second, second_rows, i, cols[3 + i]) for i in (1, 2, 3)]
    for i, (grad, rows, j, col) in enumerate(places):
        g_in[i] = grad[j]
        in_cols[i : i + 1, :] = col
        new_in[i] = step(grad[j], attn_in[i], rows[j], col, i, sizes[0])
    for i, j in ((0, 0), (1, 4)):
        col = cols[3 + j]
        g_out[i] = second[j]
        out_cols[i : i + 1, :] = col
        new_out[i] = step(second[j], attn_out[i], second_rows[j], col, 6 + i, sizes[0])
    for i in range(2):
        fin_cols[i : i + 1, :] = cols[8 + i]
        new_fin[i] = step(fin[i], ff_in[i], fin_rows[i], cols[8 + i], 8 + i, sizes[8])
    fout_cols[...] = cols[10]
    new_fout[...] = step(fout[0], ff_out[...], fout_rows[0], cols[10], 10, sizes[8])
    weight = table[:, :buckets]
    square = grad_t * grad_t + 1e-30
    by_bucket = jnp.sum(square, axis=0, keepdims=True)
    by_head = jnp.sum(square, axis=1, keepdims=True)
    overall = jnp.sum(by_head, axis=0, keepdims=True)
    mean = jnp.sum(jnp.sum(weight * weight, axis=1, keepdims=True), axis=0, keepdims=True)
    rms = jnp.sqrt(mean / (heads * buckets) + 1e-06)
    new_t = weight - 0.3 * rms * grad_t * lax.rsqrt(by_bucket * by_head / overall)
    g_table[...] = grad_t.T
    new_table[...] = new_t.T


def fold_rows(core, turned, turned_ref, out_ref, fold):
    if not fold:
        out_ref[...] = turned
        return
    turned_ref[...] = turned
    total = turned.shape[0]
    size = total // 8
    for group in range(4):
        for place, which in ((0, core), (1, 1 - core)):
            begin = pl.multiple_of(group * 2 * size + which * size, 16)
            to = place * (total // 2) + group * size
            out_ref[to : to + size, :] = turned_ref[pl.ds(begin, size), :]


def weight_grad(left_ref, right_ref, keep_ref, send_ref, index):
    half = left_ref.shape[0] // 2
    for start, size in tiles_of(right_ref.shape[1]):
        part = slice(start, start + size)
        right = right_ref[:, part]
        keep_ref[index, :, part] = dot_nn(left_ref[:half], right).astype(bf16)
        send_ref[index, :, part] = dot_nn(left_ref[half:], right).astype(bf16)


def start_weights(place, pieces, target_ref, sems, only=None):
    if len(pieces) == 2:
        size = pieces[0].shape[0] // 4
        pieces = [piece.at[pl.ds(d * size, size)] for d in range(4) for piece in pieces]
    elif len(pieces) == 4:
        size = pieces[1].shape[0]
        pieces = [
            many.at[pl.ds(d * size, size)] if d < 3 else last
            for d in range(4)
            for many, last in (pieces[:2], pieces[2:])
        ]
    rows = target_ref.shape[1] // len(pieces)
    copies = []
    for d, piece in enumerate(pieces):
        begin = pl.multiple_of((place ^ d) * rows, rows) if len(pieces) > 1 else 0
        source = piece if only is None else piece.at[only]
        copies.append(
            pltpu.make_async_copy(source, target_ref.at[:, pl.ds(begin, rows), :], sems.at[d])
        )
        copies[-1].start()
    return copies


def join_rows(place, pieces, target_ref):
    rows = pieces[0].shape[0]
    for d, piece in enumerate(pieces):
        target_ref[pl.ds(pl.multiple_of((place ^ d) * rows, 16), rows), :] = piece[...]


def join_blocks(place, pieces, target_ref):
    blocks = target_ref.shape[1] // TILE
    rows = target_ref.shape[0] // len(pieces)
    for d, piece in enumerate(pieces):
        to = pl.ds(pl.multiple_of((place ^ d) * rows, 16), rows)
        for j in range(blocks):
            target_ref[to, j * TILE : (j + 1) * TILE] = piece[j * rows : (j + 1) * rows, :]


def pack_kernel(at_ref, x_ref, m_ref, c_ref, seg_t_ref, seg_m_ref, *outs, narrow):
    local, width = x_ref.shape[1:]
    for d in range(narrow):
        first, memory, cot = outs[d], outs[narrow + d], outs[2 * narrow + d]
        row = at_ref[2] ^ d
        memory[...] = m_ref[row]
        cot[...] = c_ref[row]
        begin = 0
        for j in range(width // TILE):
            first[begin : begin + local, :] = x_ref[row, :, j * TILE : (j + 1) * TILE]
            begin += local
        for i, ref in enumerate((seg_t_ref, seg_m_ref)):
            seg = jnp.broadcast_to(ref[pl.ds(row, 1), :].astype(f32), (16, local))
            first[begin : begin + 16, i * local : (i + 1) * local] = seg.astype(bf16)


def split_rows(place, source_ref, pieces):
    rows = pieces[0].shape[0]
    for d, piece in enumerate(pieces):
        piece[...] = source_ref[pl.ds(pl.multiple_of((place ^ d) * rows, 16), rows), :].astype(
            piece.dtype
        )


def first_kernel(at_ref, *refs, pieces, narrow, chunk, bucket_count):
    x_refs, refs = refs[:narrow], refs[narrow:]
    w_refs, refs = refs[:pieces], refs[pieces:]
    near_ref = None
    if pieces == 1:
        near_ref, refs = refs[0], refs[1:]
    (allowed_ref, table_ref, w_ref, extra_ref, g_ref, x_ref, h_ref, qkv_ref, o_ref, peak_ref,
     inv_ref, ot_ref, sems) = refs
    copies = start_weights(at_ref[3], w_refs, w_ref, sems)
    join_blocks(at_ref[2], x_refs, x_ref)
    width = x_ref.shape[1]
    pick = (
        lax.broadcasted_iota(jnp.int32, (8, width), 1) % chunk
        == lax.broadcasted_iota(jnp.int32, (8, width), 0)
    ).astype(bf16)
    unit, _ = unit_of(x_ref[...].astype(f32))
    for copy in copies:
        copy.wait()
    gains = dot_nn(pick, w_ref[3])
    g_ref[...] = gains
    if near_ref is None:
        tokens = extra_ref.shape[0]
        held = w_ref[3, :, :tokens].astype(f32)
        groups = width // (narrow * chunk)
        share = tokens // (narrow * groups)
        near = jnp.concatenate(
            [
                held[(w * narrow + n + 1) * chunk - share : (w * narrow + n + 1) * chunk]
                for n in range(narrow)
                for w in range(groups)
            ],
            axis=0,
        ).T
    else:
        near = near_ref[...].astype(f32)
    extra_ref[...] = jnp.where(
        allowed_ref[...] > 0.0, near, float(bucket_count)
    ).astype(jnp.int32)
    h_ref[...] = (unit * gains[0:1]).astype(bf16)
    for i in range(3):
        def store(start, size, product, i=i):
            qkv_ref[i, :, start : start + size] = product.astype(bf16)

        project(h_ref[...], w_ref, i, store)
    attend(qkv_ref, extra_ref, table_ref, o_ref, peak_ref, inv_ref, ot_ref)


def second_kernel(at_ref, *refs, pieces, narrow):
    m_refs, refs = refs[:narrow], refs[narrow:]
    w_refs, refs = refs[:pieces], refs[pieces:]
    (x_ref, o1_ref, extra_ref, g_ref, w_ref, m_ref, x1_ref, h_ref, qkv_ref, o_ref, x2_ref, h3_ref,
     peak_ref, inv_ref, ot_ref, sems) = refs
    copies = start_weights(at_ref[3], w_refs, w_ref, sems)
    join_rows(at_ref[2], m_refs, m_ref)
    for copy in copies:
        copy.wait()

    def store_x1(start, size, product):
        part = slice(start, start + size)
        x1_ref[:, part] = x_ref[:, part].astype(f32) + product

    project(o1_ref[...], w_ref, 0, store_x1)
    unit, _ = unit_of(x1_ref[...])
    h_ref[...] = (unit * g_ref[1:2, :]).astype(bf16)
    for i in range(3):
        def store(start, size, product, i=i):
            qkv_ref[i, :, start : start + size] = product.astype(bf16)

        project(m_ref[...] if i else h_ref[...], w_ref, i + 1, store)
    attend(qkv_ref, extra_ref, None, o_ref, peak_ref, inv_ref, ot_ref)

    def store_x2(start, size, product):
        part = slice(start, start + size)
        x2_ref[:, part] = x1_ref[:, part] + product

    project(o_ref[...], w_ref, 4, store_x2)
    unit, _ = unit_of(x2_ref[...])
    h3_ref[...] = (unit * g_ref[2:3, :]).astype(bf16)


def prepare_kernel(at_ref, *refs, narrow, skip):
    in_refs, (allowed_ref, mask_ref, seg_ref) = refs[:narrow], refs[narrow:]
    tokens = mask_ref.shape[0]
    local = tokens // narrow
    for d, ref in enumerate(in_refs):
        lanes = pl.ds(pl.multiple_of((at_ref[2] ^ d) * local, 128), local)
        tail = ref[skip : skip + 16, :].astype(f32)
        seg_ref[0:8, lanes] = tail[:8, :local]
        seg_ref[8:16, lanes] = tail[:8, local : 2 * local]
    seg = seg_ref[...]
    seg_t = seg.T
    key = lax.broadcasted_iota(jnp.int32, (tokens, tokens), 0)
    query = lax.broadcasted_iota(jnp.int32, (tokens, tokens), 1)
    allowed = (key <= query) & (seg_t[:, 0:1] == seg[0:1, :])
    allowed_ref[...] = jnp.where(allowed, 1.0, 0.0)
    mask_ref[...] = jnp.where(seg_t[:, 8:9] == seg[0:1, :], 0.0, NEG)


def order_kernel(at_ref, *refs, outs):
    pieces, out_refs = refs[:-outs], refs[-outs:]
    for d, piece in enumerate(pieces):
        if piece.ndim == 2:
            out_refs[0][at_ref[2] ^ d] = piece[...]
            continue
        begin = 0
        for out_ref in out_refs:
            size = out_ref.shape[0]
            out_ref[:, at_ref[2] ^ d] = piece[begin : begin + size]
            begin += size


def read_part(refs, group):
    if len(refs) == 1:
        count, rows, cols = refs[0].shape
        rows //= 4
        part = pl.ds(pl.multiple_of(group * rows, 16), rows)
        return refs[0][:, part, :].astype(f32).reshape(count * rows, cols)
    fin, fout = refs
    rows, rows_out = fin.shape[1] // 4, fout.shape[1] // 4
    part = pl.ds(pl.multiple_of(group * rows, 16), rows)
    part_out = pl.ds(pl.multiple_of(group * rows_out, 16), rows_out)
    pieces = [
        fin[i, part, at : at + TILE].astype(f32)
        for i in range(fin.shape[0])
        for at in range(0, fin.shape[2], TILE)
    ]
    pieces += [
        fout[0, part_out, at : at + TILE].astype(f32) for at in range(0, fout.shape[2], TILE)
    ]
    return jnp.concatenate(pieces, axis=0)


def spread_kernel(at_ref, *refs, count):
    keeps, recvs = refs[:count], refs[count : 2 * count]
    own_ref, kept_x, kept_y, to_x, to_y = refs[2 * count :]
    half = own_ref.shape[0] // 2
    for d in range(4):
        total = read_part(keeps, at_ref[1] ^ d) + read_part(recvs, at_ref[1] ^ d)
        if d == 0:
            own_ref[...] = total
        elif d == 1:
            to_x[0] = total[:half].astype(bf16)
            kept_x[...] = total[half:]
        elif d == 2:
            to_y[0] = total[half:].astype(bf16)
            kept_y[...] = total[:half]
        else:
            to_x[1] = total[:half].astype(bf16)
            to_y[1] = total[half:].astype(bf16)


def middle_kernel(own_ref, kept_x, kept_y, from_x, from_y, sum_ref, to_x, to_y):
    half = own_ref.shape[0] // 2
    sum_ref[:half, :] = own_ref[:half, :] + from_x[0].astype(f32)
    sum_ref[half:, :] = own_ref[half:, :] + from_y[0].astype(f32)
    to_y[...] = (kept_y[...] + from_x[1].astype(f32)).astype(bf16)
    to_x[...] = (kept_x[...] + from_y[1].astype(f32)).astype(bf16)


def narrow_kernel(at_ref, own_ref, from_x, from_y, *refs, narrow, spots):
    riders, outs, sum_ref = refs[: -narrow - 1], refs[-narrow - 1 : -1], refs[-1]
    half = own_ref.shape[0] // 2
    sum_ref[:half, :] = own_ref[:half, :] + from_y[...].astype(f32)
    sum_ref[half:, :] = own_ref[half:, :] + from_x[...].astype(f32)
    for d, out_ref in enumerate(outs):
        place = at_ref[2] ^ d
        share = jnp.concatenate(
            [
                sum_ref[pl.ds(start + pl.multiple_of(place * rows, 8), rows), :]
                for start, rows in spots
            ],
            axis=0,
        ).astype(out_ref.dtype)
        ahead = out_ref.shape[0] - share.shape[0]
        if ahead:
            rider, cols = riders[d - 1], out_ref.shape[1]
            rows = rider.shape[0]
            for j in range(rider.shape[1] // cols):
                out_ref[j * rows : (j + 1) * rows, :] = rider[:, j * cols : (j + 1) * cols]
        out_ref[ahead:, :] = share


def join_kernel(at_ref, *refs):
    own, pieces, out_ref = refs[0], refs[1:-1], refs[-1]
    out_ref[at_ref[2]] = own[...]
    rows, width = own.shape
    for d, piece in enumerate(pieces):
        cols = piece.shape[1]
        for j in range(width // cols):
            out_ref[at_ref[2] ^ (d + 1), :, j * cols : (j + 1) * cols] = piece[
                j * rows : (j + 1) * rows, :
            ]


def total_kernel(*refs, narrow):
    total = refs[0][...]
    for ref in refs[1:narrow]:
        total = total + ref[ref.shape[0] - total.shape[0] :, :].astype(f32)
    outs = refs[narrow:]
    at = 0
    for total_ref, rows_ref, cols_ref in zip(*(outs[i::3] for i in range(3))):
        count, rows, cols = total_ref.shape
        block = total.shape[1]
        if cols == block:
            total_ref[...] = total[at : at + count * rows].reshape(count, rows, cols)
            at += count * rows
        else:
            for i in range(count):
                for j in range(cols // block):
                    total_ref[i, :, j * block : (j + 1) * block] = total[at : at + rows]
                    at += rows
        squares = total_ref[...]
        squares = squares * squares + 1e-30
        rows_ref[...] = jnp.sum(squares, axis=-1, keepdims=True)
        cols_ref[...] = jnp.sum(squares, axis=1, keepdims=True)


def ffn_kernel(at_ref, *refs, fold, narrow, pieces, first_out):
    c_refs, refs = refs[:narrow], refs[narrow:]
    fin_refs, refs = refs[:pieces], refs[pieces:]
    fout_refs, refs = refs[:pieces], refs[pieces:]
    (x2_ref, h_ref, g_ref), refs = refs[:3], refs[3:]
    out_refs, refs = refs[:narrow], refs[narrow:]
    (dx_ref, dg_ref, kin_ref, sin_ref, kout_ref, sout_ref, acc_ref, dh_ref, turned_ref, ht_ref,
     gout_ref, c_ref, fin_ref, fout_ref, fin_sems, fout_sems) = refs
    step, steps = pl.program_id(0), pl.num_programs(0)
    core = at_ref[0]

    @pl.when(step == 0)
    def _():
        copies = start_weights(at_ref[3], fin_refs, fin_ref, fin_sems, pl.ds(0, fin_ref.shape[0]))
        copies += start_weights(
            at_ref[3], fout_refs, fout_ref, fout_sems, pl.ds(first_out, fout_ref.shape[0])
        )
        join_rows(at_ref[2], c_refs, c_ref)
        acc_ref[...] = x2_ref[...]
        dh_ref[...] = jnp.zeros_like(dh_ref)
        fold_rows(core, h_ref[...].T, turned_ref, ht_ref, fold)
        for copy in copies:
            copy.wait()

    hidden_in, cot = h_ref[...], c_ref[...]
    size = fin_ref.shape[2]
    blocks = gout_ref.shape[0] // size
    for block in range(blocks):
        part = slice(block * size, (block + 1) * size)
        at_gate = step * blocks + block
        at_up = fin_ref.shape[0] // 2 + at_gate
        gate = dot_nn(hidden_in, fin_ref[at_gate])
        up = dot_nn(hidden_in, fin_ref[at_up])
        square = gate * gate
        bent = jnp.tanh(0.7978845608028654 * (gate + 0.044715 * square * gate))
        plus = 0.5 * (1.0 + bent)
        act = gate * plus
        slope = plus + 0.5 * gate * (1.0 - bent * bent) * (
            0.7978845608028654 + (3 * 0.044715 * 0.7978845608028654) * square
        )
        hidden = (act * up).astype(bf16)
        down_rows = pl.ds(pl.multiple_of(at_gate * size, size), size)
        down = jnp.concatenate(
            [fout_ref[i, down_rows, :] for i in range(fout_ref.shape[0])], axis=1
        )
        acc_ref[...] += dot_nn(hidden, down)
        grad = dot_nt(cot, down)
        d_gate = (grad * up * slope).astype(bf16)
        d_up = (grad * act).astype(bf16)
        dh_ref[...] += dot_nt(d_gate, fin_ref[at_gate]) + dot_nt(d_up, fin_ref[at_up])
        half = ht_ref.shape[0] // 2
        for index, right in ((0, d_gate), (1, d_up)):
            product = dot_nn(ht_ref[...], right).astype(bf16)
            kin_ref[index, :, part] = product[:half]
            sin_ref[index, :, part] = product[half:]
        gout_ref[part, :] = dot_nn(hidden.T, cot).astype(bf16)
    rows = gout_ref.shape[0] // 2
    kept = pl.multiple_of(core * rows, 16) if fold else 0
    sent = pl.multiple_of((1 - core) * rows, 16) if fold else rows
    kout_ref[...] = gout_ref[pl.ds(kept, rows), :]
    sout_ref[...] = gout_ref[pl.ds(sent, rows), :]

    @pl.when(step == steps - 1)
    def _():
        split_rows(at_ref[2], acc_ref, out_refs)
        back, d_gain = norm_back(dh_ref[...], x2_ref[...], g_ref[2:3, :])
        dx_ref[...] = cot.astype(f32) + back
        dg_ref[...] = d_gain


def attend_back_kernel(at_ref, *refs, pieces, which, causal):
    w_refs, refs = refs[:pieces], refs[pieces:]
    table_ref = None
    if causal:
        table_ref, refs = refs[0], refs[1:]
    dx_ref, o_ref, qkv_ref, extra_ref, peak_ref, inv_ref, dqkv_ref = refs[:7]
    ds_out, refs = (refs[7], refs[8:]) if causal else (None, refs[7:])
    do_ref, dsum_ref, p_ref, ds_ref, dqt_ref, w_ref, sems = refs
    copies = start_weights(at_ref[3], w_refs, w_ref, sems, pl.ds(which, 1))
    branch = dx_ref[...].astype(bf16)
    for copy in copies:
        copy.wait()
    for start, size in tiles_of(o_ref.shape[1]):
        do_ref[:, start : start + size] = dot_nt(
            branch, w_ref[0, start : start + size, :]
        ).astype(bf16)
    head_sums(do_ref[...], o_ref[...], dsum_ref)
    attend_back(qkv_ref, extra_ref, table_ref, do_ref, dsum_ref, peak_ref, inv_ref, dqkv_ref,
                p_ref, ds_ref, dqt_ref, ds_out)


def second_back_kernel(at_ref, *refs, pieces, narrow, fold):
    w_refs, refs = refs[:pieces], refs[pieces:]
    (dqkv_ref, dx2_ref, o_ref, h_ref, m_ref, x1_ref, o1_ref, g_ref), refs = refs[:8], refs[8:]
    gm_refs, refs = refs[:narrow], refs[narrow:]
    (dx1_ref, dg_ref, keep_ref, send_ref, turned_ref, left_ref, gm_ref, w_ref, sems) = refs
    core = at_ref[0]
    copies = start_weights(at_ref[3], w_refs, w_ref, sems, pl.ds(1, 3))
    gm_ref[...] = dx2_ref[...].astype(bf16)
    fold_rows(core, o_ref[...].T, turned_ref, left_ref, fold)
    for copy in copies:
        copy.wait()
    weight_grad(left_ref, gm_ref, keep_ref, send_ref, 4)
    fold_rows(core, h_ref[...].T, turned_ref, left_ref, fold)
    weight_grad(left_ref, dqkv_ref.at[0], keep_ref, send_ref, 1)
    fold_rows(core, m_ref[...].T, turned_ref, left_ref, fold)
    for i in (1, 2):
        weight_grad(left_ref, dqkv_ref.at[i], keep_ref, send_ref, i + 1)
    for start, size in tiles_of(o_ref.shape[1]):
        rows = slice(start, start + size)
        gm_ref[:, rows] = (
            dot_nt(dqkv_ref[1], w_ref[1, rows, :]) + dot_nt(dqkv_ref[2], w_ref[2, rows, :])
        ).astype(bf16)
        dx1_ref[:, rows] = dot_nt(dqkv_ref[0], w_ref[0, rows, :])
    split_rows(at_ref[2], gm_ref, gm_refs)
    back, d_gain = norm_back(dx1_ref[...], x1_ref[...], g_ref[1:2, :])
    d_x1 = dx2_ref[...] + back
    dx1_ref[...] = d_x1
    dg_ref[...] = d_gain
    gm_ref[...] = d_x1.astype(bf16)
    fold_rows(core, o1_ref[...].T, turned_ref, left_ref, fold)
    weight_grad(left_ref, gm_ref, keep_ref, send_ref, 0)


def first_back_kernel(at_ref, *refs, pieces, narrow, fold):
    w_refs, refs = refs[:pieces], refs[pieces:]
    (dqkv_ref, h_ref, dx1_ref, x_ref, g_ref), refs = refs[:5], refs[5:]
    gx_refs, refs = refs[:narrow], refs[narrow:]
    dg_ref, keep_ref, send_ref, turned_ref, left_ref, dh_ref, w_ref, sems = refs
    copies = start_weights(at_ref[3], w_refs, w_ref, sems, pl.ds(0, 3))
    fold_rows(at_ref[0], h_ref[...].T, turned_ref, left_ref, fold)
    for copy in copies:
        copy.wait()
    for i in range(3):
        weight_grad(left_ref, dqkv_ref.at[i], keep_ref, send_ref, i)
    for start, size in tiles_of(h_ref.shape[1]):
        rows = slice(start, start + size)
        dh_ref[:, rows] = (
            dot_nt(dqkv_ref[0], w_ref[0, rows, :])
            + dot_nt(dqkv_ref[1], w_ref[1, rows, :])
            + dot_nt(dqkv_ref[2], w_ref[2, rows, :])
        )
    back, d_gain = norm_back(dh_ref[...], x_ref[...].astype(f32), g_ref[0:1, :])
    dh_ref[...] = dx1_ref[...] + back
    split_rows(at_ref[2], dh_ref, gx_refs)
    dg_ref[...] = d_gain


def table_kernel(ds_ref, index_ref, out_ref, acc_ref, *, buckets):
    heads, keys, queries = ds_ref.shape
    acc_ref[...] = jnp.zeros_like(acc_ref)

    def group(at, carry):
        rows = pl.ds(pl.multiple_of(at * 16, 16), 16)
        index = index_ref[rows, :]
        grads = ds_ref[:, rows, :].reshape(heads * 16, queries)
        hot = jnp.concatenate(
            [(index == b).astype(f32).astype(bf16) for b in range(buckets)], axis=0
        )
        acc_ref[...] += dot_nt(grads, hot)
        return carry

    lax.fori_loop(0, keys // 16, group, 0)
    shape = acc_ref.shape
    same = (
        lax.broadcasted_iota(jnp.int32, shape, 0) % 16
        == lax.broadcasted_iota(jnp.int32, shape, 1) % 16
    )
    kept = jnp.where(same, acc_ref[...], 0.0).reshape(heads, 16, shape[1]).sum(axis=1)
    gather = (
        lax.broadcasted_iota(jnp.int32, (shape[1], 128), 0) // 16
        == lax.broadcasted_iota(jnp.int32, (shape[1], 128), 1)
    ).astype(f32)
    out_ref[...] = lax.dot_general(
        kept, gather, (((1,), (0,)), ((), ())),
        preferred_element_type=f32, precision=lax.Precision.HIGHEST,
    )


def cost_of(us):
    return pl.CostEstimate(flops=int(us * 1.15e9), bytes_accessed=MIB, transcendentals=0)


def room_for(arrays, scratch):
    size = sum(v.size * v.dtype.itemsize for v in arrays)
    for ref in scratch:
        shape = getattr(ref, "shape", ())
        if ref.memory_space == pltpu.VMEM:
            rows = -(-shape[-2] // 8) * 8
            size += math.prod(shape[:-2]) * rows * shape[-1] * jnp.dtype(ref.dtype).itemsize
    return (size // MIB + 8) * MIB


def call(kernel, outs, scratch, *args, scalars=1, loose=(), us=2, name=None):
    spaces = [
        pltpu.SMEM if i < scalars else pl.ANY if i in loose else pltpu.VMEM
        for i in range(len(args))
    ]
    return pl.pallas_call(
        kernel,
        out_shape=outs,
        in_specs=[pl.BlockSpec(memory_space=space) for space in spaces],
        out_specs=[pl.BlockSpec(memory_space=pltpu.VMEM)] * len(outs),
        scratch_shapes=scratch,
        compiler_params=pltpu.CompilerParams(
            vmem_limit_bytes=room_for(
                [v for v, space in zip(args, spaces) if space == pltpu.VMEM] + list(outs), scratch
            )
        ),
        cost_estimate=cost_of(us),
        name=name,
    )(*args)


def shape_of(shape, dtype):
    return jax.ShapeDtypeStruct(tuple(shape), dtype)


def permuted(value, wide_bits, narrow_bits):
    wide, narrow = lax.axis_size("wide"), lax.axis_size("narrow")
    pairs = [
        (w * narrow + n, (w ^ wide_bits) * narrow + (n ^ narrow_bits))
        for w in range(wide)
        for n in range(narrow)
    ]
    return lax.ppermute(value, BOTH, pairs)


def after(value, *done):
    return lax.optimization_barrier((value, *done))[0]


def ordered(at, pieces, shares=None):
    first = pieces[0]
    if first.ndim == 2:
        shapes = [(len(pieces),) + first.shape]
    else:
        shapes = [(k, len(pieces)) + first.shape[1:] for k in shares]
    outs = [shape_of(shape, first.dtype) for shape in shapes]
    return call(
        functools.partial(order_kernel, outs=len(outs)), outs, [], at, *pieces, us=1, name="order"
    )


def local_stats(gradient):
    squares = gradient * gradient + 1e-30
    return (jnp.sum(squares, axis=-1, keepdims=True), jnp.sum(squares, axis=-2, keepdims=True))


class Scatter:
    def __init__(self, at, pairs, fast, narrow):
        self.at, self.fast, self.narrow, self.pairs = at, fast, narrow, pairs
        self.done = pairs[0][0]
        if not fast:
            return
        keeps = [keep.reshape(-1, keep.shape[1], keep.shape[2]) for keep, _ in pairs]
        sends = [send for _, send in pairs]
        if len(pairs) == 2:
            keeps[1] = keeps[1].reshape(1, -1, keeps[1].shape[2])
            sends[1] = sends[1].reshape(keeps[1].shape)
        self.shapes = [(k.shape[0], k.shape[1] // 4, k.shape[2]) for k in keeps]
        size = sum(k.size for k in keeps) // 4
        cols = TILE if len(pairs) == 2 else keeps[0].shape[2]
        self.rows, self.cols = size // cols, cols
        half = (self.rows // 2, cols)
        recvs = [permuted(send, 1, 0) for send in sends]
        self.own, self.kept_x, self.kept_y, to_x, to_y = call(
            functools.partial(spread_kernel, count=len(pairs)),
            [shape_of((self.rows, cols), f32), shape_of(half, f32), shape_of(half, f32),
             shape_of((2,) + half, bf16), shape_of((2,) + half, bf16)],
            [], at, *keeps, *recvs, us=3, name="spread",
        )
        self.out = (to_x, to_y)
        self.done = self.own

    def middle(self, *done):
        if not self.fast:
            return
        self.own = after(self.own, *done)
        half = (self.rows // 2, self.cols)
        from_x, from_y = permuted(self.out[0], 2, 0), permuted(self.out[1], 4, 0)
        self.own, to_x, to_y = call(
            middle_kernel,
            [shape_of((self.rows, self.cols), f32), shape_of(half, bf16), shape_of(half, bf16)],
            [], self.own, self.kept_x, self.kept_y, from_x, from_y, scalars=0, name="middle",
        )
        self.out = (to_x, to_y)
        self.done = self.own

    def narrowed(self, riders, *done):
        self.riders = riders
        if not self.fast:
            return
        self.own = after(self.own, *done)
        from_x, from_y = permuted(self.out[0], 2, 0), permuted(self.out[1], 4, 0)
        if len(self.shapes) == 2:
            (k, rows, cols), (_, rows_out, cols_out) = self.shapes
            sizes = [rows] * (k * cols // TILE) + [rows_out] * (cols_out // TILE)
        else:
            sizes = [self.shapes[0][1]] * self.shapes[0][0]
        spots, begin = [], 0
        for size in sizes:
            spots.append((begin, size // self.narrow))
            begin += size
        share = self.rows // self.narrow
        ahead = riders[0].size // self.cols if riders else 0
        self.out = call(
            functools.partial(narrow_kernel, narrow=self.narrow, spots=spots),
            [
                shape_of((share + ahead, self.cols) if d else (share, self.cols), bf16 if d else f32)
                for d in range(self.narrow)
            ],
            [pltpu.VMEM((self.rows, self.cols), f32)], self.at, self.own, from_x, from_y,
            *riders[1:], name="narrow",
        )
        self.done = self.out[0]

    def total(self, *done):
        if not self.fast:
            results = []
            for keep, send in self.pairs:
                whole = jnp.concatenate([keep, send], axis=1)
                if keep.shape[0] == 4:
                    whole = whole.reshape(1, -1, whole.shape[2])
                total = lax.psum_scatter(whole, BOTH, scatter_dimension=1, tiled=True).astype(f32)
                results.append((total, *local_stats(total)))
            return results
        parts = [permuted(v, 0, d) if d else v for d, v in enumerate(self.out)]
        parts[0] = after(parts[0], *done)
        if self.riders:
            rider = self.riders[0]
            (self.ridden,) = call(
                join_kernel, [shape_of((self.narrow,) + rider.shape, bf16)], [], self.at,
                after(rider, *done), *parts[1:], name="join",
            )
        outs = []
        for k, rows, cols in self.shapes:
            rows //= self.narrow
            outs += [
                shape_of((k, rows, cols), f32), shape_of((k, rows, 1), f32),
                shape_of((k, 1, cols), f32),
            ]
        flat = call(
            functools.partial(total_kernel, narrow=self.narrow), outs, [], *parts, scalars=0,
            name="total",
        )
        return [
            tuple(flat[3 * i : 3 * i + 3])
            for i in range(len(self.shapes))
        ]


def summed_all(flat, fast):
    if not fast:
        return lax.psum(flat, BOTH)
    flat = flat + permuted(flat, 1, 0)
    flat = (flat + permuted(flat, 2, 0)) + (permuted(flat, 4, 0) + permuted(flat, 6, 0))
    return (flat + permuted(flat, 0, 1)) + (permuted(flat, 0, 2) + permuted(flat, 0, 3))


def body(
    targets, memory, cotangent, target_segments, memory_segments, buckets,
    attn_in, attn_out, gains, ff_in, ff_out, bias_table,
):
    wide, narrow = lax.axis_size("wide"), lax.axis_size("narrow")
    at_wide, at_narrow = lax.axis_index("wide"), lax.axis_index("narrow")
    fast = wide == 8 and narrow == 4
    at = jnp.stack([at_wide % 2, at_wide // 2, at_narrow, at_wide]).astype(jnp.int32)
    width, ff_width = attn_in.shape[2], ff_in.shape[2]
    bucket_count, heads = bias_table.shape
    chunk = gains.shape[1]
    local_tokens = targets.shape[1]
    tokens = local_tokens * narrow
    assert targets.shape[0] == narrow

    def over_narrow(pieces):
        return [permuted(v, 0, d) if d else v for d, v in enumerate(pieces)]

    def to_owners(pieces, *done):
        pieces = over_narrow(pieces)
        return ordered(at, [after(pieces[0], *done)] + pieces[1:])[0]

    device = at_wide * narrow + at_narrow
    gain_rows = lax.dynamic_update_slice(
        jnp.zeros((chunk, width), bf16), gains.astype(bf16), (0, device * chunk)
    )
    if fast:
        share = local_tokens // wide
        held = lax.dynamic_slice_in_dim(buckets, at_wide * share, share, 0).astype(bf16)
        gain_rows = lax.dynamic_update_slice(gain_rows, held, (chunk - share, 0))
    first_local = jnp.concatenate([attn_in[:3].astype(bf16), gain_rows[None]])
    second_local = jnp.concatenate([attn_out[:1], attn_in[3:], attn_out[1:]]).astype(bf16)
    piece16 = shape_of((local_tokens, width), bf16)
    near_rows = local_tokens * width // TILE + 16
    packed = call(
        functools.partial(pack_kernel, narrow=narrow),
        [shape_of((near_rows, TILE), bf16)] * narrow
        + [piece16] * (2 * narrow),
        [], at, targets, memory, cotangent, target_segments, memory_segments,
        us=4, name="pack",
    )
    near, m_out, c_out = packed[:narrow], packed[narrow : 2 * narrow], packed[2 * narrow :]
    lanes = TILE
    fin_blocks = ff_in.astype(bf16).reshape(2, chunk, ff_width // lanes, lanes)
    fin_blocks = fin_blocks.transpose(0, 2, 1, 3).reshape(-1, chunk, lanes)
    out_rows_here = ff_out.shape[0]
    fout_blocks = ff_out.astype(bf16).reshape(out_rows_here, width // lanes, lanes)
    fout_blocks = fout_blocks.transpose(1, 0, 2).reshape(-1, chunk, lanes)
    fin_count, fout_count = fin_blocks.shape[0], fout_blocks.shape[0]
    ffn_local = jnp.concatenate([fin_blocks, fout_blocks])

    def regroup_out(stack, owners):
        stack = stack.reshape(fout_count, owners, chunk, lanes).transpose(1, 0, 2, 3)
        stack = stack.reshape(owners, width // lanes, out_rows_here, lanes)
        return stack.transpose(1, 0, 2, 3).reshape(width // lanes, -1, lanes)

    def over_plane(stack):
        from_x, from_y = permuted(stack, 2, 0), permuted(stack, 4, 0)
        half = stack.shape[0] // 2
        begin, end = from_x[:half], from_y[half:]
        return [stack, from_x, from_y, permuted(begin, 4, 0), permuted(end, 2, 0)]

    def with_other_core(plane, *done):
        own = jnp.concatenate([after(plane[0], *done)] + plane[1:])
        return [own, permuted(own, 1, 0)]

    if fast:
        first_near = over_narrow([first_local] * narrow)
        first_near[0] = after(first_near[0], near[0])
        (stack,) = ordered(at, first_near, (4,))
        near = [near[0]] + [after(v, stack) for v in near[1:]]
        plane_first = over_plane(stack.reshape(4, -1, width))
        held_out = []
    else:
        w_first = [lax.all_gather(first_local, BOTH, axis=1, tiled=True)]
        w_second = [lax.all_gather(second_local, BOTH, axis=1, tiled=True)]
        held_out = [lax.all_gather(buckets.astype(bf16), "narrow", axis=0, tiled=True).T]
    near = over_narrow(near)
    allowed, cross_mask = call(
        functools.partial(
            prepare_kernel, narrow=narrow, skip=local_tokens * width // TILE,
        ),
        [shape_of((tokens, tokens), f32), shape_of((tokens, tokens), f32)],
        [pltpu.VMEM((16, tokens), f32)],
        at, *near, us=2, name="prepare",
    )
    if fast:
        w_first = with_other_core(plane_first, allowed)
        ffn_near = over_narrow([after(ffn_local, allowed)] * narrow)
    table = jnp.concatenate(
        [bias_table.T, jnp.full((heads, 128 - bucket_count), NEG, f32)], axis=1
    )
    row16 = shape_of((tokens, width), bf16)
    row32 = shape_of((tokens, width), f32)
    three = shape_of((3, tokens, width), bf16)
    stat = shape_of((heads, 1, tokens), f32)
    gain_out = shape_of((1, width), f32)
    pair_t = pltpu.VMEM((128, tokens), f32)
    pieces = len(w_first)
    weights = lambda count: pltpu.VMEM((count, width, width), bf16)
    sems = pltpu.SemaphoreType.DMA((8,))
    stack_of = lambda count: shape_of((count, width, width), bf16)
    w_first, index, g, x, h1, qkv1, o1, peak1, inv1 = call(
        functools.partial(
            first_kernel, pieces=pieces, narrow=narrow, chunk=chunk, bucket_count=bucket_count
        ),
        [stack_of(4), shape_of((tokens, tokens), jnp.int32), shape_of((8, width), f32), row16,
         row16, three, row16, stat, stat],
        [pair_t, sems],
        at, *near, *w_first, *held_out, allowed, table,
        loose=range(1 + narrow, 1 + narrow + pieces), us=16, name="first",
    )
    if fast:
        ffn_near[0] = after(ffn_near[0], h1)
        (stack,) = ordered(at, ffn_near, (fin_count + fout_count,))
        second_near = over_narrow([after(second_local, stack)] * narrow)
        stack = stack.reshape(fin_count + fout_count, -1, lanes)
        stack_out = regroup_out(stack[fin_count:], narrow).reshape(fout_count, -1, lanes)
        stack = jnp.concatenate([stack[:fin_count], stack_out])
        plane_ffn = over_plane(stack)
        second_near[0] = after(second_near[0], plane_ffn[1], plane_ffn[2])
        (stack,) = ordered(at, second_near, (5,))
        m_out = [m_out[0]] + [after(v, *second_near[1:]) for v in m_out[1:]]
        plane_second = over_plane(stack.reshape(5, -1, width))
    m_pieces = over_narrow(m_out)
    if fast:
        w_second = with_other_core(plane_second, *m_pieces[1:])
        ffn_near = with_other_core(plane_ffn[:3], *m_pieces[1:])
        o1 = after(o1, ffn_near[1])
        c_out = [c_out[0]] + [after(v, *m_pieces[1:]) for v in c_out[1:]]
    c_pieces = over_narrow(c_out)
    w_second, m, x1, h2, qkv2, o2, x2, h3, peak2, inv2 = call(
        functools.partial(second_kernel, pieces=pieces, narrow=narrow),
        [stack_of(5), row16, row32, row16, three, row16, row32, row16, stat, stat],
        [pair_t, sems],
        at, *m_pieces, *w_second, x, o1, cross_mask, g,
        loose=range(1 + narrow, 1 + narrow + pieces), us=21, name="second",
    )

    if fast:
        ffn_pieces = ffn_near + with_other_core(plane_ffn[3:], x2, *c_pieces[1:])
        ffn_pieces = [ffn_pieces[i] for i in (0, 2, 1, 3)]
        w_fin = ffn_pieces
        w_fout = [v.reshape(-1, narrow * out_rows_here, lanes) for v in ffn_pieces]
    else:
        every = lax.all_gather(ffn_local, BOTH, axis=1, tiled=True)
        w_fin, w_fout = [every], [regroup_out(every[fin_count:], wide * narrow)]
    steps = 4
    part = ff_width // steps
    half = width // 2
    whole = lambda shape: pl.BlockSpec(shape, lambda i: (0,) * len(shape))
    outs = pl.pallas_call(
        functools.partial(
            ffn_kernel, fold=fast, narrow=narrow, pieces=len(w_fin),
            first_out=w_fout[1].shape[0] - width // lanes if fast else 0,
        ),
        grid=(steps,),
        in_specs=[pl.BlockSpec(memory_space=pltpu.SMEM)]
        + [whole((local_tokens, width))] * narrow
        + [pl.BlockSpec(memory_space=pl.ANY)] * (2 * len(w_fin))
        + [whole((tokens, width)), whole((tokens, width)), whole((8, width))],
        out_specs=[whole((local_tokens, width))] * narrow
        + [
            whole((tokens, width)), whole((1, width)),
            pl.BlockSpec((2, half, part), lambda i: (0, 0, i)),
            pl.BlockSpec((2, half, part), lambda i: (0, 0, i)),
            pl.BlockSpec((None, part // 2, width), lambda i: (i, 0, 0)),
            pl.BlockSpec((None, part // 2, width), lambda i: (i, 0, 0)),
        ],
        out_shape=[piece16] * narrow
        + [
            row32, gain_out,
            shape_of((2, half, ff_width), bf16), shape_of((2, half, ff_width), bf16),
            shape_of((steps, part // 2, width), bf16), shape_of((steps, part // 2, width), bf16),
        ],
        scratch_shapes=[
            pltpu.VMEM((tokens, width), f32), pltpu.VMEM((tokens, width), f32),
            pltpu.VMEM((width, tokens), bf16), pltpu.VMEM((width, tokens), bf16),
            pltpu.VMEM((part, width), bf16), pltpu.VMEM((tokens, width), bf16),
            pltpu.VMEM((fin_count, width, lanes), bf16),
            pltpu.VMEM((width // lanes, ff_width, lanes), bf16), sems, sems,
        ],
        compiler_params=pltpu.CompilerParams(vmem_limit_bytes=40 * MIB),
        cost_estimate=cost_of(24),
        name="ffn",
    )(at, *c_pieces, *w_fin, *w_fout, x2, h3, g)
    out_pieces = outs[:narrow]
    dx2, gain3, keep_fin, send_fin, keep_fout, send_fout = outs[narrow:]
    ffn_sum = Scatter(at, [(keep_fin, send_fin), (keep_fout, send_fout)], fast, narrow)
    if fast:
        dx2 = after(dx2, ffn_sum.done)
    square = pltpu.VMEM((tokens, tokens), bf16)
    attend_scratch = [
        pltpu.VMEM((tokens, width), bf16), pltpu.VMEM((heads, 1, tokens), f32), square, square,
        pair_t, weights(1), sems,
    ]
    turned = pltpu.VMEM((width, tokens), bf16)
    grads = lambda count: shape_of((count, half, width), bf16)
    (dqkv2,) = call(
        functools.partial(attend_back_kernel, pieces=1, which=4, causal=False),
        [three], attend_scratch,
        at, w_second, dx2, o2, qkv2, cross_mask, peak2, inv2,
        loose=(1,), us=18, name="cross_back",
    )
    output = to_owners(out_pieces, dqkv2)
    ffn_sum.middle(dqkv2)
    if fast:
        dqkv2 = after(dqkv2, ffn_sum.done, output)
    outs = call(
        functools.partial(second_back_kernel, pieces=1, narrow=narrow, fold=fast),
        [piece16] * narrow + [row32, gain_out, grads(5), grads(5)],
        [turned, turned, pltpu.VMEM((tokens, width), bf16), weights(3), sems],
        at, w_second, dqkv2, dx2, o2, h2, m, x1, o1, g,
        loose=(1,), us=12, name="second_back",
    )
    gm_pieces = outs[:narrow]
    dx1, gain2, keep_second, send_second = outs[narrow:]
    ffn_sum.narrowed([], gain2)
    if fast:
        send_second = after(send_second, ffn_sum.done)
    second_sum = Scatter(at, [(keep_second, send_second)], fast, narrow)
    if fast:
        dx1 = after(dx1, second_sum.done, ffn_sum.done)
    dqkv1, ds = call(
        functools.partial(attend_back_kernel, pieces=1, which=0, causal=True),
        [three, shape_of((heads, tokens, tokens), bf16)], attend_scratch,
        at, w_second, table, dx1, o1, qkv1, index, peak1, inv1,
        loose=(1,), us=20, name="self_back",
    )
    (sum_fin, fin_rows, fin_part), (sum_fout, fout_rows, fout_part) = ffn_sum.total(dqkv1)
    second_sum.middle(dqkv1)
    if fast:
        dqkv1 = after(dqkv1, sum_fin, second_sum.done)
    outs = call(
        functools.partial(first_back_kernel, pieces=1, narrow=narrow, fold=fast),
        [piece16] * narrow + [gain_out, grads(3), grads(3)],
        [turned, turned, pltpu.VMEM((tokens, width), f32), weights(3), sems],
        at, w_first, dqkv1, h1, dx1, x, g,
        loose=(1,), us=9, name="first_back",
    )
    gx_pieces = outs[:narrow]
    gain1, keep_first, send_first = outs[narrow:]
    grad_memory = to_owners(gm_pieces, gain1)
    second_sum.narrowed([], gain1, grad_memory)
    (squares,) = call(
        square_kernel, [shape_of((16, 128), f32)], [],
        *(after(v, second_sum.done) for v in (attn_in, attn_out, ff_in, ff_out)), scalars=0,
        us=1, name="squares",
    )
    if fast:
        send_first = after(send_first, second_sum.done)
        keep_first = after(keep_first, squares)
    first_sum = Scatter(at, [(keep_first, send_first)], fast, narrow)
    if fast:
        ds = after(ds, first_sum.done, second_sum.done)
    (table_part,) = call(
        functools.partial(table_kernel, buckets=bucket_count),
        [shape_of((heads, 128), f32)],
        [pltpu.VMEM((heads * 16, bucket_count * 16), f32)], ds, index, scalars=0, us=11,
        name="table",
    )
    first_sum.middle(table_part)
    first_sum.narrowed([])
    ((sum_second, second_rows, second_part),) = second_sum.total(table_part)
    ((sum_first, first_rows, first_part),) = first_sum.total()
    grad_targets = to_owners([after(v, sum_first) for v in gx_pieces])
    parts = (gain1, gain2, gain3, first_part, second_part, fin_part, fout_part, table_part, squares)
    rows = sum(v.size for v in parts) // 128
    (tally,) = call(
        tally_kernel, [shape_of((-(-rows // 8) * 8, 128), f32)], [], *parts, scalars=0, us=1,
        name="tally",
    )
    tally = summed_all(tally, fast)
    (
        sum_in, sum_out, new_in, new_out, new_fin, new_fout, sum_gain, in_cols, out_cols, fin_cols,
        fout_cols, grad_table, new_table,
    ) = call(
        functools.partial(update_kernel, buckets=bucket_count),
        [
            shape_of(attn_in.shape, f32), shape_of(attn_out.shape, f32), shape_of(attn_in.shape, f32),
            shape_of(attn_out.shape, f32), shape_of(ff_in.shape, f32), shape_of(ff_out.shape, f32),
            shape_of((3, width), f32), shape_of((6, width), f32), shape_of((2, width), f32),
            shape_of((2, ff_width), f32), shape_of((1, width), f32),
            shape_of(bias_table.shape, f32), shape_of(bias_table.shape, f32),
        ],
        [], tally, sum_first, sum_second, sum_fin, sum_fout, first_rows, second_rows, fin_rows,
        fout_rows, attn_in, attn_out, ff_in, ff_out, table, scalars=0, us=3, name="update",
    )
    sum_gain = lax.dynamic_slice_in_dim(sum_gain, device * chunk, chunk, 1)
    in_rows = jnp.concatenate([first_rows, second_rows[1:4]])[:, :, 0]
    out_rows = jnp.stack([second_rows[0], second_rows[4]])[:, :, 0]
    return (
        output, grad_targets, grad_memory,
        sum_in, sum_out, sum_gain, sum_fin, sum_fout[0], grad_table,
        in_rows, in_cols, out_rows, out_cols, fin_rows[:, :, 0], fin_cols, fout_rows[0, :, 0],
        fout_cols[0], new_in, new_out, new_fin, new_fout, new_table,
    )


def solution(mesh):
    in_specs = (
        P("wide", "narrow", None),
        P("wide", "narrow", None),
        P("wide", "narrow", None),
        P("wide", "narrow"),
        P("wide", "narrow"),
        P("narrow", None),
        P(None, ("wide", "narrow"), None),
        P(None, ("wide", "narrow"), None),
        P(None, ("wide", "narrow")),
        P(None, ("wide", "narrow"), None),
        P(("wide", "narrow"), None),
        P(),
    )
    out_specs = (
        P("wide", "narrow", None),
        P("wide", "narrow", None),
        P("wide", "narrow", None),
        P(None, ("wide", "narrow"), None),
        P(None, ("wide", "narrow"), None),
        P(None, ("wide", "narrow")),
        P(None, ("wide", "narrow"), None),
        P(("wide", "narrow"), None),
        P(),
        P(None, ("wide", "narrow")),
        P(),
        P(None, ("wide", "narrow")),
        P(),
        P(None, ("wide", "narrow")),
        P(),
        P(("wide", "narrow")),
        P(),
        P(None, ("wide", "narrow"), None),
        P(None, ("wide", "narrow"), None),
        P(None, ("wide", "narrow"), None),
        P(("wide", "narrow"), None),
        P(),
    )
    return jax.shard_map(body, mesh=mesh, in_specs=in_specs, out_specs=out_specs, check_vma=False)
```

```python
import functools
import math

import jax
import jax.numpy as jnp
from jax import lax
from jax.experimental import pallas as pl
from jax.experimental.pallas import tpu as pltpu
from jax.sharding import PartitionSpec as P

bf16, f32 = jnp.bfloat16, jnp.float32
BOTH = ("wide", "narrow")
NEG = -1e9
TILE = 256
MIB = 1 << 20


def dot_nn(left, right):
    return lax.dot_general(left, right, (((1,), (0,)), ((), ())), preferred_element_type=f32)


def dot_nt(left, right):
    return lax.dot_general(left, right, (((1,), (1,)), ((), ())), preferred_element_type=f32)


def unit_of(values):
    inv_rms = lax.rsqrt(jnp.mean(values * values, axis=-1, keepdims=True) + 1e-06)
    return values * inv_rms, inv_rms


def norm_back(incoming, values, gain_row):
    unit, inv_rms = unit_of(values)
    scaled = incoming * gain_row
    inner = jnp.mean(scaled * unit, axis=-1, keepdims=True)
    return inv_rms * (scaled - unit * inner), jnp.sum(incoming * unit, axis=0, keepdims=True)


def tiles_of(width):
    return [(start, min(TILE, width - start)) for start in range(0, width, TILE)]


def project(left, w_ref, index, store):
    for start, size in tiles_of(w_ref.shape[2]):
        store(start, size, dot_nn(left, w_ref[index, :, start : start + size]))


def half_lanes(second):
    lane = lax.broadcasted_iota(jnp.int32, (1, 128), 1)
    return ((lane >= 64) == bool(second)).astype(bf16)


def biased(table_row, index):
    spread = jnp.broadcast_to(table_row, (index.shape[0], 128))
    return jnp.concatenate(
        [
            jnp.take_along_axis(
                spread, index[:, at : at + 128], axis=1, mode="promise_in_bounds"
            )
            for at in range(0, index.shape[1], 128)
        ],
        axis=1,
    )


def query_blocks(keys, queries, causal):
    return [
        (at, min(keys, at + TILE) if causal else keys) for at in range(0, queries, TILE)
    ]


def attend(qkv_ref, extra_ref, table_ref, o_ref, peak_ref, inv_ref, ot_ref):
    causal = table_ref is not None
    keys = qkv_ref.shape[1]

    def pair(at_pair, carry):
        lanes = pl.ds(pl.multiple_of(at_pair * 128, 128), 128)
        query, key, value = (qkv_ref[i, :, lanes] for i in range(3))
        value_t = value.T
        for second in range(2):
            head = at_pair * 2 + second
            key_half = key * half_lanes(second)
            for start, last in query_blocks(keys, keys, causal):
                part = slice(start, start + TILE)
                scores = dot_nt(key_half[:last], query[part])
                if causal:
                    scores += biased(table_ref[pl.ds(head, 1), :], extra_ref[:last, part])
                else:
                    scores += extra_ref[:last, part]
                peak = jnp.max(scores, axis=0, keepdims=True)
                grown = jnp.exp(scores - peak)
                inverse = 1.0 / jnp.sum(grown, axis=0, keepdims=True)
                mixed = dot_nn(value_t[second * 64 : second * 64 + 64, :last], grown.astype(bf16))
                ot_ref[second * 64 : second * 64 + 64, part] = mixed * inverse
                peak_ref[head, :, part] = peak
                inv_ref[head, :, part] = inverse
        o_ref[:, lanes] = ot_ref[...].T.astype(bf16)
        return carry

    lax.fori_loop(0, qkv_ref.shape[2] // 128, pair, 0)


def attend_back(
    qkv_ref, extra_ref, table_ref, do_ref, dsum_ref, peak_ref, inv_ref,
    dqkv_ref, p_ref, ds_ref, dqt_ref, ds_out,
):
    causal = table_ref is not None
    keys = qkv_ref.shape[1]
    first_half = lax.broadcasted_iota(jnp.int32, (1, 128), 1) < 64

    def pair(at_pair, carry):
        lanes = pl.ds(pl.multiple_of(at_pair * 128, 128), 128)
        query, key, value = (qkv_ref[i, :, lanes] for i in range(3))
        grad = do_ref[:, lanes]
        key_t = key.T
        for second in range(2):
            head = at_pair * 2 + second
            half = half_lanes(second)
            key_half, value_half = key * half, value * half
            for start, last in query_blocks(keys, keys, causal):
                part = slice(start, start + TILE)
                scores = dot_nt(key_half[:last], query[part])
                if causal:
                    scores += biased(table_ref[pl.ds(head, 1), :], extra_ref[:last, part])
                else:
                    scores += extra_ref[:last, part]
                weights = jnp.exp(scores - peak_ref[head, :, part]) * inv_ref[head, :, part]
                grad_weights = dot_nt(value_half[:last], grad[part])
                grad_scores = (weights * (grad_weights - dsum_ref[head, :, part])).astype(bf16)
                p_ref[:last, part] = weights.astype(bf16)
                ds_ref[:last, part] = grad_scores
                dqt_ref[second * 64 : second * 64 + 64, part] = dot_nn(
                    key_t[second * 64 : second * 64 + 64, :last], grad_scores
                )
            for start in range(0, keys, TILE):
                rows = slice(start, start + TILE)
                begin = start if causal else 0
                d_value = dot_nn(p_ref[rows, begin:], grad[begin:]).astype(bf16)
                d_key = dot_nn(ds_ref[rows, begin:], query[begin:]).astype(bf16)
                if second:
                    d_value = jnp.where(first_half, dqkv_ref[2, rows, lanes], d_value)
                    d_key = jnp.where(first_half, dqkv_ref[1, rows, lanes], d_key)
                dqkv_ref[2, rows, lanes] = d_value
                dqkv_ref[1, rows, lanes] = d_key
            if ds_out is not None:
                ds_out[head] = ds_ref[...]
        dqkv_ref[0, :, lanes] = dqt_ref[...].T.astype(bf16)
        return carry

    if causal:
        p_ref[...] = jnp.zeros_like(p_ref)
        ds_ref[...] = jnp.zeros_like(ds_ref)
    lax.fori_loop(0, qkv_ref.shape[2] // 128, pair, 0)


def head_sums(grad, mixed, dsum_ref):
    heads = dsum_ref.shape[0]
    product = grad.astype(f32) * mixed.astype(f32)
    width = product.shape[1]
    pick = (
        lax.broadcasted_iota(jnp.int32, (16, width), 1) // (width // heads)
        == lax.broadcasted_iota(jnp.int32, (16, width), 0)
    ).astype(f32)
    sums = lax.dot_general(
        pick, product, (((1,), (1,)), ((), ())),
        preferred_element_type=f32, precision=lax.Precision.HIGHEST,
    )
    for head in range(heads):
        dsum_ref[head] = sums[head : head + 1]


def square_kernel(*refs):
    row = 0
    for ref in refs[:-1]:
        parts = [ref[i] for i in range(ref.shape[0])] if len(ref.shape) == 3 else [ref[...]]
        for part in parts:
            total = jnp.sum(jnp.sum(part * part, axis=1, keepdims=True), axis=0, keepdims=True)
            refs[-1][row : row + 1, :] = jnp.broadcast_to(total, (1, 128))
            row += 1
    refs[-1][row:, :] = jnp.zeros((refs[-1].shape[0] - row, 128), f32)


def tally_kernel(gain1, gain2, gain3, first, second, fin, fout, table, squares, out_ref):
    at = 0
    rows = [ref[...] for ref in (gain1, gain2, gain3)]
    rows += [ref[i] for ref in (first, second, fin, fout) for i in range(ref.shape[0])]
    for row in rows:
        for start in range(0, row.shape[1], 128):
            out_ref[at : at + 1, :] = row[:, start : start + 128]
            at += 1
    for ref in (table, squares):
        out_ref[at : at + ref.shape[0], :] = ref[...]
        at += ref.shape[0]
    out_ref[at:, :] = jnp.zeros((out_ref.shape[0] - at, 128), f32)


def update_kernel(tally, first, second, fin, fout, first_rows, second_rows, fin_rows, fout_rows,
                  attn_in, attn_out, ff_in, ff_out, table, g_in, g_out, new_in, new_out, new_fin,
                  new_fout, gains, in_cols, out_cols, fin_cols, fout_cols, g_table, new_table,
                  *, buckets):
    at = 0

    def row(width):
        nonlocal at
        parts = [tally[at + i : at + i + 1, :] for i in range(width // 128)]
        at += width // 128
        return jnp.concatenate(parts, axis=1)

    width, ff_width = attn_in.shape[2], ff_in.shape[2]
    for i in range(3):
        gains[i : i + 1, :] = row(width)
    cols = [row(width) for _ in range(8)]
    cols += [row(ff_width), row(ff_width), row(width)]
    heads = table.shape[0]
    grad_t = tally[at : at + heads, :][:, :buckets]
    squares = at + heads
    sizes = [width * width] * 8 + [width * ff_width] * 3

    def step(grad, weight, rows, col, square, size):
        overall = jnp.sum(col, axis=1, keepdims=True)
        rms = jnp.sqrt(tally[squares + square : squares + square + 1, 0:1] / size + 1e-06)
        return weight - 0.3 * rms * grad * lax.rsqrt(rows * col / overall)

    places = [(first, first_rows, i, col) for i, col in enumerate(cols[:3])]
    places += [(second, second_rows, i, cols[3 + i]) for i in (1, 2, 3)]
    for i, (grad, rows, j, col) in enumerate(places):
        g_in[i] = grad[j]
        in_cols[i : i + 1, :] = col
        new_in[i] = step(grad[j], attn_in[i], rows[j], col, i, sizes[0])
    for i, j in ((0, 0), (1, 4)):
        col = cols[3 + j]
        g_out[i] = second[j]
        out_cols[i : i + 1, :] = col
        new_out[i] = step(second[j], attn_out[i], second_rows[j], col, 6 + i, sizes[0])
    for i in range(2):
        fin_cols[i : i + 1, :] = cols[8 + i]
        new_fin[i] = step(fin[i], ff_in[i], fin_rows[i], cols[8 + i], 8 + i, sizes[8])
    fout_cols[...] = cols[10]
    new_fout[...] = step(fout[0], ff_out[...], fout_rows[0], cols[10], 10, sizes[8])
    weight = table[:, :buckets]
    square = grad_t * grad_t + 1e-30
    by_bucket = jnp.sum(square, axis=0, keepdims=True)
    by_head = jnp.sum(square, axis=1, keepdims=True)
    overall = jnp.sum(by_head, axis=0, keepdims=True)
    mean = jnp.sum(jnp.sum(weight * weight, axis=1, keepdims=True), axis=0, keepdims=True)
    rms = jnp.sqrt(mean / (heads * buckets) + 1e-06)
    new_t = weight - 0.3 * rms * grad_t * lax.rsqrt(by_bucket * by_head / overall)
    g_table[...] = grad_t.T
    new_table[...] = new_t.T


def fold_rows(core, turned, turned_ref, out_ref, fold):
    if not fold:
        out_ref[...] = turned
        return
    turned_ref[...] = turned
    total = turned.shape[0]
    size = total // 8
    for group in range(4):
        for place, which in ((0, core), (1, 1 - core)):
            begin = pl.multiple_of(group * 2 * size + which * size, 16)
            to = place * (total // 2) + group * size
            out_ref[to : to + size, :] = turned_ref[pl.ds(begin, size), :]


def weight_grad(left_ref, right_ref, keep_ref, send_ref, index):
    half = left_ref.shape[0] // 2
    for start, size in tiles_of(right_ref.shape[1]):
        part = slice(start, start + size)
        right = right_ref[:, part]
        keep_ref[index, :, part] = dot_nn(left_ref[:half], right).astype(bf16)
        send_ref[index, :, part] = dot_nn(left_ref[half:], right).astype(bf16)


def start_weights(place, pieces, target_ref, sems, only=None):
    if len(pieces) == 2:
        size = pieces[0].shape[0] // 4
        pieces = [piece.at[pl.ds(d * size, size)] for d in range(4) for piece in pieces]
    elif len(pieces) == 4:
        size = pieces[1].shape[0]
        pieces = [
            many.at[pl.ds(d * size, size)] if d < 3 else last
            for d in range(4)
            for many, last in (pieces[:2], pieces[2:])
        ]
    rows = target_ref.shape[1] // len(pieces)
    copies = []
    for d, piece in enumerate(pieces):
        begin = pl.multiple_of((place ^ d) * rows, rows) if len(pieces) > 1 else 0
        source = piece if only is None else piece.at[only]
        copies.append(
            pltpu.make_async_copy(source, target_ref.at[:, pl.ds(begin, rows), :], sems.at[d])
        )
        copies[-1].start()
    return copies


def join_rows(place, pieces, target_ref):
    rows = pieces[0].shape[0]
    for d, piece in enumerate(pieces):
        target_ref[pl.ds(pl.multiple_of((place ^ d) * rows, 16), rows), :] = piece[...]


def join_blocks(place, pieces, target_ref):
    blocks = target_ref.shape[1] // TILE
    rows = target_ref.shape[0] // len(pieces)
    for d, piece in enumerate(pieces):
        to = pl.ds(pl.multiple_of((place ^ d) * rows, 16), rows)
        for j in range(blocks):
            target_ref[to, j * TILE : (j + 1) * TILE] = piece[j * rows : (j + 1) * rows, :]


def pack_kernel(at_ref, x_ref, m_ref, c_ref, seg_t_ref, seg_m_ref, *outs, narrow):
    local, width = x_ref.shape[1:]
    for d in range(narrow):
        first, memory, cot = outs[d], outs[narrow + d], outs[2 * narrow + d]
        row = at_ref[2] ^ d
        memory[...] = m_ref[row]
        cot[...] = c_ref[row]
        begin = 0
        for j in range(width // TILE):
            first[begin : begin + local, :] = x_ref[row, :, j * TILE : (j + 1) * TILE]
            begin += local
        for i, ref in enumerate((seg_t_ref, seg_m_ref)):
            seg = jnp.broadcast_to(ref[pl.ds(row, 1), :].astype(f32), (16, local))
            first[begin : begin + 16, i * local : (i + 1) * local] = seg.astype(bf16)


def split_rows(place, source_ref, pieces):
    rows = pieces[0].shape[0]
    for d, piece in enumerate(pieces):
        piece[...] = source_ref[pl.ds(pl.multiple_of((place ^ d) * rows, 16), rows), :].astype(
            piece.dtype
        )


def first_kernel(at_ref, *refs, pieces, narrow, chunk, bucket_count):
    x_refs, refs = refs[:narrow], refs[narrow:]
    w_refs, refs = refs[:pieces], refs[pieces:]
    near_ref = None
    if pieces == 1:
        near_ref, refs = refs[0], refs[1:]
    (allowed_ref, table_ref, w_ref, extra_ref, g_ref, x_ref, h_ref, qkv_ref, o_ref, peak_ref,
     inv_ref, ot_ref, sems) = refs
    copies = start_weights(at_ref[3], w_refs, w_ref, sems)
    join_blocks(at_ref[2], x_refs, x_ref)
    width = x_ref.shape[1]
    pick = (
        lax.broadcasted_iota(jnp.int32, (8, width), 1) % chunk
        == lax.broadcasted_iota(jnp.int32, (8, width), 0)
    ).astype(bf16)
    unit, _ = unit_of(x_ref[...].astype(f32))
    for copy in copies:
        copy.wait()
    gains = dot_nn(pick, w_ref[3])
    g_ref[...] = gains
    if near_ref is None:
        tokens = extra_ref.shape[0]
        held = w_ref[3, :, :tokens].astype(f32)
        groups = width // (narrow * chunk)
        share = tokens // (narrow * groups)
        near = jnp.concatenate(
            [
                held[(w * narrow + n + 1) * chunk - share : (w * narrow + n + 1) * chunk]
                for n in range(narrow)
                for w in range(groups)
            ],
            axis=0,
        ).T
    else:
        near = near_ref[...].astype(f32)
    extra_ref[...] = jnp.where(
        allowed_ref[...] > 0.0, near, float(bucket_count)
    ).astype(jnp.int32)
    h_ref[...] = (unit * gains[0:1]).astype(bf16)
    for i in range(3):
        def store(start, size, product, i=i):
            qkv_ref[i, :, start : start + size] = product.astype(bf16)

        project(h_ref[...], w_ref, i, store)
    attend(qkv_ref, extra_ref, table_ref, o_ref, peak_ref, inv_ref, ot_ref)


def second_kernel(at_ref, *refs, pieces, narrow):
    m_refs, refs = refs[:narrow], refs[narrow:]
    w_refs, refs = refs[:pieces], refs[pieces:]
    (x_ref, o1_ref, extra_ref, g_ref, w_ref, m_ref, x1_ref, h_ref, qkv_ref, o_ref, x2_ref, h3_ref,
     peak_ref, inv_ref, ot_ref, sems) = refs
    copies = start_weights(at_ref[3], w_refs, w_ref, sems)
    join_rows(at_ref[2], m_refs, m_ref)
    for copy in copies:
        copy.wait()

    def store_x1(start, size, product):
        part = slice(start, start + size)
        x1_ref[:, part] = x_ref[:, part].astype(f32) + product

    project(o1_ref[...], w_ref, 0, store_x1)
    unit, _ = unit_of(x1_ref[...])
    h_ref[...] = (unit * g_ref[1:2, :]).astype(bf16)
    for i in range(3):
        def store(start, size, product, i=i):
            qkv_ref[i, :, start : start + size] = product.astype(bf16)

        project(m_ref[...] if i else h_ref[...], w_ref, i + 1, store)
    attend(qkv_ref, extra_ref, None, o_ref, peak_ref, inv_ref, ot_ref)

    def store_x2(start, size, product):
        part = slice(start, start + size)
        x2_ref[:, part] = x1_ref[:, part] + product

    project(o_ref[...], w_ref, 4, store_x2)
    unit, _ = unit_of(x2_ref[...])
    h3_ref[...] = (unit * g_ref[2:3, :]).astype(bf16)


def prepare_kernel(at_ref, *refs, narrow, skip):
    in_refs, (allowed_ref, mask_ref, seg_ref) = refs[:narrow], refs[narrow:]
    tokens = mask_ref.shape[0]
    local = tokens // narrow
    for d, ref in enumerate(in_refs):
        lanes = pl.ds(pl.multiple_of((at_ref[2] ^ d) * local, 128), local)
        tail = ref[skip : skip + 16, :].astype(f32)
        seg_ref[0:8, lanes] = tail[:8, :local]
        seg_ref[8:16, lanes] = tail[:8, local : 2 * local]
    seg = seg_ref[...]
    seg_t = seg.T
    key = lax.broadcasted_iota(jnp.int32, (tokens, tokens), 0)
    query = lax.broadcasted_iota(jnp.int32, (tokens, tokens), 1)
    allowed = (key <= query) & (seg_t[:, 0:1] == seg[0:1, :])
    allowed_ref[...] = jnp.where(allowed, 1.0, 0.0)
    mask_ref[...] = jnp.where(seg_t[:, 8:9] == seg[0:1, :], 0.0, NEG)


def order_kernel(at_ref, *refs, outs):
    pieces, out_refs = refs[:-outs], refs[-outs:]
    for d, piece in enumerate(pieces):
        if piece.ndim == 2:
            out_refs[0][at_ref[2] ^ d] = piece[...]
            continue
        begin = 0
        for out_ref in out_refs:
            size = out_ref.shape[0]
            out_ref[:, at_ref[2] ^ d] = piece[begin : begin + size]
            begin += size


def read_part(refs, group):
    if len(refs) == 1:
        count, rows, cols = refs[0].shape
        rows //= 4
        part = pl.ds(pl.multiple_of(group * rows, 16), rows)
        return refs[0][:, part, :].astype(f32).reshape(count * rows, cols)
    fin, fout = refs
    rows, rows_out = fin.shape[1] // 4, fout.shape[1] // 4
    part = pl.ds(pl.multiple_of(group * rows, 16), rows)
    part_out = pl.ds(pl.multiple_of(group * rows_out, 16), rows_out)
    pieces = [
        fin[i, part, at : at + TILE].astype(f32)
        for i in range(fin.shape[0])
        for at in range(0, fin.shape[2], TILE)
    ]
    pieces += [
        fout[0, part_out, at : at + TILE].astype(f32) for at in range(0, fout.shape[2], TILE)
    ]
    return jnp.concatenate(pieces, axis=0)


def spread_kernel(at_ref, *refs, count):
    keeps, recvs = refs[:count], refs[count : 2 * count]
    own_ref, kept_x, kept_y, to_x, to_y = refs[2 * count :]
    half = own_ref.shape[0] // 2
    for d in range(4):
        total = read_part(keeps, at_ref[1] ^ d) + read_part(recvs, at_ref[1] ^ d)
        if d == 0:
            own_ref[...] = total
        elif d == 1:
            to_x[0] = total[:half].astype(bf16)
            kept_x[...] = total[half:]
        elif d == 2:
            to_y[0] = total[half:].astype(bf16)
            kept_y[...] = total[:half]
        else:
            to_x[1] = total[:half].astype(bf16)
            to_y[1] = total[half:].astype(bf16)


def middle_kernel(own_ref, kept_x, kept_y, from_x, from_y, sum_ref, to_x, to_y):
    half = own_ref.shape[0] // 2
    sum_ref[:half, :] = own_ref[:half, :] + from_x[0].astype(f32)
    sum_ref[half:, :] = own_ref[half:, :] + from_y[0].astype(f32)
    to_y[...] = (kept_y[...] + from_x[1].astype(f32)).astype(bf16)
    to_x[...] = (kept_x[...] + from_y[1].astype(f32)).astype(bf16)


def narrow_kernel(at_ref, own_ref, from_x, from_y, *refs, narrow, spots):
    riders, outs, sum_ref = refs[: -narrow - 1], refs[-narrow - 1 : -1], refs[-1]
    half = own_ref.shape[0] // 2
    sum_ref[:half, :] = own_ref[:half, :] + from_y[...].astype(f32)
    sum_ref[half:, :] = own_ref[half:, :] + from_x[...].astype(f32)
    for d, out_ref in enumerate(outs):
        place = at_ref[2] ^ d
        share = jnp.concatenate(
            [
                sum_ref[pl.ds(start + pl.multiple_of(place * rows, 8), rows), :]
                for start, rows in spots
            ],
            axis=0,
        ).astype(out_ref.dtype)
        ahead = out_ref.shape[0] - share.shape[0]
        if ahead:
            rider, cols = riders[d - 1], out_ref.shape[1]
            rows = rider.shape[0]
            for j in range(rider.shape[1] // cols):
                out_ref[j * rows : (j + 1) * rows, :] = rider[:, j * cols : (j + 1) * cols]
        out_ref[ahead:, :] = share


def join_kernel(at_ref, *refs):
    own, pieces, out_ref = refs[0], refs[1:-1], refs[-1]
    out_ref[at_ref[2]] = own[...]
    rows, width = own.shape
    for d, piece in enumerate(pieces):
        cols = piece.shape[1]
        for j in range(width // cols):
            out_ref[at_ref[2] ^ (d + 1), :, j * cols : (j + 1) * cols] = piece[
                j * rows : (j + 1) * rows, :
            ]


def total_kernel(*refs, narrow):
    total = refs[0][...]
    for ref in refs[1:narrow]:
        total = total + ref[ref.shape[0] - total.shape[0] :, :].astype(f32)
    outs = refs[narrow:]
    at = 0
    for total_ref, rows_ref, cols_ref in zip(*(outs[i::3] for i in range(3))):
        count, rows, cols = total_ref.shape
        block = total.shape[1]
        if cols == block:
            total_ref[...] = total[at : at + count * rows].reshape(count, rows, cols)
            at += count * rows
        else:
            for i in range(count):
                for j in range(cols // block):
                    total_ref[i, :, j * block : (j + 1) * block] = total[at : at + rows]
                    at += rows
        squares = total_ref[...]
        squares = squares * squares + 1e-30
        rows_ref[...] = jnp.sum(squares, axis=-1, keepdims=True)
        cols_ref[...] = jnp.sum(squares, axis=1, keepdims=True)


def ffn_kernel(at_ref, *refs, fold, narrow, pieces, first_out):
    c_refs, refs = refs[:narrow], refs[narrow:]
    fin_refs, refs = refs[:pieces], refs[pieces:]
    fout_refs, refs = refs[:pieces], refs[pieces:]
    (x2_ref, h_ref, g_ref), refs = refs[:3], refs[3:]
    out_refs, refs = refs[:narrow], refs[narrow:]
    (dx_ref, dg_ref, kin_ref, sin_ref, kout_ref, sout_ref, acc_ref, dh_ref, turned_ref, ht_ref,
     gout_ref, c_ref, fin_ref, fout_ref, fin_sems, fout_sems) = refs
    step, steps = pl.program_id(0), pl.num_programs(0)
    core = at_ref[0]

    @pl.when(step == 0)
    def _():
        copies = start_weights(at_ref[3], fin_refs, fin_ref, fin_sems, pl.ds(0, fin_ref.shape[0]))
        copies += start_weights(
            at_ref[3], fout_refs, fout_ref, fout_sems, pl.ds(first_out, fout_ref.shape[0])
        )
        join_rows(at_ref[2], c_refs, c_ref)
        acc_ref[...] = x2_ref[...]
        dh_ref[...] = jnp.zeros_like(dh_ref)
        fold_rows(core, h_ref[...].T, turned_ref, ht_ref, fold)
        for copy in copies:
            copy.wait()

    hidden_in, cot = h_ref[...], c_ref[...]
    size = fin_ref.shape[2]
    blocks = gout_ref.shape[0] // size
    for block in range(blocks):
        part = slice(block * size, (block + 1) * size)
        at_gate = step * blocks + block
        at_up = fin_ref.shape[0] // 2 + at_gate
        gate = dot_nn(hidden_in, fin_ref[at_gate])
        up = dot_nn(hidden_in, fin_ref[at_up])
        square = gate * gate
        bent = jnp.tanh(0.7978845608028654 * (gate + 0.044715 * square * gate))
        plus = 0.5 * (1.0 + bent)
        act = gate * plus
        slope = plus + 0.5 * gate * (1.0 - bent * bent) * (
            0.7978845608028654 + (3 * 0.044715 * 0.7978845608028654) * square
        )
        hidden = (act * up).astype(bf16)
        down_rows = pl.ds(pl.multiple_of(at_gate * size, size), size)
        down = jnp.concatenate(
            [fout_ref[i, down_rows, :] for i in range(fout_ref.shape[0])], axis=1
        )
        acc_ref[...] += dot_nn(hidden, down)
        grad = dot_nt(cot, down)
        d_gate = (grad * up * slope).astype(bf16)
        d_up = (grad * act).astype(bf16)
        dh_ref[...] += dot_nt(d_gate, fin_ref[at_gate]) + dot_nt(d_up, fin_ref[at_up])
        half = ht_ref.shape[0] // 2
        for index, right in ((0, d_gate), (1, d_up)):
            product = dot_nn(ht_ref[...], right).astype(bf16)
            kin_ref[index, :, part] = product[:half]
            sin_ref[index, :, part] = product[half:]
        gout_ref[part, :] = dot_nn(hidden.T, cot).astype(bf16)
    rows = gout_ref.shape[0] // 2
    kept = pl.multiple_of(core * rows, 16) if fold else 0
    sent = pl.multiple_of((1 - core) * rows, 16) if fold else rows
    kout_ref[...] = gout_ref[pl.ds(kept, rows), :]
    sout_ref[...] = gout_ref[pl.ds(sent, rows), :]

    @pl.when(step == steps - 1)
    def _():
        split_rows(at_ref[2], acc_ref, out_refs)
        back, d_gain = norm_back(dh_ref[...], x2_ref[...], g_ref[2:3, :])
        dx_ref[...] = cot.astype(f32) + back
        dg_ref[...] = d_gain


def attend_back_kernel(at_ref, *refs, pieces, which, causal):
    w_refs, refs = refs[:pieces], refs[pieces:]
    table_ref = None
    if causal:
        table_ref, refs = refs[0], refs[1:]
    dx_ref, o_ref, qkv_ref, extra_ref, peak_ref, inv_ref, dqkv_ref = refs[:7]
    ds_out, refs = (refs[7], refs[8:]) if causal else (None, refs[7:])
    do_ref, dsum_ref, p_ref, ds_ref, dqt_ref, w_ref, sems = refs
    copies = start_weights(at_ref[3], w_refs, w_ref, sems, pl.ds(which, 1))
    branch = dx_ref[...].astype(bf16)
    for copy in copies:
        copy.wait()
    for start, size in tiles_of(o_ref.shape[1]):
        do_ref[:, start : start + size] = dot_nt(
            branch, w_ref[0, start : start + size, :]
        ).astype(bf16)
    head_sums(do_ref[...], o_ref[...], dsum_ref)
    attend_back(qkv_ref, extra_ref, table_ref, do_ref, dsum_ref, peak_ref, inv_ref, dqkv_ref,
                p_ref, ds_ref, dqt_ref, ds_out)


def second_back_kernel(at_ref, *refs, pieces, narrow, fold):
    w_refs, refs = refs[:pieces], refs[pieces:]
    (dqkv_ref, dx2_ref, o_ref, h_ref, m_ref, x1_ref, o1_ref, g_ref), refs = refs[:8], refs[8:]
    gm_refs, refs = refs[:narrow], refs[narrow:]
    (dx1_ref, dg_ref, keep_ref, send_ref, turned_ref, left_ref, gm_ref, w_ref, sems) = refs
    core = at_ref[0]
    copies = start_weights(at_ref[3], w_refs, w_ref, sems, pl.ds(1, 3))
    gm_ref[...] = dx2_ref[...].astype(bf16)
    fold_rows(core, o_ref[...].T, turned_ref, left_ref, fold)
    for copy in copies:
        copy.wait()
    weight_grad(left_ref, gm_ref, keep_ref, send_ref, 4)
    fold_rows(core, h_ref[...].T, turned_ref, left_ref, fold)
    weight_grad(left_ref, dqkv_ref.at[0], keep_ref, send_ref, 1)
    fold_rows(core, m_ref[...].T, turned_ref, left_ref, fold)
    for i in (1, 2):
        weight_grad(left_ref, dqkv_ref.at[i], keep_ref, send_ref, i + 1)
    for start, size in tiles_of(o_ref.shape[1]):
        rows = slice(start, start + size)
        gm_ref[:, rows] = (
            dot_nt(dqkv_ref[1], w_ref[1, rows, :]) + dot_nt(dqkv_ref[2], w_ref[2, rows, :])
        ).astype(bf16)
        dx1_ref[:, rows] = dot_nt(dqkv_ref[0], w_ref[0, rows, :])
    split_rows(at_ref[2], gm_ref, gm_refs)
    back, d_gain = norm_back(dx1_ref[...], x1_ref[...], g_ref[1:2, :])
    d_x1 = dx2_ref[...] + back
    dx1_ref[...] = d_x1
    dg_ref[...] = d_gain
    gm_ref[...] = d_x1.astype(bf16)
    fold_rows(core, o1_ref[...].T, turned_ref, left_ref, fold)
    weight_grad(left_ref, gm_ref, keep_ref, send_ref, 0)


def first_back_kernel(at_ref, *refs, pieces, narrow, fold):
    w_refs, refs = refs[:pieces], refs[pieces:]
    (dqkv_ref, h_ref, dx1_ref, x_ref, g_ref), refs = refs[:5], refs[5:]
    gx_refs, refs = refs[:narrow], refs[narrow:]
    dg_ref, keep_ref, send_ref, turned_ref, left_ref, dh_ref, w_ref, sems = refs
    copies = start_weights(at_ref[3], w_refs, w_ref, sems, pl.ds(0, 3))
    fold_rows(at_ref[0], h_ref[...].T, turned_ref, left_ref, fold)
    for copy in copies:
        copy.wait()
    for i in range(3):
        weight_grad(left_ref, dqkv_ref.at[i], keep_ref, send_ref, i)
    for start, size in tiles_of(h_ref.shape[1]):
        rows = slice(start, start + size)
        dh_ref[:, rows] = (
            dot_nt(dqkv_ref[0], w_ref[0, rows, :])
            + dot_nt(dqkv_ref[1], w_ref[1, rows, :])
            + dot_nt(dqkv_ref[2], w_ref[2, rows, :])
        )
    back, d_gain = norm_back(dh_ref[...], x_ref[...].astype(f32), g_ref[0:1, :])
    dh_ref[...] = dx1_ref[...] + back
    split_rows(at_ref[2], dh_ref, gx_refs)
    dg_ref[...] = d_gain


def table_kernel(ds_ref, index_ref, out_ref, acc_ref, *, buckets):
    heads, keys, queries = ds_ref.shape
    acc_ref[...] = jnp.zeros_like(acc_ref)

    def group(at, begin):
        rows = pl.ds(pl.multiple_of(at * 16, 16), 16)
        index = index_ref[rows, begin:]
        grads = ds_ref[:, rows, begin:].reshape(heads * 16, queries - begin)
        hot = jnp.concatenate(
            [(index == b).astype(f32).astype(bf16) for b in range(buckets)], axis=0
        )
        acc_ref[...] += dot_nt(grads, hot)

    half = keys // 32
    lax.fori_loop(0, half, lambda at, carry: (group(at, 0), carry)[1], 0)
    lax.fori_loop(half, 2 * half, lambda at, carry: (group(at, queries // 2), carry)[1], 0)
    shape = acc_ref.shape
    same = (
        lax.broadcasted_iota(jnp.int32, shape, 0) % 16
        == lax.broadcasted_iota(jnp.int32, shape, 1) % 16
    )
    kept = jnp.where(same, acc_ref[...], 0.0).reshape(heads, 16, shape[1]).sum(axis=1)
    gather = (
        lax.broadcasted_iota(jnp.int32, (shape[1], 128), 0) // 16
        == lax.broadcasted_iota(jnp.int32, (shape[1], 128), 1)
    ).astype(f32)
    out_ref[...] = lax.dot_general(
        kept, gather, (((1,), (0,)), ((), ())),
        preferred_element_type=f32, precision=lax.Precision.HIGHEST,
    )


def cost_of(us):
    return pl.CostEstimate(flops=int(us * 1.15e9), bytes_accessed=MIB, transcendentals=0)


def room_for(arrays, scratch):
    size = sum(v.size * v.dtype.itemsize for v in arrays)
    for ref in scratch:
        shape = getattr(ref, "shape", ())
        if ref.memory_space == pltpu.VMEM:
            rows = -(-shape[-2] // 8) * 8
            size += math.prod(shape[:-2]) * rows * shape[-1] * jnp.dtype(ref.dtype).itemsize
    return (size // MIB + 8) * MIB


def call(kernel, outs, scratch, *args, scalars=1, loose=(), us=2, name=None):
    spaces = [
        pltpu.SMEM if i < scalars else pl.ANY if i in loose else pltpu.VMEM
        for i in range(len(args))
    ]
    return pl.pallas_call(
        kernel,
        out_shape=outs,
        in_specs=[pl.BlockSpec(memory_space=space) for space in spaces],
        out_specs=[pl.BlockSpec(memory_space=pltpu.VMEM)] * len(outs),
        scratch_shapes=scratch,
        compiler_params=pltpu.CompilerParams(
            vmem_limit_bytes=room_for(
                [v for v, space in zip(args, spaces) if space == pltpu.VMEM] + list(outs), scratch
            )
        ),
        cost_estimate=cost_of(us),
        name=name,
    )(*args)


def shape_of(shape, dtype):
    return jax.ShapeDtypeStruct(tuple(shape), dtype)


def permuted(value, wide_bits, narrow_bits):
    wide, narrow = lax.axis_size("wide"), lax.axis_size("narrow")
    pairs = [
        (w * narrow + n, (w ^ wide_bits) * narrow + (n ^ narrow_bits))
        for w in range(wide)
        for n in range(narrow)
    ]
    return lax.ppermute(value, BOTH, pairs)


def after(value, *done):
    return lax.optimization_barrier((value, *done))[0]


def ordered(at, pieces, shares=None):
    first = pieces[0]
    if first.ndim == 2:
        shapes = [(len(pieces),) + first.shape]
    else:
        shapes = [(k, len(pieces)) + first.shape[1:] for k in shares]
    outs = [shape_of(shape, first.dtype) for shape in shapes]
    return call(
        functools.partial(order_kernel, outs=len(outs)), outs, [], at, *pieces, us=1, name="order"
    )


def local_stats(gradient):
    squares = gradient * gradient + 1e-30
    return (jnp.sum(squares, axis=-1, keepdims=True), jnp.sum(squares, axis=-2, keepdims=True))


class Scatter:
    def __init__(self, at, pairs, fast, narrow):
        self.at, self.fast, self.narrow, self.pairs = at, fast, narrow, pairs
        self.done = pairs[0][0]
        if not fast:
            return
        keeps = [keep.reshape(-1, keep.shape[1], keep.shape[2]) for keep, _ in pairs]
        sends = [send for _, send in pairs]
        if len(pairs) == 2:
            keeps[1] = keeps[1].reshape(1, -1, keeps[1].shape[2])
            sends[1] = sends[1].reshape(keeps[1].shape)
        self.shapes = [(k.shape[0], k.shape[1] // 4, k.shape[2]) for k in keeps]
        size = sum(k.size for k in keeps) // 4
        cols = TILE if len(pairs) == 2 else keeps[0].shape[2]
        self.rows, self.cols = size // cols, cols
        half = (self.rows // 2, cols)
        recvs = [permuted(send, 1, 0) for send in sends]
        self.own, self.kept_x, self.kept_y, to_x, to_y = call(
            functools.partial(spread_kernel, count=len(pairs)),
            [shape_of((self.rows, cols), f32), shape_of(half, f32), shape_of(half, f32),
             shape_of((2,) + half, bf16), shape_of((2,) + half, bf16)],
            [], at, *keeps, *recvs, us=3, name="spread",
        )
        self.out = (to_x, to_y)
        self.done = self.own

    def middle(self, *done):
        if not self.fast:
            return
        self.own = after(self.own, *done)
        half = (self.rows // 2, self.cols)
        from_x, from_y = permuted(self.out[0], 2, 0), permuted(self.out[1], 4, 0)
        self.own, to_x, to_y = call(
            middle_kernel,
            [shape_of((self.rows, self.cols), f32), shape_of(half, bf16), shape_of(half, bf16)],
            [], self.own, self.kept_x, self.kept_y, from_x, from_y, scalars=0, name="middle",
        )
        self.out = (to_x, to_y)
        self.done = self.own

    def narrowed(self, riders, *done):
        self.riders = riders
        if not self.fast:
            return
        self.own = after(self.own, *done)
        from_x, from_y = permuted(self.out[0], 2, 0), permuted(self.out[1], 4, 0)
        if len(self.shapes) == 2:
            (k, rows, cols), (_, rows_out, cols_out) = self.shapes
            sizes = [rows] * (k * cols // TILE) + [rows_out] * (cols_out // TILE)
        else:
            sizes = [self.shapes[0][1]] * self.shapes[0][0]
        spots, begin = [], 0
        for size in sizes:
            spots.append((begin, size // self.narrow))
            begin += size
        share = self.rows // self.narrow
        ahead = riders[0].size // self.cols if riders else 0
        self.out = call(
            functools.partial(narrow_kernel, narrow=self.narrow, spots=spots),
            [
                shape_of((share + ahead, self.cols) if d else (share, self.cols), bf16 if d else f32)
                for d in range(self.narrow)
            ],
            [pltpu.VMEM((self.rows, self.cols), f32)], self.at, self.own, from_x, from_y,
            *riders[1:], name="narrow",
        )
        self.done = self.out[0]

    def total(self, *done):
        if not self.fast:
            results = []
            for keep, send in self.pairs:
                whole = jnp.concatenate([keep, send], axis=1)
                if keep.shape[0] == 4:
                    whole = whole.reshape(1, -1, whole.shape[2])
                total = lax.psum_scatter(whole, BOTH, scatter_dimension=1, tiled=True).astype(f32)
                results.append((total, *local_stats(total)))
            return results
        parts = [permuted(v, 0, d) if d else v for d, v in enumerate(self.out)]
        parts[0] = after(parts[0], *done)
        if self.riders:
            rider = self.riders[0]
            (self.ridden,) = call(
                join_kernel, [shape_of((self.narrow,) + rider.shape, bf16)], [], self.at,
                after(rider, *done), *parts[1:], name="join",
            )
        outs = []
        for k, rows, cols in self.shapes:
            rows //= self.narrow
            outs += [
                shape_of((k, rows, cols), f32), shape_of((k, rows, 1), f32),
                shape_of((k, 1, cols), f32),
            ]
        flat = call(
            functools.partial(total_kernel, narrow=self.narrow), outs, [], *parts, scalars=0,
            name="total",
        )
        return [
            tuple(flat[3 * i : 3 * i + 3])
            for i in range(len(self.shapes))
        ]


def summed_all(flat, fast):
    if not fast:
        return lax.psum(flat, BOTH)
    flat = flat + permuted(flat, 1, 0)
    flat = (flat + permuted(flat, 2, 0)) + (permuted(flat, 4, 0) + permuted(flat, 6, 0))
    return (flat + permuted(flat, 0, 1)) + (permuted(flat, 0, 2) + permuted(flat, 0, 3))


def body(
    targets, memory, cotangent, target_segments, memory_segments, buckets,
    attn_in, attn_out, gains, ff_in, ff_out, bias_table,
):
    wide, narrow = lax.axis_size("wide"), lax.axis_size("narrow")
    at_wide, at_narrow = lax.axis_index("wide"), lax.axis_index("narrow")
    fast = wide == 8 and narrow == 4
    at = jnp.stack([at_wide % 2, at_wide // 2, at_narrow, at_wide]).astype(jnp.int32)
    width, ff_width = attn_in.shape[2], ff_in.shape[2]
    bucket_count, heads = bias_table.shape
    chunk = gains.shape[1]
    local_tokens = targets.shape[1]
    tokens = local_tokens * narrow
    assert targets.shape[0] == narrow

    def over_narrow(pieces):
        return [permuted(v, 0, d) if d else v for d, v in enumerate(pieces)]

    def to_owners(pieces, *done):
        pieces = over_narrow(pieces)
        return ordered(at, [after(pieces[0], *done)] + pieces[1:])[0]

    device = at_wide * narrow + at_narrow
    gain_rows = lax.dynamic_update_slice(
        jnp.zeros((chunk, width), bf16), gains.astype(bf16), (0, device * chunk)
    )
    if fast:
        share = local_tokens // wide
        held = lax.dynamic_slice_in_dim(buckets, at_wide * share, share, 0).astype(bf16)
        gain_rows = lax.dynamic_update_slice(gain_rows, held, (chunk - share, 0))
    first_local = jnp.concatenate([attn_in[:3].astype(bf16), gain_rows[None]])
    second_local = jnp.concatenate([attn_out[:1], attn_in[3:], attn_out[1:]]).astype(bf16)
    piece16 = shape_of((local_tokens, width), bf16)
    near_rows = local_tokens * width // TILE + 16
    packed = call(
        functools.partial(pack_kernel, narrow=narrow),
        [shape_of((near_rows, TILE), bf16)] * narrow
        + [piece16] * (2 * narrow),
        [], at, targets, memory, cotangent, target_segments, memory_segments,
        us=4, name="pack",
    )
    near, m_out, c_out = packed[:narrow], packed[narrow : 2 * narrow], packed[2 * narrow :]
    lanes = TILE
    fin_blocks = ff_in.astype(bf16).reshape(2, chunk, ff_width // lanes, lanes)
    fin_blocks = fin_blocks.transpose(0, 2, 1, 3).reshape(-1, chunk, lanes)
    out_rows_here = ff_out.shape[0]
    fout_blocks = ff_out.astype(bf16).reshape(out_rows_here, width // lanes, lanes)
    fout_blocks = fout_blocks.transpose(1, 0, 2).reshape(-1, chunk, lanes)
    fin_count, fout_count = fin_blocks.shape[0], fout_blocks.shape[0]
    ffn_local = jnp.concatenate([fin_blocks, fout_blocks])

    def regroup_out(stack, owners):
        stack = stack.reshape(fout_count, owners, chunk, lanes).transpose(1, 0, 2, 3)
        stack = stack.reshape(owners, width // lanes, out_rows_here, lanes)
        return stack.transpose(1, 0, 2, 3).reshape(width // lanes, -1, lanes)

    def over_plane(stack):
        from_x, from_y = permuted(stack, 2, 0), permuted(stack, 4, 0)
        half = stack.shape[0] // 2
        begin, end = from_x[:half], from_y[half:]
        return [stack, from_x, from_y, permuted(begin, 4, 0), permuted(end, 2, 0)]

    def with_other_core(plane, *done):
        own = jnp.concatenate([after(plane[0], *done)] + plane[1:])
        return [own, permuted(own, 1, 0)]

    if fast:
        first_near = over_narrow([first_local] * narrow)
        first_near[0] = after(first_near[0], near[0])
        (stack,) = ordered(at, first_near, (4,))
        near = [near[0]] + [after(v, stack) for v in near[1:]]
        plane_first = over_plane(stack.reshape(4, -1, width))
        held_out = []
    else:
        w_first = [lax.all_gather(first_local, BOTH, axis=1, tiled=True)]
        w_second = [lax.all_gather(second_local, BOTH, axis=1, tiled=True)]
        held_out = [lax.all_gather(buckets.astype(bf16), "narrow", axis=0, tiled=True).T]
    near = over_narrow(near)
    allowed, cross_mask = call(
        functools.partial(
            prepare_kernel, narrow=narrow, skip=local_tokens * width // TILE,
        ),
        [shape_of((tokens, tokens), f32), shape_of((tokens, tokens), f32)],
        [pltpu.VMEM((16, tokens), f32)],
        at, *near, us=2, name="prepare",
    )
    if fast:
        w_first = with_other_core(plane_first, allowed)
        ffn_near = over_narrow([after(ffn_local, allowed)] * narrow)
    table = jnp.concatenate(
        [bias_table.T, jnp.full((heads, 128 - bucket_count), NEG, f32)], axis=1
    )
    row16 = shape_of((tokens, width), bf16)
    row32 = shape_of((tokens, width), f32)
    three = shape_of((3, tokens, width), bf16)
    stat = shape_of((heads, 1, tokens), f32)
    gain_out = shape_of((1, width), f32)
    pair_t = pltpu.VMEM((128, tokens), f32)
    pieces = len(w_first)
    weights = lambda count: pltpu.VMEM((count, width, width), bf16)
    sems = pltpu.SemaphoreType.DMA((8,))
    stack_of = lambda count: shape_of((count, width, width), bf16)
    w_first, index, g, x, h1, qkv1, o1, peak1, inv1 = call(
        functools.partial(
            first_kernel, pieces=pieces, narrow=narrow, chunk=chunk, bucket_count=bucket_count
        ),
        [stack_of(4), shape_of((tokens, tokens), jnp.int32), shape_of((8, width), f32), row16,
         row16, three, row16, stat, stat],
        [pair_t, sems],
        at, *near, *w_first, *held_out, allowed, table,
        loose=range(1 + narrow, 1 + narrow + pieces), us=16, name="first",
    )
    if fast:
        ffn_near[0] = after(ffn_near[0], h1)
        (stack,) = ordered(at, ffn_near, (fin_count + fout_count,))
        second_near = over_narrow([after(second_local, stack)] * narrow)
        stack = stack.reshape(fin_count + fout_count, -1, lanes)
        stack_out = regroup_out(stack[fin_count:], narrow).reshape(fout_count, -1, lanes)
        stack = jnp.concatenate([stack[:fin_count], stack_out])
        plane_ffn = over_plane(stack)
        second_near[0] = after(second_near[0], plane_ffn[1], plane_ffn[2])
        (stack,) = ordered(at, second_near, (5,))
        m_out = [m_out[0]] + [after(v, *second_near[1:]) for v in m_out[1:]]
        plane_second = over_plane(stack.reshape(5, -1, width))
    m_pieces = over_narrow(m_out)
    if fast:
        w_second = with_other_core(plane_second, *m_pieces[1:])
        ffn_near = with_other_core(plane_ffn[:3], *m_pieces[1:])
        o1 = after(o1, ffn_near[1])
        c_out = [c_out[0]] + [after(v, *m_pieces[1:]) for v in c_out[1:]]
    c_pieces = over_narrow(c_out)
    w_second, m, x1, h2, qkv2, o2, x2, h3, peak2, inv2 = call(
        functools.partial(second_kernel, pieces=pieces, narrow=narrow),
        [stack_of(5), row16, row32, row16, three, row16, row32, row16, stat, stat],
        [pair_t, sems],
        at, *m_pieces, *w_second, x, o1, cross_mask, g,
        loose=range(1 + narrow, 1 + narrow + pieces), us=21, name="second",
    )

    if fast:
        ffn_pieces = ffn_near + with_other_core(plane_ffn[3:], x2, *c_pieces[1:])
        ffn_pieces = [ffn_pieces[i] for i in (0, 2, 1, 3)]
        w_fin = ffn_pieces
        w_fout = [v.reshape(-1, narrow * out_rows_here, lanes) for v in ffn_pieces]
    else:
        every = lax.all_gather(ffn_local, BOTH, axis=1, tiled=True)
        w_fin, w_fout = [every], [regroup_out(every[fin_count:], wide * narrow)]
    steps = 4
    part = ff_width // steps
    half = width // 2
    whole = lambda shape: pl.BlockSpec(shape, lambda i: (0,) * len(shape))
    outs = pl.pallas_call(
        functools.partial(
            ffn_kernel, fold=fast, narrow=narrow, pieces=len(w_fin),
            first_out=w_fout[1].shape[0] - width // lanes if fast else 0,
        ),
        grid=(steps,),
        in_specs=[pl.BlockSpec(memory_space=pltpu.SMEM)]
        + [whole((local_tokens, width))] * narrow
        + [pl.BlockSpec(memory_space=pl.ANY)] * (2 * len(w_fin))
        + [whole((tokens, width)), whole((tokens, width)), whole((8, width))],
        out_specs=[whole((local_tokens, width))] * narrow
        + [
            whole((tokens, width)), whole((1, width)),
            pl.BlockSpec((2, half, part), lambda i: (0, 0, i)),
            pl.BlockSpec((2, half, part), lambda i: (0, 0, i)),
            pl.BlockSpec((None, part // 2, width), lambda i: (i, 0, 0)),
            pl.BlockSpec((None, part // 2, width), lambda i: (i, 0, 0)),
        ],
        out_shape=[piece16] * narrow
        + [
            row32, gain_out,
            shape_of((2, half, ff_width), bf16), shape_of((2, half, ff_width), bf16),
            shape_of((steps, part // 2, width), bf16), shape_of((steps, part // 2, width), bf16),
        ],
        scratch_shapes=[
            pltpu.VMEM((tokens, width), f32), pltpu.VMEM((tokens, width), f32),
            pltpu.VMEM((width, tokens), bf16), pltpu.VMEM((width, tokens), bf16),
            pltpu.VMEM((part, width), bf16), pltpu.VMEM((tokens, width), bf16),
            pltpu.VMEM((fin_count, width, lanes), bf16),
            pltpu.VMEM((width // lanes, ff_width, lanes), bf16), sems, sems,
        ],
        compiler_params=pltpu.CompilerParams(vmem_limit_bytes=40 * MIB),
        cost_estimate=cost_of(24),
        name="ffn",
    )(at, *c_pieces, *w_fin, *w_fout, x2, h3, g)
    out_pieces = outs[:narrow]
    dx2, gain3, keep_fin, send_fin, keep_fout, send_fout = outs[narrow:]
    ffn_sum = Scatter(at, [(keep_fin, send_fin), (keep_fout, send_fout)], fast, narrow)
    if fast:
        dx2 = after(dx2, ffn_sum.done)
    square = pltpu.VMEM((tokens, tokens), bf16)
    attend_scratch = [
        pltpu.VMEM((tokens, width), bf16), pltpu.VMEM((heads, 1, tokens), f32), square, square,
        pair_t, weights(1), sems,
    ]
    turned = pltpu.VMEM((width, tokens), bf16)
    grads = lambda count: shape_of((count, half, width), bf16)
    (dqkv2,) = call(
        functools.partial(attend_back_kernel, pieces=1, which=4, causal=False),
        [three], attend_scratch,
        at, w_second, dx2, o2, qkv2, cross_mask, peak2, inv2,
        loose=(1,), us=18, name="cross_back",
    )
    output = to_owners(out_pieces, dqkv2)
    ffn_sum.middle(dqkv2)
    if fast:
        dqkv2 = after(dqkv2, ffn_sum.done, output)
    outs = call(
        functools.partial(second_back_kernel, pieces=1, narrow=narrow, fold=fast),
        [piece16] * narrow + [row32, gain_out, grads(5), grads(5)],
        [turned, turned, pltpu.VMEM((tokens, width), bf16), weights(3), sems],
        at, w_second, dqkv2, dx2, o2, h2, m, x1, o1, g,
        loose=(1,), us=12, name="second_back",
    )
    gm_pieces = outs[:narrow]
    dx1, gain2, keep_second, send_second = outs[narrow:]
    ffn_sum.narrowed([], gain2)
    if fast:
        send_second = after(send_second, ffn_sum.done)
    second_sum = Scatter(at, [(keep_second, send_second)], fast, narrow)
    if fast:
        dx1 = after(dx1, second_sum.done, ffn_sum.done)
    dqkv1, ds = call(
        functools.partial(attend_back_kernel, pieces=1, which=0, causal=True),
        [three, shape_of((heads, tokens, tokens), bf16)], attend_scratch,
        at, w_second, table, dx1, o1, qkv1, index, peak1, inv1,
        loose=(1,), us=20, name="self_back",
    )
    (sum_fin, fin_rows, fin_part), (sum_fout, fout_rows, fout_part) = ffn_sum.total(dqkv1)
    second_sum.middle(dqkv1)
    if fast:
        dqkv1 = after(dqkv1, sum_fin, second_sum.done)
    outs = call(
        functools.partial(first_back_kernel, pieces=1, narrow=narrow, fold=fast),
        [piece16] * narrow + [gain_out, grads(3), grads(3)],
        [turned, turned, pltpu.VMEM((tokens, width), f32), weights(3), sems],
        at, w_first, dqkv1, h1, dx1, x, g,
        loose=(1,), us=9, name="first_back",
    )
    gx_pieces = outs[:narrow]
    gain1, keep_first, send_first = outs[narrow:]
    grad_memory = to_owners(gm_pieces, gain1)
    second_sum.narrowed([], gain1, grad_memory)
    (squares,) = call(
        square_kernel, [shape_of((16, 128), f32)], [],
        *(after(v, second_sum.done) for v in (attn_in, attn_out, ff_in, ff_out)), scalars=0,
        us=1, name="squares",
    )
    if fast:
        send_first = after(send_first, second_sum.done)
        keep_first = after(keep_first, squares)
    first_sum = Scatter(at, [(keep_first, send_first)], fast, narrow)
    if fast:
        ds = after(ds, first_sum.done, second_sum.done)
    (table_part,) = call(
        functools.partial(table_kernel, buckets=bucket_count),
        [shape_of((heads, 128), f32)],
        [pltpu.VMEM((heads * 16, bucket_count * 16), f32)], ds, index, scalars=0, us=11,
        name="table",
    )
    first_sum.middle(table_part)
    first_sum.narrowed([])
    ((sum_second, second_rows, second_part),) = second_sum.total(table_part)
    ((sum_first, first_rows, first_part),) = first_sum.total()
    grad_targets = to_owners([after(v, sum_first) for v in gx_pieces])
    parts = (gain1, gain2, gain3, first_part, second_part, fin_part, fout_part, table_part, squares)
    rows = sum(v.size for v in parts) // 128
    (tally,) = call(
        tally_kernel, [shape_of((-(-rows // 8) * 8, 128), f32)], [], *parts, scalars=0, us=1,
        name="tally",
    )
    tally = summed_all(tally, fast)
    (
        sum_in, sum_out, new_in, new_out, new_fin, new_fout, sum_gain, in_cols, out_cols, fin_cols,
        fout_cols, grad_table, new_table,
    ) = call(
        functools.partial(update_kernel, buckets=bucket_count),
        [
            shape_of(attn_in.shape, f32), shape_of(attn_out.shape, f32), shape_of(attn_in.shape, f32),
            shape_of(attn_out.shape, f32), shape_of(ff_in.shape, f32), shape_of(ff_out.shape, f32),
            shape_of((3, width), f32), shape_of((6, width), f32), shape_of((2, width), f32),
            shape_of((2, ff_width), f32), shape_of((1, width), f32),
            shape_of(bias_table.shape, f32), shape_of(bias_table.shape, f32),
        ],
        [], tally, sum_first, sum_second, sum_fin, sum_fout, first_rows, second_rows, fin_rows,
        fout_rows, attn_in, attn_out, ff_in, ff_out, table, scalars=0, us=3, name="update",
    )
    sum_gain = lax.dynamic_slice_in_dim(sum_gain, device * chunk, chunk, 1)
    in_rows = jnp.concatenate([first_rows, second_rows[1:4]])[:, :, 0]
    out_rows = jnp.stack([second_rows[0], second_rows[4]])[:, :, 0]
    return (
        output, grad_targets, grad_memory,
        sum_in, sum_out, sum_gain, sum_fin, sum_fout[0], grad_table,
        in_rows, in_cols, out_rows, out_cols, fin_rows[:, :, 0], fin_cols, fout_rows[0, :, 0],
        fout_cols[0], new_in, new_out, new_fin, new_fout, new_table,
    )


def solution(mesh):
    in_specs = (
        P("wide", "narrow", None),
        P("wide", "narrow", None),
        P("wide", "narrow", None),
        P("wide", "narrow"),
        P("wide", "narrow"),
        P("narrow", None),
        P(None, ("wide", "narrow"), None),
        P(None, ("wide", "narrow"), None),
        P(None, ("wide", "narrow")),
        P(None, ("wide", "narrow"), None),
        P(("wide", "narrow"), None),
        P(),
    )
    out_specs = (
        P("wide", "narrow", None),
        P("wide", "narrow", None),
        P("wide", "narrow", None),
        P(None, ("wide", "narrow"), None),
        P(None, ("wide", "narrow"), None),
        P(None, ("wide", "narrow")),
        P(None, ("wide", "narrow"), None),
        P(("wide", "narrow"), None),
        P(),
        P(None, ("wide", "narrow")),
        P(),
        P(None, ("wide", "narrow")),
        P(),
        P(None, ("wide", "narrow")),
        P(),
        P(("wide", "narrow")),
        P(),
        P(None, ("wide", "narrow"), None),
        P(None, ("wide", "narrow"), None),
        P(None, ("wide", "narrow"), None),
        P(("wide", "narrow"), None),
        P(),
    )
    return jax.shard_map(body, mesh=mesh, in_specs=in_specs, out_specs=out_specs, check_vma=False)
```
